32 devices in a mesh: frame: 8 (over z, x), row: 4 (over y, core).
Axes of the slice: x: 2, y: 2, z: 4, core: 2. Of those that a mesh axis runs over, the one named last changes fastest.
Arguments:
- block_input: bfloat16 [4096, 1024], P(('frame', 'row')), may hold values from -6 to 6
- cotangent: bfloat16 [4096, 1024], P(('frame', 'row')), may hold values from -6 to 6
- frame_lengths: int32 [8], replicated, may hold values from 170 to 512, as said below
- frame_scenes: int32 [8], replicated, may hold values from 0 to 1, as said below
- qkv_weight: bfloat16 [2, 1024, 3, 1024], P(None, 'frame', None, 'row'), may hold values from -0.1875 to 0.1875
- out_weight: bfloat16 [2, 1024, 1024], P(None, 'row', 'frame')
- up_weight: bfloat16 [2, 1024, 4096], P(None, 'frame', 'row'), may hold values from -0.1875 to 0.1875
- down_weight: bfloat16 [2, 4096, 1024], P(None, 'row', 'frame'), may hold values from -0.09375 to 0.09375
- block_gains: bfloat16 [2, 6, 1024], P(None, None, 'frame'), may hold values from 0.25 to 1.75
Outputs:
- block_output: bfloat16 [4096, 1024], P(('frame', 'row'))
- input_grad: bfloat16 [4096, 1024], P(('frame', 'row'))
- qkv_grad: float32 [2, 1024, 3, 1024], P(None, 'frame', None, 'row')
- out_grad: float32 [2, 1024, 1024], P(None, 'row', 'frame')
- up_grad: float32 [2, 1024, 4096], P(None, 'frame', 'row')
- down_grad: float32 [2, 4096, 1024], P(None, 'row', 'frame')
- gains_grad: float32 [2, 6, 1024], P(None, None, 'frame')
The draws below stay inside these ranges and needn't reach their ends.
Inputs may be any that keep to these rules, and one draw needn't show every extreme that they name: `frame_lengths`: every draw has a frame of 512 tokens. `frame_scenes`: 4 frames in each scene; frames 0, 4 and 7 are in scene 0.
All inputs are finite; a program needn't handle non-finite values.
Results may differ from the reference program's by a relative error of at most 0.02.
Values may be sent and summed in bfloat16 or wider, within the bound.
No kernel may reach another device: no remote copies, remote signals or barrier semaphores. Data moves between devices by JAX's collectives and lax.ppermute only.
A program may use at most 448 MiB of HBM per device.

```python
import math
import jax
import jax.numpy as jnp
from jax import lax

HEADS = 16
HEAD_DIM = 64
D = 1024
FF = 4096
FLEN = 512
FRAMES = 8
TOKENS = 4096


def draw_frame_lengths(key, part):
    key = jax.random.fold_in(key, 3)
    length_key, chosen_key = jax.random.split(key)
    lengths = jax.random.randint(length_key, (FRAMES,), FLEN // 3, FLEN + 1, dtype=jnp.int32)
    chosen = jax.random.randint(chosen_key, (), 0, FRAMES, dtype=jnp.int32)
    return jnp.where(jnp.arange(FRAMES, dtype=jnp.int32) == chosen, FLEN, lengths).astype(jnp.int32)


def draw_frame_scenes(key, part):
    key = jax.random.fold_in(key, 5)
    others = FRAMES - 3
    order = jax.random.permutation(key, others)
    remaining = (order >= FRAMES // 2 - 3).astype(jnp.int32)
    slots = jnp.arange(FRAMES, dtype=jnp.int32)
    position = slots - 1 - (slots > FRAMES // 2).astype(jnp.int32)
    pinned = (slots == 0) | (slots == FRAMES // 2) | (slots == FRAMES - 1)
    picked = remaining[jnp.clip(position, 0, others - 1)]
    return jnp.where(pinned, 0, picked).astype(jnp.int32)


def draw_out_weight(key, part):
    key = jax.random.fold_in(key, 11)
    normals = jax.random.normal(key, (2, D, D), jnp.float32)
    normals = jnp.clip(normals, -6.0, 6.0)
    frame_keys = FLEN / 4.0
    scene_keys = FLEN * FRAMES / 8.0
    scales = jnp.sqrt(jnp.array([frame_keys, scene_keys], jnp.float32) / D)
    return (normals * scales[:, None, None]).astype(jnp.bfloat16)


def shard_levels(stream_key, shape, cuts, low, high):
    factor_of = 1.0
    for dim, shards_of in cuts:
        heights = jax.random.uniform(jax.random.fold_in(jax.random.fold_in(stream_key, 6), dim), (shards_of,), jnp.float32, low / len(cuts), high / len(cuts))
        factor_of = factor_of * jnp.repeat(jnp.exp(heights), shape[dim] // shards_of).reshape((-1,) + (1,) * (len(shape) - 1 - dim))
    return factor_of


def normal_values(own_key, extent, deviation, limit, pieces=(), held_as=jnp.bfloat16):
    values = jax.random.normal(own_key, extent, jnp.float32) * deviation
    if len(pieces) > 0:
        values = shard_levels(own_key, extent, pieces, -0.22, 0.18) * values
    return jnp.clip(values, min=-limit, max=limit).astype(held_as)


def setup_inputs(seed: int = 0) -> dict:
    seeds = jax.random.split(jax.random.key(seed), 10)
    block_input = normal_values(seeds[0], (TOKENS, D), 1.0, 6.0, ((0, 32),))
    cotangent = normal_values(seeds[1], (TOKENS, D), 1.0, 6.0, ((0, 32),))
    frame_lengths = draw_frame_lengths(jax.random.fold_in(seeds[9], 71), 0)
    frame_scenes = draw_frame_scenes(jax.random.fold_in(seeds[9], 71), 0)
    qkv_weight = normal_values(seeds[4], (2, D, 3, D), D ** -0.5, 0.1875, ((1, 8), (3, 4)))
    out_weight = draw_out_weight(jax.random.fold_in(seeds[9], 71), 0)
    up_weight = normal_values(seeds[6], (2, D, FF), D ** -0.5, 0.1875, ((1, 8), (2, 4)))
    down_weight = normal_values(seeds[7], (2, FF, D), FF ** -0.5, 0.09375, ((1, 4), (2, 8)))
    block_gains = jnp.clip(1.0 + 0.15 * jax.random.normal(seeds[8], (2, 6, D), jnp.float32), 0.25, 1.75).astype(jnp.bfloat16)
    return dict(block_input=block_input, cotangent=cotangent, frame_lengths=frame_lengths, frame_scenes=frame_scenes, qkv_weight=qkv_weight, out_weight=out_weight, up_weight=up_weight, down_weight=down_weight, block_gains=block_gains)


MASKED = -1e+30
EPSILON = 1e-06
PRECISE = lax.Precision.HIGHEST

@jax.custom_vjp
def low(v):
    return lax.optimization_barrier(v.astype(jnp.bfloat16)).astype(jnp.float32)

@jax.custom_vjp
def low_back(v):
    return v

def low_keep(v):
    return (low(v), None)

def low_pass(kept, grad):
    return (grad,)

def back_keep(v):
    return (v, None)

def back_low(kept, grad):
    return (low(grad),)
low.defvjp(low_keep, low_pass)
low_back.defvjp(back_keep, back_low)

def layer_norm(values, gain_vec):
    center = values - lax.optimization_barrier(jnp.mean(values, axis=-1, keepdims=True))
    spread = lax.optimization_barrier(jnp.mean(center * center, axis=-1, keepdims=True))
    return center * lax.rsqrt(spread + EPSILON) * gain_vec

def head_norm(values, gain_vec):
    shaped = values.reshape(values.shape[0], HEADS, HEAD_DIM)
    return layer_norm(shaped, gain_vec.reshape(HEADS, HEAD_DIM)).reshape(values.shape)

def matmul(left, right):
    return jnp.dot(left, right, precision=PRECISE)

def attend(queries, key_rows, value_rows, usable):
    scaling = HEAD_DIM ** (-0.5)

    def one_head(operands):
        head_q, head_k, head_v = operands
        scores = low_back(matmul(head_q, head_k.T) * scaling)
        scores = jnp.where(usable[None, :], scores, MASKED)
        weights = low(jax.nn.softmax(scores, axis=-1))
        return matmul(weights, head_v)
    result = lax.map(jax.checkpoint(one_head), (jnp.swapaxes(queries, 0, 1), jnp.swapaxes(key_rows, 0, 1), jnp.swapaxes(value_rows, 0, 1)))
    return jnp.swapaxes(result, 0, 1)

def reference(block_input, cotangent, frame_lengths, frame_scenes, qkv_weight, out_weight, up_weight, down_weight, block_gains):
    positions = jnp.arange(TOKENS, dtype=jnp.int32)
    frame_ids = positions // FLEN
    token_valid = positions - frame_ids * FLEN < frame_lengths[frame_ids]
    token_scene = frame_scenes[frame_ids]
    per_group = math.gcd(FRAMES, max(1, 4096 // FLEN))

    def grouped(array):
        return array.reshape(FRAMES // per_group, per_group * FLEN, array.shape[-1])

    def by_frames(array):
        return array.reshape(FRAMES, FLEN, HEADS, HEAD_DIM)

    def forward(hidden, qkv_all, out_all, up_all, down_all, gains_all):
        for block_id in range(2):
            gain_rows = gains_all[block_id]
            qkv_full = qkv_all[block_id].reshape(D, 3 * D)
            out_full = out_all[block_id]
            up_full = up_all[block_id]
            down_full = down_all[block_id]

            def first_half(rows_in):
                normed = low(layer_norm(rows_in, gain_rows[0]))
                projected = low_back(matmul(normed, qkv_full))
                queries = low(head_norm(projected[:, :D], gain_rows[4]))
                key_rows = low(head_norm(projected[:, D:2 * D], gain_rows[5]))
                value_rows = low(projected[:, 2 * D:])
                return (queries, key_rows, value_rows)
            queries, key_rows, value_rows = lax.map(jax.checkpoint(first_half), grouped(hidden))
            queries = queries.reshape(TOKENS, D)
            key_rows = key_rows.reshape(TOKENS, D)
            value_rows = value_rows.reshape(TOKENS, D)
            if block_id == 0:

                def frame_attend(operands):
                    frame_q, frame_k, frame_v, frame_len = operands
                    usable = jnp.arange(FLEN, dtype=jnp.int32) < frame_len
                    return attend(frame_q, frame_k, frame_v, usable)
                attended = lax.map(jax.checkpoint(frame_attend), (by_frames(queries), by_frames(key_rows), by_frames(value_rows), frame_lengths))
            else:
                all_keys = key_rows.reshape(TOKENS, HEADS, HEAD_DIM)
                all_values = value_rows.reshape(TOKENS, HEADS, HEAD_DIM)

                def scene_attend(operands):
                    frame_q, frame_scene = operands
                    return attend(frame_q, all_keys, all_values, token_valid & (token_scene == frame_scene))
                attended = lax.map(jax.checkpoint(scene_attend), (by_frames(queries), frame_scenes))
            attended = low_back(low(attended.reshape(TOKENS, D)))

            def second_half(operands):
                rows_in, rows_att = operands
                branch = low_back(matmul(rows_att, out_full))
                middle = rows_in + gain_rows[2] * branch
                second = low(layer_norm(middle, gain_rows[1]))
                up_values = low_back(matmul(second, up_full))
                active = low(jax.nn.gelu(up_values, approximate=False))
                down_values = low_back(matmul(active, down_full))
                return middle + gain_rows[3] * down_values
            hidden = lax.map(jax.checkpoint(second_half), (grouped(hidden), grouped(attended))).reshape(TOKENS, D)
        return hidden
    output, pullback = jax.vjp(forward, block_input.astype(jnp.float32), qkv_weight.astype(jnp.float32), out_weight.astype(jnp.float32), up_weight.astype(jnp.float32), down_weight.astype(jnp.float32), block_gains.astype(jnp.float32))
    cotan_seed = cotangent.astype(jnp.float32) * token_valid[:, None].astype(jnp.float32)
    gradients = pullback(cotan_seed)
    return (output.astype(jnp.bfloat16), gradients[0].astype(jnp.bfloat16), gradients[1], gradients[2], gradients[3], gradients[4], gradients[5])
```

```python
import functools

import jax
import jax.numpy as jnp
from jax import lax
from jax.experimental import pallas as pl
from jax.experimental.pallas import tpu as pltpu
from jax.sharding import PartitionSpec as P

HEAD_DIM = 64
FLEN = 512
EPSILON = 1e-06
F32 = jnp.float32
BF16 = jnp.bfloat16


def ring_split(frames):
    return (4, 2) if frames == 8 else None


def frame_permute(value, frames, down, across):
    rows, cols = ring_split(frames)
    pairs = []
    for z in range(rows):
        for x in range(cols):
            pairs.append((((z + down) % rows) * cols + (x ^ across), z * cols + x))
    return lax.ppermute(value, "frame", pairs)


def row_permute(value, bit):
    return lax.ppermute(value, "row", [(i ^ bit, i) for i in range(4)])


def gather_frame(shard):
    frames = lax.axis_size("frame")
    if ring_split(frames) is None:
        whole = lax.all_gather(shard, "frame", axis=0, tiled=False)
        return [whole[i] for i in range(frames)]
    rows, cols = ring_split(frames)
    blocks = []
    for down in range(rows):
        own = frame_permute(shard, frames, down, 0) if down else shard
        blocks.append(own)
        blocks.append(frame_permute(own, frames, 0, 1))
    return blocks


def scatter_frame(blocks):
    frames = lax.axis_size("frame")
    if ring_split(frames) is None:
        return lax.psum_scatter(jnp.stack(blocks), "frame", scatter_dimension=0, tiled=False).astype(F32)
    rows, cols = ring_split(frames)
    total = None
    for down in list(range(1, rows)) + [0]:
        keep, give = blocks[down * cols], blocks[down * cols + 1]
        both = keep.astype(F32) + frame_permute(give, frames, 0, 1).astype(F32)
        if down:
            both = frame_permute(both.astype(BF16), frames, rows - down, 0).astype(F32)
        total = both if total is None else total + both
    return total


def to_relative(values):
    frames = lax.axis_size("frame")
    if ring_split(frames) is None:
        return values
    rows, cols = ring_split(frames)
    me = lax.axis_index("frame")
    width = values.shape[-1] // frames
    lead = values.shape[:-1]
    twice = jnp.concatenate([values, values], axis=-1)
    turned = lax.dynamic_slice_in_dim(twice, (me // cols) * cols * width, frames * width, -1)
    shaped = turned.reshape(lead + (rows, cols, width))
    swapped = jnp.concatenate([shaped[..., 1:2, :], shaped[..., 0:1, :]], axis=-2)
    return jnp.where(me % cols == 1, swapped, shaped).reshape(values.shape)


def to_absolute(values):
    frames = lax.axis_size("frame")
    if ring_split(frames) is None:
        return values
    rows, cols = ring_split(frames)
    me = lax.axis_index("frame")
    width = values.shape[-1] // frames
    lead = values.shape[:-1]
    shaped = values.reshape(lead + (rows, cols, width))
    swapped = jnp.concatenate([shaped[..., 1:2, :], shaped[..., 0:1, :]], axis=-2)
    values = jnp.where(me % cols == 1, swapped, shaped).reshape(values.shape)
    twice = jnp.concatenate([values, values], axis=-1)
    start = ((rows - me // cols) % rows) * cols * width
    return lax.dynamic_slice_in_dim(twice, start, frames * width, -1)


def relative_frames():
    frames = lax.axis_size("frame")
    if ring_split(frames) is None:
        return jnp.arange(frames, dtype=jnp.int32)
    rows, cols = ring_split(frames)
    me = lax.axis_index("frame")
    places = jnp.arange(frames, dtype=jnp.int32)
    return ((me // cols + places // cols) % rows) * cols + ((me % cols) ^ (places % cols))


def gather_rows(own):
    across = row_permute(own, 2)
    near = jnp.concatenate([own, row_permute(own, 1)], axis=0)
    far = jnp.concatenate([across, row_permute(across, 1)], axis=0)
    return near, far


def scatter_rows(near, far):
    count = near.shape[0] // 2
    far_sum = far[:count] + row_permute(far[count:].astype(BF16), 1).astype(F32)
    far_in = row_permute(far_sum.astype(BF16), 2).astype(F32)
    near_sum = near[:count] + row_permute(near[count:].astype(BF16), 1).astype(F32)
    return near_sum + far_in


def head_mask(shape, head):
    lanes = lax.broadcasted_iota(jnp.int32, shape, len(shape) - 1)
    return (lanes // HEAD_DIM) == head


def dot_nt(a, b):
    return lax.dot_general(a, b, (((1,), (1,)), ((), ())), preferred_element_type=F32)


def dot_nn(a, b):
    return lax.dot_general(a, b, (((1,), (0,)), ((), ())), preferred_element_type=F32)


def live_rows(place_ref, lens_ref, block, count):
    slots = lax.broadcasted_iota(jnp.int32, (count, 1), 0) ^ (place_ref[0] * (count // 4))
    return slots < lens_ref[block]


def forward_kernel(table_ref, lens_ref, place_ref, q_ref, k_ref, v_ref, out_ref, lse_ref, acc, sums):
    step = pl.program_id(0)
    count, width = q_ref.shape
    heads = width // HEAD_DIM

    @pl.when(step == 0)
    def _():
        acc[...] = jnp.zeros_like(acc)
        sums[...] = jnp.zeros_like(sums)

    live = live_rows(place_ref, lens_ref, table_ref[step], k_ref.shape[1])
    keys = k_ref[0]
    values_t = v_ref[0].T
    queries = q_ref[...]
    for head in range(heads):
        mine = jnp.where(head_mask(queries.shape, head), queries, 0) * BF16(HEAD_DIM**-0.5)
        scores = dot_nt(keys, mine)
        powers = jnp.where(live, jnp.exp(scores), 0.0)
        sums[head : head + 1, :] += jnp.sum(powers, axis=0, keepdims=True)
        lanes = slice(head * HEAD_DIM, (head + 1) * HEAD_DIM)
        acc[lanes, :] += dot_nn(values_t[lanes, :], powers.astype(BF16))

    @pl.when(step == pl.num_programs(0) - 1)
    def _():
        lse_ref[...] = jnp.log(sums[...])
        for head in range(heads):
            lanes = slice(head * HEAD_DIM, (head + 1) * HEAD_DIM)
            acc[lanes, :] = acc[lanes, :] / sums[head : head + 1, :]
        out_ref[...] = acc[...].T.astype(BF16)


def backward_kernel(
    table_ref, lens_ref, place_ref, q_ref, g_ref, o_ref, lse_ref, k_ref, v_ref, unused_ref, dq_ref, dkv_ref, acc, delta
):
    step = pl.program_id(0)
    count, width = q_ref.shape
    heads = width // HEAD_DIM

    @pl.when(step == 0)
    def _():
        acc[...] = jnp.zeros_like(acc)
        product = g_ref[...].astype(F32) * o_ref[...].astype(F32)
        turned = product.T
        for head in range(heads):
            lanes = slice(head * HEAD_DIM, (head + 1) * HEAD_DIM)
            delta[head : head + 1, :] = jnp.sum(turned[lanes, :], axis=0, keepdims=True)

    live = live_rows(place_ref, lens_ref, table_ref[step], k_ref.shape[1])
    keys = k_ref[0]
    keys_t = keys.T
    values = v_ref[0]
    queries = q_ref[...]
    grads = g_ref[...]
    grad_k = jnp.zeros(keys.shape, F32)
    grad_v = jnp.zeros(keys.shape, F32)
    for head in range(heads):
        inside = head_mask(queries.shape, head)
        mine = jnp.where(inside, queries, 0) * BF16(HEAD_DIM**-0.5)
        mine_g = jnp.where(inside, grads, 0)
        scores = dot_nt(keys, mine)
        full = jnp.where(live, jnp.exp(scores - lse_ref[head : head + 1, :]), 0.0)
        grad_probs = dot_nt(values, mine_g)
        steep = (full * (grad_probs - delta[head : head + 1, :])).astype(BF16)
        grad_v += dot_nn(full.astype(BF16), mine_g)
        grad_k += dot_nn(steep, mine)
        lanes = slice(head * HEAD_DIM, (head + 1) * HEAD_DIM)
        acc[lanes, :] += dot_nn(keys_t[lanes, :], steep)
    dkv_ref[0, :, :width] = grad_k.astype(dkv_ref.dtype)
    dkv_ref[0, :, width:] = grad_v.astype(dkv_ref.dtype)

    @pl.when(step == pl.num_programs(0) - 1)
    def _():
        dq_ref[...] = acc[...].T * (HEAD_DIM**-0.5)


def attend(queries, kv_blocks, table, lens, place):
    count, width = queries.shape
    flen = kv_blocks.shape[1]
    whole = lambda j, t, l, p: (0, 0)
    return pl.pallas_call(
        forward_kernel,
        grid_spec=pltpu.PrefetchScalarGridSpec(
            num_scalar_prefetch=3,
            grid=(table.shape[0],),
            in_specs=[
                pl.BlockSpec((count, width), whole),
                pl.BlockSpec((1, flen, width), lambda j, t, l, p: (t[j], 0, 0)),
                pl.BlockSpec((1, flen, width), lambda j, t, l, p: (t[j], 0, 1)),
            ],
            out_specs=[
                pl.BlockSpec((count, width), whole),
                pl.BlockSpec((8, count), whole),
            ],
            scratch_shapes=[pltpu.VMEM((width, count), F32), pltpu.VMEM((8, count), F32)],
        ),
        out_shape=[
            jax.ShapeDtypeStruct((count, width), BF16),
            jax.ShapeDtypeStruct((8, count), F32),
        ],
        compiler_params=pltpu.CompilerParams(vmem_limit_bytes=48 * 1024 * 1024),
        cost_estimate=pl.CostEstimate(
            flops=4 * count * flen * width * table.shape[0] * 4,
            bytes_accessed=4 * flen * width * table.shape[0],
            transcendentals=count * flen * table.shape[0] * 4,
        ),
    )(table, lens, place, queries, kv_blocks, kv_blocks)


def attend_back(queries, grads, attended, lse, kv_blocks, table, lens, place, dtype):
    count, width = queries.shape
    flen = kv_blocks.shape[1]
    whole = lambda j, t, l, p: (0, 0)
    blank = jnp.zeros(kv_blocks.shape, dtype)
    return pl.pallas_call(
        backward_kernel,
        grid_spec=pltpu.PrefetchScalarGridSpec(
            num_scalar_prefetch=3,
            grid=(table.shape[0],),
            in_specs=[
                pl.BlockSpec((count, width), whole),
                pl.BlockSpec((count, width), whole),
                pl.BlockSpec((count, width), whole),
                pl.BlockSpec((8, count), whole),
                pl.BlockSpec((1, flen, width), lambda j, t, l, p: (t[j], 0, 0)),
                pl.BlockSpec((1, flen, width), lambda j, t, l, p: (t[j], 0, 1)),
                pl.BlockSpec(memory_space=pl.ANY),
            ],
            out_specs=[
                pl.BlockSpec((count, width), whole),
                pl.BlockSpec((1, flen, 2 * width), lambda j, t, l, p: (t[j], 0, 0)),
            ],
            scratch_shapes=[pltpu.VMEM((width, count), F32), pltpu.VMEM((8, count), F32)],
        ),
        out_shape=[
            jax.ShapeDtypeStruct((count, width), F32),
            jax.ShapeDtypeStruct(kv_blocks.shape, dtype),
        ],
        input_output_aliases={9: 1},
        compiler_params=pltpu.CompilerParams(vmem_limit_bytes=48 * 1024 * 1024),
        cost_estimate=pl.CostEstimate(
            flops=10 * count * flen * width * table.shape[0] * 4,
            bytes_accessed=8 * flen * width * table.shape[0],
            transcendentals=count * flen * table.shape[0] * 4,
        ),
    )(table, lens, place, queries, grads, attended, lse, kv_blocks, kv_blocks, blank)


def norm_parts(values):
    center = values - jnp.mean(values, axis=-1, keepdims=True)
    scale = lax.rsqrt(jnp.mean(center * center, axis=-1, keepdims=True) + EPSILON)
    return center * scale, scale


def norm_back(unit, scale, gain, grad):
    inner = grad * gain
    return scale * (
        inner
        - jnp.mean(inner, axis=-1, keepdims=True)
        - unit * jnp.mean(inner * unit, axis=-1, keepdims=True)
    )


def head_means(values):
    width = values.shape[-1]
    ids = jnp.arange(width, dtype=jnp.int32) // HEAD_DIM
    spread = jnp.where(ids[:, None] == ids[None, :], F32(1.0 / HEAD_DIM), F32(0))
    return jnp.dot(values, spread, precision=lax.Precision.HIGHEST, preferred_element_type=F32)


def head_parts(values):
    center = values - head_means(values)
    scale = lax.rsqrt(head_means(center * center) + EPSILON)
    return center * scale, scale


def head_back(unit, scale, gain, grad):
    inner = grad * gain
    return scale * (inner - head_means(inner) - unit * head_means(inner * unit))


def gelu(values):
    return 0.5 * values * (1.0 + lax.erf(values * F32(0.7071067811865476)))


def gelu_slope(values):
    bell = jnp.exp(-0.5 * values * values) * F32(0.3989422804014327)
    return 0.5 * (1.0 + lax.erf(values * F32(0.7071067811865476))) + values * bell


def dot(a, b):
    return jnp.dot(a, b, preferred_element_type=F32)


def dot_t(a, b):
    return lax.dot_general(a, b, (((1,), (1,)), ((), ())), preferred_element_type=F32)


def t_dot(a, b):
    return lax.dot_general(a, b, (((0,), (0,)), ((), ())), preferred_element_type=F32)


def per_device(
    block_input,
    cotangent,
    frame_lengths,
    frame_scenes,
    qkv_weight,
    out_weight,
    up_weight,
    down_weight,
    block_gains,
):
    row_count, model_width = block_input.shape
    frames = lax.axis_size("frame")
    my_frame = lax.axis_index("frame")
    my_row = lax.axis_index("row")
    local_width = qkv_weight.shape[3]
    shard = model_width // frames
    place = my_row.astype(jnp.int32).reshape(1)
    slots = my_row * row_count + jnp.arange(row_count, dtype=jnp.int32)
    row_live = (slots < frame_lengths[my_frame]).astype(F32)

    order = relative_frames()
    rel_lens = frame_lengths[order]
    other = (frame_scenes[order] != frame_scenes[my_frame]).astype(jnp.int32)
    picked = jnp.argsort(other * frames + jnp.arange(frames, dtype=jnp.int32))
    scene_table = picked[: frames // 2].astype(jnp.int32)
    frame_table = jnp.zeros((1,), jnp.int32)
    frame_lens = frame_lengths[my_frame].reshape(1)

    qkv_shard = jnp.transpose(qkv_weight, (0, 2, 1, 3))
    gain_abs = lax.all_gather(block_gains, "frame", axis=2, tiled=True).astype(F32)
    gain_rel = to_relative(gain_abs)
    gain_heads = lax.dynamic_slice_in_dim(gain_abs, my_row * local_width, local_width, 2)

    hidden = to_relative(block_input).astype(F32)
    stored = []
    for block in range(2):
        gain = gain_rel[block]
        gain_q, gain_k = gain_heads[block, 4], gain_heads[block, 5]
        w_qkv = jnp.concatenate(gather_frame(qkv_shard[block]), axis=1)
        w_out = jnp.concatenate(gather_frame(out_weight[block]), axis=1)
        w_up = jnp.concatenate(gather_frame(up_weight[block]), axis=0)
        w_down = jnp.concatenate(gather_frame(down_weight[block]), axis=1)

        unit_one, scale_one = norm_parts(hidden)
        normed = gather_rows((unit_one * gain[0]).astype(BF16))
        mixed = [[dot(part, w_qkv[i]) for part in normed] for i in range(3)]
        q_parts = [head_parts(part) for part in mixed[0]]
        k_parts = [head_parts(part) for part in mixed[1]]
        queries = jnp.concatenate([(u * gain_q).astype(BF16) for u, _ in q_parts])
        kv = jnp.concatenate(
            [
                jnp.concatenate([(u * gain_k).astype(BF16), v.astype(BF16)], axis=1)
                for (u, _), v in zip(k_parts, mixed[2], strict=True)
            ]
        )
        if block == 0:
            kv_blocks, table, lens = kv[None], frame_table, frame_lens
        else:
            kv_blocks, table, lens = jnp.stack(gather_frame(kv)), scene_table, rel_lens
        attended, lse = attend(queries, kv_blocks, table, lens, place)
        half = attended.shape[0] // 2
        branch_far = dot(attended[half:], w_out)
        branch = scatter_rows(dot(attended[:half], w_out), branch_far)
        middle = hidden + gain[2] * branch
        unit_two, scale_two = norm_parts(middle)
        second = gather_rows((unit_two * gain[1]).astype(BF16))
        up_values = [dot(part, w_up) for part in second]
        active = [gelu(part).astype(BF16) for part in up_values]
        down_far = dot(active[1], w_down)
        down_values = scatter_rows(dot(active[0], w_down), down_far)
        result = middle + gain[3] * down_values
        stored.append(
            (
                (w_qkv, w_out, w_up, w_down),
                (unit_one, scale_one, jnp.concatenate(normed), q_parts, k_parts),
                (queries, kv_blocks, table, lens, attended, lse),
                (branch, unit_two, scale_two, jnp.concatenate(second), up_values),
                (jnp.concatenate(active), down_values),
            )
        )
        hidden = result
    output = to_absolute(hidden.astype(BF16))

    grad = to_relative(cotangent).astype(F32) * row_live[:, None]
    shares = [None, None]
    for block in (1, 0):
        gain = gain_rel[block]
        gain_q, gain_k = gain_heads[block, 4], gain_heads[block, 5]
        (
            (w_qkv, w_out, w_up, w_down),
            (unit_one, scale_one, normed, q_parts, k_parts),
            (queries, kv_blocks, table, lens, attended, lse),
            (branch, unit_two, scale_two, second, up_values),
            (active, down_values),
        ) = stored[block]
        gain_three = jnp.sum(grad * down_values, axis=0)
        grad_down = gather_rows((gain[3] * grad).astype(BF16))
        grad_up = [
            (dot_t(part, w_down) * gelu_slope(up)).astype(BF16)
            for part, up in zip(grad_down, up_values, strict=True)
        ]
        grad_second_far = dot_t(grad_up[1], w_up)
        grad_second = scatter_rows(dot_t(grad_up[0], w_up), grad_second_far)
        down_grad = t_dot(active, jnp.concatenate(grad_down)).astype(BF16)
        up_grad = t_dot(second, jnp.concatenate(grad_up)).astype(BF16)
        gain_one = jnp.sum(grad_second * unit_two, axis=0)
        grad_middle = grad + norm_back(unit_two, scale_two, gain[1], grad_second)
        gain_two = jnp.sum(grad_middle * branch, axis=0)
        grad_branch = gather_rows((gain[2] * grad_middle).astype(BF16))
        grad_attended = jnp.concatenate([dot_t(part, w_out).astype(BF16) for part in grad_branch])
        out_grad = t_dot(attended, jnp.concatenate(grad_branch)).astype(BF16)
        if block == 0:
            grad_q, grad_kv = attend_back(
                queries, grad_attended, attended, lse, kv_blocks, table, lens, place, F32
            )
            grad_kv = grad_kv[0]
        else:
            grad_q, partial_kv = attend_back(
                queries, grad_attended, attended, lse, kv_blocks, table, lens, place, BF16
            )
            grad_kv = scatter_frame([partial_kv[i] for i in range(frames)])
        grad_k, grad_v = grad_kv[:, :local_width], grad_kv[:, local_width:]
        unit_q = jnp.concatenate([u for u, _ in q_parts])
        unit_k = jnp.concatenate([u for u, _ in k_parts])
        scale_q = jnp.concatenate([s for _, s in q_parts])
        scale_k = jnp.concatenate([s for _, s in k_parts])
        gain_four = jnp.sum(grad_q * unit_q, axis=0)
        gain_five = jnp.sum(grad_k * unit_k, axis=0)
        mixed_grads = [
            head_back(unit_q, scale_q, gain_q, grad_q).astype(BF16),
            head_back(unit_k, scale_k, gain_k, grad_k).astype(BF16),
            grad_v.astype(BF16),
        ]
        half = unit_q.shape[0] // 2
        halves = [
            sum(dot_t(part[rows], w_qkv[i]) for i, part in enumerate(mixed_grads))
            for rows in (slice(0, half), slice(half, None))
        ]
        grad_normed = scatter_rows(*halves)
        qkv_grad = jnp.stack([t_dot(normed, part) for part in mixed_grads]).astype(BF16)
        gain_zero = jnp.sum(grad_normed * unit_one, axis=0)
        grad = grad_middle + norm_back(unit_one, scale_one, gain[0], grad_normed)

        def cut(array, axis):
            return [
                lax.slice_in_dim(array, i * shard, (i + 1) * shard, axis=axis) for i in range(frames)
            ]

        per_row = to_absolute(jnp.stack([gain_zero, gain_one, gain_two, gain_three]))
        per_head = lax.dynamic_update_slice_in_dim(
            jnp.zeros((2, model_width), F32),
            jnp.stack([gain_four, gain_five]),
            my_row * local_width,
            1,
        )
        shares[block] = (
            scatter_frame(cut(qkv_grad, 1)),
            scatter_frame(cut(out_grad, 1)),
            scatter_frame(cut(up_grad, 0)),
            scatter_frame(cut(down_grad, 1)),
            jnp.concatenate([per_row, per_head]),
        )
    gains = lax.psum(jnp.stack([shares[0][4], shares[1][4]]), ("frame", "row"))
    return (
        output,
        to_absolute(grad.astype(BF16)),
        jnp.transpose(jnp.stack([shares[0][0], shares[1][0]]), (0, 2, 1, 3)),
        jnp.stack([shares[0][1], shares[1][1]]),
        jnp.stack([shares[0][2], shares[1][2]]),
        jnp.stack([shares[0][3], shares[1][3]]),
        lax.dynamic_slice_in_dim(gains, my_frame * shard, shard, 2),
    )


def solution(mesh):
    return jax.shard_map(
        per_device,
        mesh=mesh,
        in_specs=(
            P(("frame", "row"), None),
            P(("frame", "row"), None),
            P(),
            P(),
            P(None, "frame", None, "row"),
            P(None, "row", "frame"),
            P(None, "frame", "row"),
            P(None, "row", "frame"),
            P(None, None, "frame"),
        ),
        out_specs=(
            P(("frame", "row"), None),
            P(("frame", "row"), None),
            P(None, "frame", None, "row"),
            P(None, "row", "frame"),
            P(None, "frame", "row"),
            P(None, "row", "frame"),
            P(None, None, "frame"),
        ),
        check_vma=False,
    )
```

```python
import functools

import jax
import jax.numpy as jnp
from jax import lax
from jax.experimental import pallas as pl
from jax.experimental.pallas import tpu as pltpu
from jax.sharding import PartitionSpec as P

HEAD_DIM = 64
EPSILON = 1e-06
F32 = jnp.float32
BF16 = jnp.bfloat16
LANES = 128
TILE = 256
ROOT_HALF = 0.7071067811865476
BELL = 0.3989422804014327
SCALING = HEAD_DIM**-0.5

RING = (0, 2, 4, 6, 7, 5, 3, 1)


def on_ring():
    return lax.axis_size("frame") == len(RING)


def ring_take(value, step):
    count = len(RING)
    return lax.ppermute(value, "frame", [(RING[(i + step) % count], RING[i]) for i in range(count)])


def row_take(value, bit):
    return lax.ppermute(value, "row", [(i ^ bit, i) for i in range(4)])


def ring_gather(shard, cut):
    ahead, behind = [shard], [shard]
    for _ in range(3):
        ahead.append(ring_take(ahead[-1], 1))
        behind.append(ring_take(behind[-1], -1))
    far_low = ring_take(ahead[3][:cut], 1)
    far_high = ring_take(behind[3][cut:], -1)
    return ahead + [far_low, far_high] + behind[3:0:-1]


def add_pair(a, b):
    return (a.astype(F32) + b.astype(F32)).astype(BF16)


def ring_scatter(pieces):
    ahead = pieces[1:4]
    far_low, far_high = pieces[4:6]
    behind = pieces[8:5:-1]
    cut = far_low.shape[0]
    low = ring_take(far_low, -1)
    high = ring_take(far_high, 1)
    right = jnp.concatenate([add_pair(ahead[2][:cut], low), ahead[2][cut:]])
    left = jnp.concatenate([behind[2][:cut], add_pair(behind[2][cut:], high)])
    for place in (1, 0):
        right = add_pair(ahead[place], ring_take(right, -1))
        left = add_pair(behind[place], ring_take(left, 1))
    return pieces[0], ring_take(right, -1), ring_take(left, 1)


def dot_nt(a, b):
    return lax.dot_general(a, b, (((1,), (1,)), ((), ())), preferred_element_type=F32)


def dot_nn(a, b):
    return lax.dot_general(a, b, (((1,), (0,)), ((), ())), preferred_element_type=F32)


def whole(shape):
    return pl.BlockSpec(shape, lambda *_: (0,) * len(shape))


def column(rows, place):
    return pl.BlockSpec((rows, TILE), lambda j, *_: (0, place(j)))


def cost(us):
    return pl.CostEstimate(flops=int(us * 1.0e9), bytes_accessed=int(us * 2.0e6), transcendentals=0)


def run(kernel, grid, in_specs, out_specs, out_shape, scratch, operands, us, prefetch=0, aliases=None):
    return pl.pallas_call(
        kernel,
        grid_spec=pltpu.PrefetchScalarGridSpec(
            num_scalar_prefetch=prefetch,
            grid=grid,
            in_specs=in_specs,
            out_specs=out_specs,
            scratch_shapes=scratch,
        ),
        out_shape=out_shape,
        input_output_aliases=aliases or {},
        compiler_params=pltpu.CompilerParams(vmem_limit_bytes=56 * 1024 * 1024),
        cost_estimate=cost(us),
    )(*operands)


def shaped(*shape, dtype=F32):
    return jax.ShapeDtypeStruct(shape, dtype)


def norm_parts(values):
    center = values - jnp.mean(values, axis=-1, keepdims=True)
    scale = lax.rsqrt(jnp.mean(center * center, axis=-1, keepdims=True) + EPSILON)
    return center * scale, scale


def norm_back(unit, scale, gain, grad):
    inner = grad * gain
    return scale * (
        inner
        - jnp.mean(inner, axis=-1, keepdims=True)
        - unit * jnp.mean(inner * unit, axis=-1, keepdims=True)
    )


def head_means(values):
    width = values.shape[-1]
    rows = lax.broadcasted_iota(jnp.int32, (width, width), 0) // HEAD_DIM
    cols = lax.broadcasted_iota(jnp.int32, (width, width), 1) // HEAD_DIM
    spread = jnp.where(rows == cols, F32(1.0 / HEAD_DIM), F32(0)).astype(BF16)
    high = values.astype(BF16)
    low = (values - high.astype(F32)).astype(BF16)
    return dot_nn(high, spread) + dot_nn(low, spread)


def head_parts(values):
    center = values - head_means(values)
    scale = lax.rsqrt(head_means(center * center) + EPSILON)
    return center * scale, scale


def head_back(unit, scale, gain, grad):
    inner = grad * gain
    return scale * (inner - head_means(inner) - unit * head_means(inner * unit))


def joined(refs):
    if len(refs) == 1:
        return refs[0][...]
    return jnp.concatenate([ref[...] for ref in refs], axis=0)


def head_mask(shape, head):
    lanes = lax.broadcasted_iota(jnp.int32, shape, 1)
    return (lanes // HEAD_DIM) == head


def live_keys(count, core, length):
    place = lax.broadcasted_iota(jnp.int32, (count, 1), 0)
    quarter = count // 4
    half = place // (2 * quarter)
    chip = (place // quarter) % 2
    slot = (chip * 2 + (half ^ core)) * quarter + place % quarter
    return slot < length


def pack_kernel(with_gains, qkv_ref, out_ref, up_ref, down_ref, gains_ref, at_ref, ff_ref):
    rows = up_ref.shape[1]
    width = qkv_ref.shape[3]
    for i in range(3):
        at_ref[:rows, i * width : (i + 1) * width] = qkv_ref[0, i]
    at_ref[:rows, 3 * width :] = out_ref[0].T
    ff = up_ref.shape[2]
    ff_ref[:, :ff] = up_ref[0]
    ff_ref[:, ff:] = down_ref[0].T
    if with_gains:
        at_ref[rows:, :] = jnp.zeros((16, at_ref.shape[1]), BF16)
        flat = jnp.concatenate([gains_ref[0], gains_ref[1], jnp.zeros((4, rows), BF16)], axis=0)
        at_ref[rows:, :rows] = flat


def gains_kernel(inverse_ref, *refs):
    pieces, (wide_ref, heads_ref) = refs[:-2], refs[-2:]
    for k, piece in enumerate(pieces):
        wide_ref[:, k * LANES : (k + 1) * LANES] = piece[...].astype(F32)
    for k in range(2):
        start = pl.multiple_of(inverse_ref[k] * LANES, LANES)
        heads_ref[:, k * LANES : (k + 1) * LANES] = wide_ref[:, pl.ds(start, LANES)]


def enter_kernel(masked, order_ref, facts_ref, own_ref, far_ref, out_ref):
    rows = own_ref.shape[0]
    chip, core, length = facts_ref[0], facts_ref[1], facts_ref[2]
    for k in range(own_ref.shape[1] // LANES):
        lanes = pl.ds(pl.multiple_of(order_ref[k] * LANES, LANES), LANES)
        for source, place in ((own_ref, chip), (far_ref, 1 - chip)):
            values = source[:, lanes].astype(F32)
            if masked:
                slots = (place * 2 + core) * rows + lax.broadcasted_iota(jnp.int32, (rows, 1), 0)
                values = jnp.where(slots < length, values, 0.0)
            start = pl.multiple_of(place * rows, rows)
            out_ref[pl.ds(start, rows), k * LANES : (k + 1) * LANES] = values


def leave(values_ref, order_ref, facts_ref, out_ref):
    rows = out_ref.shape[0]
    start = pl.multiple_of(facts_ref[0] * rows, rows)
    for k in range(out_ref.shape[1] // LANES):
        lanes = pl.ds(pl.multiple_of(order_ref[k] * LANES, LANES), LANES)
        values = values_ref[pl.ds(start, rows), k * LANES : (k + 1) * LANES]
        out_ref[:, lanes] = values.astype(out_ref.dtype)


def first_norm_kernel(row, h_ref, gains_ref, normed_ref):
    unit, _ = norm_parts(h_ref[...])
    normed_ref[...] = (unit * gains_ref[row : row + 1, :]).astype(BF16)


def total_of(own_ref, far_ref):
    return own_ref[...].astype(F32) + far_ref[...].astype(F32)


def residual_kernel(scale_row, norm_row, h_ref, own_ref, far_ref, gains_ref, next_ref, normed_ref):
    value = h_ref[...] + gains_ref[scale_row : scale_row + 1, :] * total_of(own_ref, far_ref)
    next_ref[...] = value
    unit, _ = norm_parts(value)
    normed_ref[...] = (unit * gains_ref[norm_row : norm_row + 1, :]).astype(BF16)


def output_kernel(scale_row, order_ref, facts_ref, h_ref, own_ref, far_ref, gains_ref, out_ref, held):
    held[...] = h_ref[...] + gains_ref[scale_row : scale_row + 1, :] * total_of(own_ref, far_ref)
    leave(held, order_ref, facts_ref, out_ref)


def seed_kernel(row, grad_ref, own_ref, far_ref, gains_ref, scaled_ref, sums_ref):
    grad = grad_ref[...]
    scaled_ref[...] = (grad * gains_ref[row : row + 1, :]).astype(BF16)
    sums_ref[...] = jnp.sum(grad * total_of(own_ref, far_ref), axis=0, keepdims=True)


def middle_back_kernel(
    base, grad_ref, own_ref, far_ref, middle_ref, b_own_ref, b_far_ref, gains_ref, next_ref, scaled_ref, sums_ref
):
    grad_in = total_of(own_ref, far_ref)
    unit, scale = norm_parts(middle_ref[...])
    sums_ref[0:1, :] = jnp.sum(grad_in * unit, axis=0, keepdims=True)
    grad = grad_ref[...] + norm_back(unit, scale, gains_ref[base + 1 : base + 2, :], grad_in)
    next_ref[...] = grad
    sums_ref[1:2, :] = jnp.sum(grad * total_of(b_own_ref, b_far_ref), axis=0, keepdims=True)
    scaled_ref[...] = (grad * gains_ref[base + 2 : base + 3, :]).astype(BF16)


def first_back_kernel(base, grad_ref, own_ref, far_ref, h_ref, gains_ref, next_ref, sums_ref):
    grad_in = total_of(own_ref, far_ref)
    unit, scale = norm_parts(h_ref[...])
    sums_ref[...] = jnp.sum(grad_in * unit, axis=0, keepdims=True)
    next_ref[...] = grad_ref[...] + norm_back(unit, scale, gains_ref[base : base + 1, :], grad_in)


def last_back_kernel(order_ref, facts_ref, grad_ref, own_ref, far_ref, h_ref, gains_ref, out_ref, sums_ref, held):
    first_back_kernel(0, grad_ref, own_ref, far_ref, h_ref, gains_ref, held, sums_ref)
    leave(held, order_ref, facts_ref, out_ref)


def project_kernel(row_q, count, own_ref, other_ref, *refs):
    pieces = refs[:count]
    heads_ref, q_ref, kv_ref, mixed_ref = refs[count:]
    step = pl.program_id(0)
    weight = joined(pieces)
    half = own_ref.shape[0]
    mixed = jnp.concatenate([dot_nn(own_ref[...], weight), dot_nn(other_ref[...], weight)], axis=0)

    @pl.when(step < 2)
    def _():
        mixed_ref[...] = mixed
        unit, _ = head_parts(mixed)
        gain = jnp.where(step == 0, heads_ref[row_q : row_q + 1, :], heads_ref[row_q + 1 : row_q + 2, :])
        scaled = (unit * gain).astype(BF16)

        @pl.when(step == 0)
        def _():
            q_ref[...] = scaled

        @pl.when(step == 1)
        def _():
            kv_ref[...] = scaled

    @pl.when(step == 2)
    def _():
        kv_ref[...] = mixed.astype(BF16)


def project(normed, pieces, heads, row_q):
    own, other = normed
    half, wide = own.shape
    width = heads.shape[1]
    rows = [min(p.shape[0], limit) for p, limit in pieces]
    return run(
        functools.partial(project_kernel, row_q, len(pieces)),
        (3,),
        [whole(own.shape), whole(other.shape)]
        + [column(r, lambda j: j) for r in rows]
        + [whole(heads.shape)],
        [
            whole((2 * half, width)),
            column(2 * half, lambda j: jnp.maximum(j - 1, 0)),
            column(2 * half, lambda j: jnp.minimum(j, 1)),
        ],
        [
            shaped(2 * half, width, dtype=BF16),
            shaped(2 * half, 2 * width, dtype=BF16),
            shaped(2 * half, 2 * width),
        ],
        [],
        [own, other] + [p for p, _ in pieces] + [heads],
        5,
    )


def project_back_kernel(row_q, count, dq_ref, dkv_ref, mixed_ref, heads_ref, *refs):
    pieces = refs[:count]
    grad_ref, other_ref, own_ref, sums_ref, acc = refs[count:]
    step = pl.program_id(0)

    @pl.when(step == 0)
    def _():
        acc[...] = jnp.zeros_like(acc)

    def normed(incoming, row, place):
        unit, scale = head_parts(mixed_ref[...])
        sums_ref[place : place + 1, :] = jnp.sum(incoming * unit, axis=0, keepdims=True)
        grad_ref[...] = head_back(unit, scale, heads_ref[row : row + 1, :], incoming).astype(BF16)

    @pl.when(step == 0)
    def _():
        normed(dq_ref[...], row_q, 0)

    @pl.when(step == 1)
    def _():
        normed(dkv_ref[...].astype(F32), row_q + 1, 1)

    @pl.when(step == 2)
    def _():
        grad_ref[...] = dkv_ref[...].astype(BF16)

    acc[...] += dot_nt(grad_ref[...], joined(pieces))

    @pl.when(step == 2)
    def _():
        half = own_ref.shape[0]
        own_ref[...] = acc[:half, :]
        other_ref[...] = acc[half:, :].astype(BF16)


def project_back(dq, dkv, mixed, pieces, heads, row_q, wide):
    full, width = dq.shape
    rows = [min(p.shape[0], limit) for p, limit in pieces]
    return run(
        functools.partial(project_back_kernel, row_q, len(pieces)),
        (3,),
        [
            whole(dq.shape),
            column(full, lambda j: jnp.maximum(j - 1, 0)),
            column(full, lambda j: jnp.minimum(j, 1)),
            whole(heads.shape),
        ]
        + [column(r, lambda j: j) for r in rows],
        [column(full, lambda j: j), whole((full // 2, wide)), whole((full // 2, wide)), whole((2, width))],
        [
            shaped(full, 3 * width, dtype=BF16),
            shaped(full // 2, wide, dtype=BF16),
            shaped(full // 2, wide),
            shaped(2, width),
        ],
        [pltpu.VMEM((full, wide), F32)],
        [dq, dkv, mixed, heads] + [p for p, _ in pieces],
        6,
    )


def feed_kernel(count, own_ref, other_ref, *refs):
    ups, downs = refs[:count], refs[count : 2 * count]
    values_ref, active_ref, part_other_ref, part_own_ref, acc = refs[2 * count :]
    step = pl.program_id(0)

    @pl.when(step == 0)
    def _():
        acc[...] = jnp.zeros_like(acc)

    weight = joined(ups)
    half = own_ref.shape[0]
    for source, start in ((own_ref, 0), (other_ref, half)):
        values = dot_nn(source[...], weight)
        values_ref[start : start + half, :] = values
        active_ref[start : start + half, :] = (
            0.5 * values * (1.0 + lax.erf(values * F32(ROOT_HALF)))
        ).astype(BF16)
    acc[...] += dot_nt(active_ref[...], joined(downs))

    @pl.when(step == pl.num_programs(0) - 1)
    def _():
        part_own_ref[...] = acc[:half, :]
        part_other_ref[...] = acc[half:, :].astype(BF16)


def feed(second, pieces, hidden):
    own, other = second
    half, wide = own.shape
    steps = hidden // TILE
    rows = [min(p.shape[0], limit) for p, limit in pieces]
    arrays = [p for p, _ in pieces]
    return run(
        functools.partial(feed_kernel, len(pieces)),
        (steps,),
        [whole(own.shape), whole(other.shape)]
        + [column(r, lambda j: j) for r in rows]
        + [column(r, lambda j: j + steps) for r in rows],
        [
            column(2 * half, lambda j: j),
            column(2 * half, lambda j: j),
            whole((half, wide)),
            whole((half, wide)),
        ],
        [
            shaped(2 * half, hidden),
            shaped(2 * half, hidden, dtype=BF16),
            shaped(half, wide, dtype=BF16),
            shaped(half, wide),
        ],
        [pltpu.VMEM((2 * half, wide), F32)],
        [own, other] + arrays + arrays,
        7,
    )


def feed_back_kernel(count, own_ref, other_ref, values_ref, *refs):
    ups, downs = refs[:count], refs[count : 2 * count]
    grad_ref, part_other_ref, part_own_ref, acc = refs[2 * count :]
    step = pl.program_id(0)

    @pl.when(step == 0)
    def _():
        acc[...] = jnp.zeros_like(acc)

    weight = joined(downs)
    half = own_ref.shape[0]
    for source, start in ((own_ref, 0), (other_ref, half)):
        incoming = dot_nn(source[...], weight)
        values = values_ref[start : start + half, :]
        slope = 0.5 * (1.0 + lax.erf(values * F32(ROOT_HALF))) + values * (
            jnp.exp(-0.5 * values * values) * F32(BELL)
        )
        grad_ref[start : start + half, :] = (incoming * slope).astype(BF16)
    acc[...] += dot_nt(grad_ref[...], joined(ups))

    @pl.when(step == pl.num_programs(0) - 1)
    def _():
        part_own_ref[...] = acc[:half, :]
        part_other_ref[...] = acc[half:, :].astype(BF16)


def feed_back(grads, values, pieces):
    own, other = grads
    half, wide = own.shape
    hidden = values.shape[1]
    steps = hidden // TILE
    rows = [min(p.shape[0], limit) for p, limit in pieces]
    arrays = [p for p, _ in pieces]
    return run(
        functools.partial(feed_back_kernel, len(pieces)),
        (steps,),
        [whole(own.shape), whole(other.shape), column(2 * half, lambda j: j)]
        + [column(r, lambda j: j) for r in rows]
        + [column(r, lambda j: j + steps) for r in rows],
        [column(2 * half, lambda j: j), whole((half, wide)), whole((half, wide))],
        [
            shaped(2 * half, hidden, dtype=BF16),
            shaped(half, wide, dtype=BF16),
            shaped(half, wide),
        ],
        [pltpu.VMEM((2 * half, wide), F32)],
        [own, other, values] + arrays + arrays,
        8,
    )


def weight_kernel(split, rows, a_own, a_other, b_own, b_other, first_ref, second_ref, *refs):
    outs, turned = refs[:-1], refs[-1]
    step = pl.program_id(0)
    half = a_own.shape[0]

    def turn(own, other):
        turned[:, :half] = own[...].T
        turned[:, half:] = other[...].T

    @pl.when(step == 0)
    def _():
        turn(a_own, a_other)

    @pl.when(step == split)
    def _():
        turn(b_own, b_other)

    def store(right):
        start = 0
        for out, count in zip(outs, rows, strict=True):
            out[...] = dot_nn(turned[start : start + count, :], right).astype(BF16)
            start += count

    @pl.when(step < split)
    def _():
        store(first_ref[...])

    @pl.when(step >= split)
    def _():
        store(second_ref[...])


def weight_grads(a, first, b, second, rows, us):
    half, wide = a[0].shape
    split = first.shape[1] // TILE
    steps = split + second.shape[1] // TILE
    return run(
        functools.partial(weight_kernel, split, rows),
        (steps,),
        [whole((half, wide))] * 4
        + [
            column(2 * half, lambda j: jnp.minimum(j, split - 1)),
            column(2 * half, lambda j: jnp.maximum(j - split, 0)),
        ],
        [column(r, lambda j: j) for r in rows],
        [shaped(r, steps * TILE, dtype=BF16) for r in rows],
        [pltpu.VMEM((wide, 2 * half), BF16)],
        [*a, *b, first, second],
        us,
    )


def finish_ff_kernel(own_ref, right_ref, left_ref, *refs):
    up_ref, down_ref = refs[-2:]
    hidden = up_ref.shape[2]
    up_ref[0] = total_of(own_ref.at[:, :hidden], right_ref.at[:, :hidden]) + left_ref[:, :hidden].astype(F32)
    down = total_of(own_ref.at[:, hidden:], right_ref.at[:, hidden:]) + left_ref[:, hidden:].astype(F32)
    down_ref[0] = down.T


def finish_at_kernel(own_ref, right_ref, left_ref, *refs):
    qkv_ref, out_ref = refs[-2:]
    width = qkv_ref.shape[3]
    for i in range(4):
        lanes = slice(i * width, (i + 1) * width)
        part = total_of(own_ref.at[:, lanes], right_ref.at[:, lanes]) + left_ref[:, lanes].astype(F32)
        if i < 3:
            qkv_ref[0, i] = part
        else:
            out_ref[0] = part.T


def finish(kernel, parts, shapes, block, earlier):
    specs = [
        pl.BlockSpec((1,) + s[1:], functools.partial(lambda b, r, *_: (b,) + (0,) * (r - 1), block, len(s)))
        for s in shapes
    ]
    return run(
        kernel,
        (1,),
        [whole(p.shape) for p in parts] + [pl.BlockSpec(memory_space=pl.ANY)] * len(earlier),
        specs,
        [shaped(*s) for s in shapes],
        [],
        [*parts, *earlier],
        2,
        aliases={3 + i: i for i in range(len(earlier))},
    )


def fetch_start(table_ref, sources, ring, buffer, sems, count):
    flen = buffer.shape[1]
    for j in range(count):
        if not ring:
            start = pl.multiple_of(table_ref[j] * flen, flen)
            pltpu.make_async_copy(sources[0].at[pl.ds(start, flen)], buffer.at[j], sems.at[j]).start()
            continue
        for k in range(8):

            @pl.when(table_ref[j] == k)
            def _(j=j, k=k):
                if k == 4:
                    cut = sources[4].shape[0]
                    pltpu.make_async_copy(sources[4], buffer.at[j, pl.ds(0, cut)], sems.at[j]).start()
                    pltpu.make_async_copy(
                        sources[5], buffer.at[j, pl.ds(cut, flen - cut)], sems.at[j]
                    ).start()
                else:
                    source = sources[k if k < 4 else k + 1]
                    pltpu.make_async_copy(source, buffer.at[j], sems.at[j]).start()


def fetch_wait(sources, buffer, sems, j):
    pltpu.make_async_copy(buffer.at[j], buffer.at[j], sems.at[j]).wait()


def attend_kernel(ring, n_kv, count, table_ref, lens_ref, facts_ref, q_ref, *refs):
    sources, pieces = refs[:n_kv], refs[n_kv : n_kv + count]
    out_ref, lse_ref, part_other_ref, part_own_ref = refs[n_kv + count : n_kv + count + 4]
    acc, sums, buffer, sems = refs[n_kv + count + 4 :]
    step = pl.program_id(0)
    steps = buffer.shape[0]
    rows, width = q_ref.shape
    heads = width // HEAD_DIM

    @pl.when(step == 0)
    def _():
        fetch_start(table_ref, sources, ring, buffer, sems, steps)
        acc[...] = jnp.zeros_like(acc)
        sums[...] = jnp.ones_like(sums)
        sums[:heads, :] = jnp.zeros((heads, rows), F32)

    fetch_wait(sources, buffer, sems, step)
    live = live_keys(buffer.shape[1], facts_ref[1], lens_ref[table_ref[step]])
    keys = buffer[step, :, :width]
    values_t = buffer[step, :, width:].T
    queries = q_ref[...]
    for head in range(heads):
        mine = jnp.where(head_mask(queries.shape, head), queries, 0) * BF16(SCALING)
        scores = dot_nt(keys, mine)
        powers = jnp.where(live, jnp.exp(scores), 0.0)
        sums[head : head + 1, :] += jnp.sum(powers, axis=0, keepdims=True)
        lanes = slice(head * HEAD_DIM, (head + 1) * HEAD_DIM)
        acc[lanes, :] += dot_nn(values_t[lanes, :], powers.astype(BF16))

    @pl.when(step == steps - 1)
    def _():
        lse_ref[...] = jnp.log(sums[...])
        for head in range(heads):
            lanes = slice(head * HEAD_DIM, (head + 1) * HEAD_DIM)
            acc[lanes, :] = acc[lanes, :] / sums[head : head + 1, :]
        out_ref[...] = acc[...].T.astype(BF16)
        weight = joined(pieces)
        half = rows // 2
        part_other_ref[...] = dot_nt(out_ref[half:, :], weight).astype(BF16)
        part_own_ref[...] = dot_nt(out_ref[:half, :], weight)


def attend(queries, sources, ring, pieces, table, lens, facts, wide):
    rows, width = queries.shape
    steps = table.shape[0]
    counts = [min(p.shape[0], limit) for p, limit in pieces]
    return run(
        functools.partial(attend_kernel, ring, len(sources), len(pieces)),
        (steps,),
        [whole(queries.shape)]
        + [pl.BlockSpec(memory_space=pl.ANY)] * len(sources)
        + [column(r, lambda j: 3) for r in counts],
        [whole((rows, width)), whole((8, rows)), whole((rows // 2, wide)), whole((rows // 2, wide))],
        [
            shaped(rows, width, dtype=BF16),
            shaped(8, rows),
            shaped(rows // 2, wide, dtype=BF16),
            shaped(rows // 2, wide),
        ],
        [
            pltpu.VMEM((width, rows), F32),
            pltpu.VMEM((8, rows), F32),
            pltpu.VMEM((steps, rows, 2 * width), BF16),
            pltpu.SemaphoreType.DMA((steps,)),
        ],
        [table, lens, facts, queries, *sources] + [p for p, _ in pieces],
        3 + 2 * steps,
        prefetch=3,
    )


def attend_back_kernel(ring, n_kv, count, n_out, table_ref, lens_ref, facts_ref, *refs):
    q_ref, o_ref, lse_ref, g_own_ref, g_other_ref = refs[:5]
    refs = refs[5:]
    sources, pieces = refs[:n_kv], refs[n_kv : n_kv + count]
    dq_ref = refs[n_kv + count]
    outs = refs[n_kv + count + 1 : n_kv + count + 1 + n_out]
    acc, delta, grads, buffer, sems = refs[n_kv + count + 1 + n_out :]
    step = pl.program_id(0)
    steps = buffer.shape[0]
    rows, width = q_ref.shape
    heads = width // HEAD_DIM
    half = rows // 2

    @pl.when(step == 0)
    def _():
        fetch_start(table_ref, sources, ring, buffer, sems, steps)
        acc[...] = jnp.zeros_like(acc)
        if ring:
            for out in outs:
                out[...] = jnp.zeros_like(out)
        weight = joined(pieces)
        grads[:half, :] = dot_nn(g_own_ref[...], weight).astype(BF16)
        grads[half:, :] = dot_nn(g_other_ref[...], weight).astype(BF16)
        turned = (grads[...].astype(F32) * o_ref[...].astype(F32)).T
        for head in range(heads):
            lanes = slice(head * HEAD_DIM, (head + 1) * HEAD_DIM)
            delta[head : head + 1, :] = jnp.sum(turned[lanes, :], axis=0, keepdims=True)

    fetch_wait(sources, buffer, sems, step)
    live = live_keys(buffer.shape[1], facts_ref[1], lens_ref[table_ref[step]])
    keys = buffer[step, :, :width]
    values = buffer[step, :, width:]
    keys_t = keys.T
    queries = q_ref[...]
    incoming = grads[...]
    grad_k = jnp.zeros(keys.shape, F32)
    grad_v = jnp.zeros(keys.shape, F32)
    for head in range(heads):
        inside = head_mask(queries.shape, head)
        mine = jnp.where(inside, queries, 0) * BF16(SCALING)
        mine_g = jnp.where(inside, incoming, 0)
        scores = dot_nt(keys, mine)
        full = jnp.where(live, jnp.exp(scores - lse_ref[head : head + 1, :]), 0.0)
        grad_probs = dot_nt(values, mine_g)
        steep = (full * (grad_probs - delta[head : head + 1, :])).astype(BF16)
        grad_v += dot_nn(full.astype(BF16), mine_g)
        grad_k += dot_nn(steep, mine)
        lanes = slice(head * HEAD_DIM, (head + 1) * HEAD_DIM)
        acc[lanes, :] += dot_nn(keys_t[lanes, :], steep)

    if not ring:
        outs[0][0, :, :width] = grad_k.astype(outs[0].dtype)
        outs[0][0, :, width:] = grad_v.astype(outs[0].dtype)
    else:
        for k in range(8):

            @pl.when(table_ref[step] == k)
            def _(k=k):
                if k == 4:
                    cut = outs[4].shape[0]
                    outs[4][:, :width] = grad_k[:cut].astype(BF16)
                    outs[4][:, width:] = grad_v[:cut].astype(BF16)
                    outs[5][:, :width] = grad_k[cut:].astype(BF16)
                    outs[5][:, width:] = grad_v[cut:].astype(BF16)
                else:
                    out = outs[k if k < 4 else k + 1]
                    out[:, :width] = grad_k.astype(BF16)
                    out[:, width:] = grad_v.astype(BF16)

    @pl.when(step == steps - 1)
    def _():
        dq_ref[...] = acc[...].T * F32(SCALING)


def attend_back(queries, grads, attended, lse, sources, ring, pieces, table, lens, facts, dtype):
    rows, width = queries.shape
    steps = table.shape[0]
    counts = [min(p.shape[0], limit) for p, limit in pieces]
    wide = grads[0].shape[1]
    if ring:
        out_specs = [whole(s.shape) for s in sources]
        out_shape = [shaped(*s.shape, dtype=BF16) for s in sources]
    else:
        out_specs = [pl.BlockSpec((1, rows, 2 * width), lambda j, *_: (j, 0, 0))]
        out_shape = [shaped(steps, rows, 2 * width, dtype=dtype)]
    return run(
        functools.partial(attend_back_kernel, ring, len(sources), len(pieces), len(out_specs)),
        (steps,),
        [
            whole((rows, width)),
            whole((rows, width)),
            whole((8, rows)),
            whole((rows // 2, wide)),
            whole((rows // 2, wide)),
        ]
        + [pl.BlockSpec(memory_space=pl.ANY)] * len(sources)
        + [column(r, lambda j: 3) for r in counts],
        [whole((rows, width))] + out_specs,
        [shaped(rows, width)] + out_shape,
        [
            pltpu.VMEM((width, rows), F32),
            pltpu.VMEM((8, rows), F32),
            pltpu.VMEM((rows, width), BF16),
            pltpu.VMEM((steps, rows, 2 * width), BF16),
            pltpu.SemaphoreType.DMA((steps,)),
        ],
        [table, lens, facts, queries, attended, lse, *grads, *sources] + [p for p, _ in pieces],
        4 + 4 * steps,
        prefetch=3,
    )


def per_device(
    block_input,
    cotangent,
    frame_lengths,
    frame_scenes,
    qkv_weight,
    out_weight,
    up_weight,
    down_weight,
    block_gains,
):
    quarter, wide = block_input.shape
    frames = lax.axis_size("frame")
    ring = on_ring()
    my_frame = lax.axis_index("frame")
    my_row = lax.axis_index("row")
    chip, core = my_row // 2, my_row % 2
    width = qkv_weight.shape[3]
    hidden = up_weight.shape[2]
    shard = wide // frames
    half = 2 * quarter
    facts = jnp.stack([chip, core, frame_lengths[my_frame]]).astype(jnp.int32)

    if ring:
        walk = jnp.array(RING, jnp.int32)
        at = jnp.argmax(walk == my_frame).astype(jnp.int32)
        order = lax.dynamic_slice_in_dim(jnp.concatenate([walk, walk]), at, frames)
        lane_order = order
    else:
        order = jnp.arange(frames, dtype=jnp.int32)
        lane_order = jnp.arange(wide // LANES, dtype=jnp.int32)
    rel_lens = frame_lengths[order]
    other_scene = (frame_scenes[order] != frame_scenes[my_frame]).astype(jnp.int32)
    scene_table = jnp.argsort(other_scene, stable=True)[: frames // 2].astype(jnp.int32)
    frame_table = jnp.zeros((1,), jnp.int32)
    frame_lens = frame_lengths[my_frame].reshape(1)

    qkv_shard = jnp.transpose(qkv_weight, (0, 2, 1, 3))
    if ring:
        packed = []
        for block in range(2):
            lead = shard + (16 if block == 0 else 0)
            pick = lambda s, b=block: pl.BlockSpec((1,) + s[1:], lambda *_: (b,) + (0,) * (len(s) - 1))
            packed.append(
                run(
                    functools.partial(pack_kernel, block == 0),
                    (1,),
                    [
                        pick(qkv_shard.shape),
                        pick(out_weight.shape),
                        pick(up_weight.shape),
                        pick(down_weight.shape),
                        whole(block_gains.shape),
                    ],
                    [whole((lead, 4 * width)), whole((shard, 2 * hidden))],
                    [shaped(lead, 4 * width, dtype=BF16), shaped(shard, 2 * hidden, dtype=BF16)],
                    [],
                    [qkv_shard, out_weight, up_weight, down_weight, block_gains],
                    2,
                )
            )
        limits = [shard] * 4 + [shard // 2] * 2 + [shard] * 3
        weights = []
        for block in range(2):
            at_pieces = ring_gather(packed[block][0], shard // 2)
            ff_pieces = ring_gather(packed[block][1], shard // 2)
            weights.append((list(zip(at_pieces, limits)), list(zip(ff_pieces, limits))))
        raw = [p for p, _ in weights[0][0]]
        gain_sources = raw[:4] + raw[5:]
        gain_specs = [
            pl.BlockSpec((16, LANES), functools.partial(lambda r, *_: (r, 0), (p.shape[0] - 16) // 16))
            for p in gain_sources
        ]
        inverse = jnp.argmax(order[None, :] == (2 * my_row + jnp.arange(2))[:, None], axis=1)
        gains, heads = run(
            gains_kernel,
            (1,),
            gain_specs,
            [whole((16, wide)), whole((16, width))],
            [shaped(16, wide), shaped(16, width)],
            [],
            [inverse.astype(jnp.int32), *gain_sources],
            1,
            prefetch=1,
        )
    else:
        limits = [wide]
        weights = []
        for block in range(2):
            at = jnp.concatenate(
                [qkv_shard[block, 0], qkv_shard[block, 1], qkv_shard[block, 2], out_weight[block].T], axis=1
            )
            ff = jnp.concatenate([up_weight[block], down_weight[block].T], axis=1)
            weights.append(
                tuple([(lax.all_gather(w, "frame", axis=0, tiled=True), wide)] for w in (at, ff))
            )
        gains = lax.all_gather(block_gains, "frame", axis=2, tiled=True).astype(F32).reshape(12, wide)
        gains = jnp.concatenate([gains, jnp.zeros((4, wide), F32)])
        heads = lax.dynamic_slice_in_dim(gains, my_row * width, width, 1)
    piece_rows = limits

    def enter(values, masked):
        return run(
            functools.partial(enter_kernel, masked),
            (1,),
            [whole(values.shape)] * 2,
            whole((half, wide)),
            shaped(half, wide),
            [],
            [lane_order, facts, values, row_take(values, 2)],
            1,
            prefetch=2,
        )

    big = whole((half, wide))
    gspec = whole(gains.shape)

    def reduce_rows(other, own):
        near = (own + row_take(other, 1).astype(F32)).astype(BF16)
        return near, row_take(near, 2)

    h = enter(block_input, False)
    normed = run(
        functools.partial(first_norm_kernel, 0),
        (1,),
        [big, gspec],
        big,
        shaped(half, wide, dtype=BF16),
        [],
        [h, gains],
        1,
    )
    stored = []
    output = None
    for block in range(2):
        base = 6 * block
        at, ff = weights[block]
        normed = (normed, row_take(normed, 1))
        queries, kv, mixed = project(normed, at, heads, base + 4)
        if block == 0:
            sources, walking, table, lens = [kv], False, frame_table, frame_lens
        else:
            table, lens, walking = scene_table, rel_lens, ring
            sources = ring_gather(kv, half) if ring else [lax.all_gather(kv, "frame", axis=0, tiled=True)]
        attended, lse, part_other, part_own = attend(
            queries, sources, walking, at, table, lens, facts, wide
        )
        branch = reduce_rows(part_other, part_own)
        middle, second = run(
            functools.partial(residual_kernel, base + 2, base + 1),
            (1,),
            [big, big, big, gspec],
            [big, big],
            [shaped(half, wide), shaped(half, wide, dtype=BF16)],
            [],
            [h, *branch, gains],
            2,
        )
        second = (second, row_take(second, 1))
        up_values, active, part_other, part_own = feed(second, ff, hidden)
        down = reduce_rows(part_other, part_own)
        stored.append(
            (h, normed, queries, mixed, (sources, walking, table, lens), attended, lse, branch)
            + (middle, second, up_values, active, down)
        )
        if block == 0:
            h, normed = run(
                functools.partial(residual_kernel, base + 3, base + 6),
                (1,),
                [big, big, big, gspec],
                [big, big],
                [shaped(half, wide), shaped(half, wide, dtype=BF16)],
                [],
                [middle, *down, gains],
                2,
            )
        else:
            output = run(
                functools.partial(output_kernel, base + 3),
                (1,),
                [big, big, big, gspec],
                whole((quarter, wide)),
                shaped(quarter, wide, dtype=BF16),
                [pltpu.VMEM((half, wide), F32)],
                [lane_order, facts, middle, *down, gains],
                1,
                prefetch=2,
            )

    grad = enter(cotangent, True)
    at_shapes = [(2, 3, shard, width), (2, width, shard)]
    ff_shapes = [(2, shard, hidden), (2, hidden, shard)]
    at_out, ff_out = [], []
    gain_sums = [None, None]
    input_grad = None
    for block in (1, 0):
        base = 6 * block
        at, ff = weights[block]
        h, normed, queries, mixed, keys, attended, lse, branch, middle, second, up_values, active, down = stored[
            block
        ]
        sources, walking, table, lens = keys
        scaled, sum_three = run(
            functools.partial(seed_kernel, base + 3),
            (1,),
            [big, big, big, gspec],
            [big, whole((1, wide))],
            [shaped(half, wide, dtype=BF16), shaped(1, wide)],
            [],
            [grad, *down, gains],
            1,
        )
        grad_down = (scaled, row_take(scaled, 1))
        grad_up, part_other, part_own = feed_back(grad_down, up_values, ff)
        incoming = reduce_rows(part_other, part_own)
        ff_grads = weight_grads(second, grad_up, grad_down, active, piece_rows, 8)
        grad_middle, scaled, sums_middle = run(
            functools.partial(middle_back_kernel, base),
            (1,),
            [big] * 6 + [gspec],
            [big, big, whole((2, wide))],
            [shaped(half, wide), shaped(half, wide, dtype=BF16), shaped(2, wide)],
            [],
            [grad, *incoming, middle, *branch, gains],
            2,
        )
        grad_branch = (scaled, row_take(scaled, 1))
        dq, *dkv_parts = attend_back(
            queries,
            grad_branch,
            attended,
            lse,
            sources,
            walking,
            at,
            table,
            lens,
            facts,
            F32 if block == 0 else BF16,
        )
        if block == 0:
            dkv = dkv_parts[0][0]
        elif ring:
            own, right, left = ring_scatter(dkv_parts)
            dkv = own.astype(F32) + right.astype(F32) + left.astype(F32)
        else:
            spread = jnp.zeros((frames,) + dkv_parts[0].shape[1:], BF16).at[table].set(dkv_parts[0])
            dkv = lax.psum_scatter(spread, "frame", scatter_dimension=0, tiled=False).astype(F32)
        grad_mixed, part_other, part_own, sums_heads = project_back(
            dq, dkv, mixed, at, heads, base + 4, wide
        )
        incoming = reduce_rows(part_other, part_own)
        at_grads = weight_grads(normed, grad_mixed, grad_branch, attended, piece_rows, 4)
        if block == 1:
            grad, sum_zero = run(
                functools.partial(first_back_kernel, base),
                (1,),
                [big] * 4 + [gspec],
                [big, whole((1, wide))],
                [shaped(half, wide), shaped(1, wide)],
                [],
                [grad_middle, *incoming, h, gains],
                2,
            )
        else:
            input_grad, sum_zero = run(
                last_back_kernel,
                (1,),
                [big] * 4 + [gspec],
                [whole((quarter, wide)), whole((1, wide))],
                [shaped(quarter, wide, dtype=BF16), shaped(1, wide)],
                [pltpu.VMEM((half, wide), F32)],
                [lane_order, facts, grad_middle, *incoming, h, gains],
                2,
                prefetch=2,
            )
        gain_sums[block] = (
            jnp.concatenate([sum_zero, sums_middle, sum_three]) * F32(0.5),
            sums_heads,
        )
        if ring:
            ff_out = finish(finish_ff_kernel, ring_scatter(ff_grads), ff_shapes, block, ff_out)
            at_out = finish(finish_at_kernel, ring_scatter(at_grads), at_shapes, block, at_out)
        else:
            ff_sum = lax.psum_scatter(ff_grads[0], "frame", scatter_dimension=0, tiled=True).astype(F32)
            at_sum = lax.psum_scatter(at_grads[0], "frame", scatter_dimension=0, tiled=True).astype(F32)
            ff_out = [(ff_sum[:, :hidden], ff_sum[:, hidden:].T)] + ff_out
            at_out = [
                (
                    jnp.stack([at_sum[:, i * width : (i + 1) * width] for i in range(3)]),
                    at_sum[:, 3 * width :].T,
                )
            ] + at_out
    if not ring:
        ff_out = [jnp.stack(both) for both in zip(*ff_out, strict=True)]
        at_out = [jnp.stack(both) for both in zip(*at_out, strict=True)]

    rows = jnp.stack([gain_sums[0][0], gain_sums[1][0]])
    blocks = rows.reshape(2, 4, wide // LANES, LANES)
    rows = jnp.zeros_like(blocks).at[:, :, lane_order].set(blocks).reshape(2, 4, wide)
    per_head = lax.dynamic_update_slice_in_dim(
        jnp.zeros((2, 2, wide), F32),
        jnp.stack([gain_sums[0][1], gain_sums[1][1]]),
        my_row * width,
        2,
    )
    total = lax.psum(jnp.concatenate([rows, per_head], axis=1), ("frame", "row"))
    gains_grad = lax.dynamic_slice_in_dim(total, my_frame * shard, shard, 2)
    return (
        output,
        input_grad,
        jnp.transpose(at_out[0], (0, 2, 1, 3)),
        at_out[1],
        ff_out[0],
        ff_out[1],
        gains_grad,
    )


def solution(mesh):
    return jax.shard_map(
        per_device,
        mesh=mesh,
        in_specs=(
            P(("frame", "row"), None),
            P(("frame", "row"), None),
            P(),
            P(),
            P(None, "frame", None, "row"),
            P(None, "row", "frame"),
            P(None, "frame", "row"),
            P(None, "row", "frame"),
            P(None, None, "frame"),
        ),
        out_specs=(
            P(("frame", "row"), None),
            P(("frame", "row"), None),
            P(None, "frame", None, "row"),
            P(None, "row", "frame"),
            P(None, "frame", "row"),
            P(None, "row", "frame"),
            P(None, None, "frame"),
        ),
        check_vma=False,
    )
```

```python
import functools

import jax
import jax.numpy as jnp
from jax import lax
from jax.experimental import pallas as pl
from jax.experimental.pallas import tpu as pltpu
from jax.sharding import PartitionSpec as P

HEAD_DIM = 64
EPSILON = 1e-06
F32 = jnp.float32
BF16 = jnp.bfloat16
LANES = 128
TILE = 256
ROOT_HALF = 0.7071067811865476
BELL = 0.3989422804014327
SCALING = HEAD_DIM**-0.5

RING = (0, 2, 4, 6, 7, 5, 3, 1)


def on_ring():
    return lax.axis_size("frame") == len(RING)


def frame_groups():
    return [list(RING)] if on_ring() else None


def frame_order(frames):
    return RING if on_ring() else tuple(range(frames))


def ring_take(value, step):
    count = len(RING)
    return lax.ppermute(value, "frame", [(RING[(i + step) % count], RING[i]) for i in range(count)])


def row_take(value, bit):
    return lax.ppermute(value, "row", [(i ^ bit, i) for i in range(4)])


def ring_gather(shard, cut):
    ahead, behind = [shard], [shard]
    for _ in range(3):
        ahead.append(ring_take(ahead[-1], 1))
        behind.append(ring_take(behind[-1], -1))
    far_low = ring_take(ahead[3][:cut], 1)
    far_high = ring_take(behind[3][cut:], -1)
    return ahead + [far_low, far_high] + behind[3:0:-1]


def add_pair(a, b):
    return (a.astype(F32) + b.astype(F32)).astype(BF16)


def ring_scatter(pieces):
    ahead = pieces[1:4]
    far_low, far_high = pieces[4:6]
    behind = pieces[8:5:-1]
    cut = far_low.shape[0]
    low = ring_take(far_low, -1)
    high = ring_take(far_high, 1)
    right = jnp.concatenate([add_pair(ahead[2][:cut], low), ahead[2][cut:]])
    left = jnp.concatenate([behind[2][:cut], add_pair(behind[2][cut:], high)])
    for place in (1, 0):
        right = add_pair(ahead[place], ring_take(right, -1))
        left = add_pair(behind[place], ring_take(left, 1))
    return pieces[0], ring_take(right, -1), ring_take(left, 1)


def dot_nt(a, b):
    return lax.dot_general(a, b, (((1,), (1,)), ((), ())), preferred_element_type=F32)


def dot_nn(a, b):
    return lax.dot_general(a, b, (((1,), (0,)), ((), ())), preferred_element_type=F32)


def whole(shape):
    return pl.BlockSpec(shape, lambda *_: (0,) * len(shape))


def column(rows, place):
    return pl.BlockSpec((rows, TILE), lambda j, *_: (0, place(j)))


WEIGH = 3.0


def cost(us):
    return pl.CostEstimate(
        flops=int(us * WEIGH * 1.0e9), bytes_accessed=int(us * WEIGH * 2.0e6), transcendentals=0
    )


def run(kernel, grid, in_specs, out_specs, out_shape, scratch, operands, us, prefetch=0, aliases=None, after=()):
    count = len(operands)

    def body(*refs):
        kernel(*refs[:count], *refs[count + len(after) :])

    in_specs = list(in_specs) + [pl.BlockSpec(memory_space=pl.ANY)] * len(after)
    operands = [*operands, *after]
    return pl.pallas_call(
        body,
        grid_spec=pltpu.PrefetchScalarGridSpec(
            num_scalar_prefetch=prefetch,
            grid=grid,
            in_specs=in_specs,
            out_specs=out_specs,
            scratch_shapes=scratch,
        ),
        out_shape=out_shape,
        input_output_aliases=aliases or {},
        compiler_params=pltpu.CompilerParams(vmem_limit_bytes=56 * 1024 * 1024),
        cost_estimate=cost(us),
    )(*operands)


def shaped(*shape, dtype=F32):
    return jax.ShapeDtypeStruct(shape, dtype)


def norm_parts(values):
    center = values - jnp.mean(values, axis=-1, keepdims=True)
    scale = lax.rsqrt(jnp.mean(center * center, axis=-1, keepdims=True) + EPSILON)
    return center * scale, scale


def norm_back(unit, scale, gain, grad):
    inner = grad * gain
    return scale * (
        inner
        - jnp.mean(inner, axis=-1, keepdims=True)
        - unit * jnp.mean(inner * unit, axis=-1, keepdims=True)
    )


def head_means(values):
    width = values.shape[-1]
    rows = lax.broadcasted_iota(jnp.int32, (width, width), 0) // HEAD_DIM
    cols = lax.broadcasted_iota(jnp.int32, (width, width), 1) // HEAD_DIM
    spread = jnp.where(rows == cols, F32(1.0 / HEAD_DIM), F32(0)).astype(BF16)
    high = values.astype(BF16)
    low = (values - high.astype(F32)).astype(BF16)
    return dot_nn(high, spread) + dot_nn(low, spread)


def head_parts(values):
    center = values - head_means(values)
    scale = lax.rsqrt(head_means(center * center) + EPSILON)
    return center * scale, scale


def head_back(unit, scale, gain, grad):
    inner = grad * gain
    return scale * (inner - head_means(inner) - unit * head_means(inner * unit))


def joined(refs):
    if len(refs) == 1:
        return refs[0][...]
    return jnp.concatenate([ref[...] for ref in refs], axis=0)


def head_mask(shape, head):
    lanes = lax.broadcasted_iota(jnp.int32, shape, 1)
    return (lanes // HEAD_DIM) == head


def live_keys(count, core, length):
    place = lax.broadcasted_iota(jnp.int32, (count, 1), 0)
    quarter = count // 4
    half = place // (2 * quarter)
    chip = (place // quarter) % 2
    slot = (chip * 2 + (half ^ core)) * quarter + place % quarter
    return slot < length


def pack_at_kernel(qkv_ref, out_ref, at_ref):
    rows = out_ref.shape[2]
    width = qkv_ref.shape[3]
    for i in range(3):
        at_ref[:rows, i * width : (i + 1) * width] = qkv_ref[0, i]
    at_ref[:rows, 3 * width :] = out_ref[0].T


def pack_ff_kernel(up_ref, down_ref, ff_ref):
    ff = up_ref.shape[2]
    ff_ref[:, :ff] = up_ref[0]
    ff_ref[:, ff:] = down_ref[0].T


def gain_sums_kernel(order, facts_ref, *refs):
    out_ref = refs[-1]
    out_ref[...] = jnp.zeros_like(out_ref)
    row = facts_ref[0] * 2 + facts_ref[1]
    for block in range(2):
        zero, middle, three, heads = refs[4 * block : 4 * block + 4]
        base = 6 * block
        for k in range(out_ref.shape[0]):
            lanes = slice(k * LANES, (k + 1) * LANES)
            place = order[k]
            out_ref[place, base : base + 1, :] = zero[:, lanes]
            out_ref[place, base + 1 : base + 3, :] = middle[:, lanes] * 0.5
            out_ref[place, base + 3 : base + 4, :] = three[:, lanes] * 0.5
        for k in range(2):
            lanes = slice(k * LANES, (k + 1) * LANES)
            out_ref[row * 2 + k, base + 4 : base + 6, :] = heads[:, lanes]


def enter_kernel(masked, order, facts_ref, own_ref, far_ref, out_ref):
    rows = own_ref.shape[0]
    chip, core, length = facts_ref[0], facts_ref[1], facts_ref[2]
    for k in range(len(order)):
        lanes = slice(order[k] * LANES, (order[k] + 1) * LANES)
        for source, place in ((own_ref, chip), (far_ref, 1 - chip)):
            values = source[:, lanes].astype(F32)
            if masked:
                slots = (place * 2 + core) * rows + lax.broadcasted_iota(jnp.int32, (rows, 1), 0)
                values = jnp.where(slots < length, values, 0.0)
            start = pl.multiple_of(place * rows, rows)
            out_ref[pl.ds(start, rows), k * LANES : (k + 1) * LANES] = values


def leave(values_ref, order, facts_ref, out_ref):
    rows = out_ref.shape[0]
    start = pl.multiple_of(facts_ref[0] * rows, rows)
    for k in range(len(order)):
        lanes = slice(order[k] * LANES, (order[k] + 1) * LANES)
        values = values_ref[pl.ds(start, rows), k * LANES : (k + 1) * LANES]
        out_ref[:, lanes] = values.astype(out_ref.dtype)


def first_norm_kernel(row, h_ref, gains_ref, normed_ref):
    unit, _ = norm_parts(h_ref[...])
    normed_ref[...] = (unit * gains_ref[row : row + 1, :]).astype(BF16)


def total_of(own_ref, far_ref):
    return own_ref[...].astype(F32) + far_ref[...].astype(F32)


def residual_kernel(scale_row, norm_row, h_ref, own_ref, far_ref, gains_ref, next_ref, normed_ref):
    value = h_ref[...] + gains_ref[scale_row : scale_row + 1, :] * total_of(own_ref, far_ref)
    next_ref[...] = value
    unit, _ = norm_parts(value)
    normed_ref[...] = (unit * gains_ref[norm_row : norm_row + 1, :]).astype(BF16)


def output_kernel(scale_row, order, facts_ref, h_ref, own_ref, far_ref, gains_ref, out_ref, held):
    held[...] = h_ref[...] + gains_ref[scale_row : scale_row + 1, :] * total_of(own_ref, far_ref)
    leave(held, order, facts_ref, out_ref)


def seed_kernel(row, grad_ref, own_ref, far_ref, gains_ref, scaled_ref, sums_ref):
    grad = grad_ref[...]
    scaled_ref[...] = (grad * gains_ref[row : row + 1, :]).astype(BF16)
    sums_ref[...] = jnp.sum(grad * total_of(own_ref, far_ref), axis=0, keepdims=True)


def middle_back_kernel(
    base, grad_ref, own_ref, far_ref, middle_ref, b_own_ref, b_far_ref, gains_ref, next_ref, scaled_ref, sums_ref
):
    grad_in = total_of(own_ref, far_ref)
    unit, scale = norm_parts(middle_ref[...])
    sums_ref[0:1, :] = jnp.sum(grad_in * unit, axis=0, keepdims=True)
    grad = grad_ref[...] + norm_back(unit, scale, gains_ref[base + 1 : base + 2, :], grad_in)
    next_ref[...] = grad
    sums_ref[1:2, :] = jnp.sum(grad * total_of(b_own_ref, b_far_ref), axis=0, keepdims=True)
    scaled_ref[...] = (grad * gains_ref[base + 2 : base + 3, :]).astype(BF16)


def first_back_kernel(base, grad_ref, own_ref, far_ref, h_ref, gains_ref, next_ref):
    grad_in = total_of(own_ref, far_ref)
    unit, scale = norm_parts(h_ref[...])
    next_ref[...] = grad_ref[...] + norm_back(unit, scale, gains_ref[base : base + 1, :], grad_in)


def last_back_kernel(order, facts_ref, grad_ref, own_ref, far_ref, h_ref, gains_ref, out_ref, held):
    first_back_kernel(0, grad_ref, own_ref, far_ref, h_ref, gains_ref, held)
    leave(held, order, facts_ref, out_ref)


def project_kernel(row_q, count, own_ref, other_ref, *refs):
    pieces = refs[:count]
    heads_ref, q_ref, kv_ref, mixed_ref = refs[count:]
    step = pl.program_id(0)
    weight = joined(pieces)
    half = own_ref.shape[0]
    mixed = jnp.concatenate([dot_nn(own_ref[...], weight), dot_nn(other_ref[...], weight)], axis=0)

    @pl.when(step < 2)
    def _():
        mixed_ref[...] = mixed
        unit, _ = head_parts(mixed)
        gain = jnp.where(step == 0, heads_ref[row_q : row_q + 1, :], heads_ref[row_q + 1 : row_q + 2, :])
        scaled = (unit * gain).astype(BF16)

        @pl.when(step == 0)
        def _():
            q_ref[...] = scaled

        @pl.when(step == 1)
        def _():
            kv_ref[...] = scaled

    @pl.when(step == 2)
    def _():
        kv_ref[...] = mixed.astype(BF16)


def project(normed, pieces, heads, row_q):
    own, other = normed
    half, wide = own.shape
    width = heads.shape[1]
    rows = [min(p.shape[0], limit) for p, limit in pieces]
    return run(
        functools.partial(project_kernel, row_q, len(pieces)),
        (3,),
        [whole(own.shape), whole(other.shape)]
        + [column(r, lambda j: j) for r in rows]
        + [whole(heads.shape)],
        [
            whole((2 * half, width)),
            column(2 * half, lambda j: jnp.maximum(j - 1, 0)),
            column(2 * half, lambda j: jnp.minimum(j, 1)),
        ],
        [
            shaped(2 * half, width, dtype=BF16),
            shaped(2 * half, 2 * width, dtype=BF16),
            shaped(2 * half, 2 * width),
        ],
        [],
        [own, other] + [p for p, _ in pieces] + [heads],
        5,
    )


def project_back_kernel(row_q, count, dq_ref, dkv_ref, mixed_ref, heads_ref, n_own_ref, n_other_ref, gains_ref, *refs):
    pieces = refs[:count]
    grad_ref, other_ref, own_ref, sums_ref, zero_ref, acc = refs[count:]
    step = pl.program_id(0)

    @pl.when(step == 0)
    def _():
        acc[...] = jnp.zeros_like(acc)

    def normed(incoming, row, place):
        unit, scale = head_parts(mixed_ref[...])
        sums_ref[place : place + 1, :] = jnp.sum(incoming * unit, axis=0, keepdims=True)
        grad_ref[...] = head_back(unit, scale, heads_ref[row : row + 1, :], incoming).astype(BF16)

    @pl.when(step == 0)
    def _():
        normed(dq_ref[...], row_q, 0)

    @pl.when(step == 1)
    def _():
        normed(dkv_ref[...].astype(F32), row_q + 1, 1)

    @pl.when(step == 2)
    def _():
        grad_ref[...] = dkv_ref[...].astype(BF16)

    acc[...] += dot_nt(grad_ref[...], joined(pieces))

    @pl.when(step == 2)
    def _():
        half = own_ref.shape[0]
        own_ref[...] = acc[:half, :]
        other_ref[...] = acc[half:, :].astype(BF16)
        products = acc[:half, :] * n_own_ref[...].astype(F32) + acc[half:, :] * n_other_ref[...].astype(F32)
        row_g = row_q - 4
        zero_ref[...] = jnp.sum(products, axis=0, keepdims=True) / gains_ref[row_g : row_g + 1, :]


def project_back(dq, dkv, mixed, pieces, heads, row_q, normed, gains):
    full, width = dq.shape
    wide = gains.shape[1]
    rows = [min(p.shape[0], limit) for p, limit in pieces]
    return run(
        functools.partial(project_back_kernel, row_q, len(pieces)),
        (3,),
        [
            whole(dq.shape),
            column(full, lambda j: jnp.maximum(j - 1, 0)),
            column(full, lambda j: jnp.minimum(j, 1)),
            whole(heads.shape),
            whole((full // 2, wide)),
            whole((full // 2, wide)),
            whole(gains.shape),
        ]
        + [column(r, lambda j: j) for r in rows],
        [
            column(full, lambda j: j),
            whole((full // 2, wide)),
            whole((full // 2, wide)),
            whole((2, width)),
            whole((1, wide)),
        ],
        [
            shaped(full, 3 * width, dtype=BF16),
            shaped(full // 2, wide, dtype=BF16),
            shaped(full // 2, wide),
            shaped(2, width),
            shaped(1, wide),
        ],
        [pltpu.VMEM((full, wide), F32)],
        [dq, dkv, mixed, heads, *normed, gains] + [p for p, _ in pieces],
        6,
    )


def feed_kernel(count, own_ref, other_ref, *refs):
    ups, downs = refs[:count], refs[count : 2 * count]
    values_ref, active_ref, part_other_ref, part_own_ref, acc = refs[2 * count :]
    step = pl.program_id(0)

    @pl.when(step == 0)
    def _():
        acc[...] = jnp.zeros_like(acc)

    weight = joined(ups)
    half = own_ref.shape[0]
    for source, start in ((own_ref, 0), (other_ref, half)):
        values = dot_nn(source[...], weight)
        values_ref[start : start + half, :] = values
        active_ref[start : start + half, :] = (
            0.5 * values * (1.0 + lax.erf(values * F32(ROOT_HALF)))
        ).astype(BF16)
    acc[...] += dot_nt(active_ref[...], joined(downs))

    @pl.when(step == pl.num_programs(0) - 1)
    def _():
        part_own_ref[...] = acc[:half, :]
        part_other_ref[...] = acc[half:, :].astype(BF16)


def feed(second, pieces, hidden):
    own, other = second
    half, wide = own.shape
    steps = hidden // TILE
    rows = [min(p.shape[0], limit) for p, limit in pieces]
    arrays = [p for p, _ in pieces]
    return run(
        functools.partial(feed_kernel, len(pieces)),
        (steps,),
        [whole(own.shape), whole(other.shape)]
        + [column(r, lambda j: j) for r in rows]
        + [column(r, lambda j: j + steps) for r in rows],
        [
            column(2 * half, lambda j: j),
            column(2 * half, lambda j: j),
            whole((half, wide)),
            whole((half, wide)),
        ],
        [
            shaped(2 * half, hidden),
            shaped(2 * half, hidden, dtype=BF16),
            shaped(half, wide, dtype=BF16),
            shaped(half, wide),
        ],
        [pltpu.VMEM((2 * half, wide), F32)],
        [own, other] + arrays + arrays,
        7,
    )


def feed_back_kernel(count, own_ref, other_ref, values_ref, *refs):
    ups, downs = refs[:count], refs[count : 2 * count]
    grad_ref, part_other_ref, part_own_ref, acc = refs[2 * count :]
    step = pl.program_id(0)

    @pl.when(step == 0)
    def _():
        acc[...] = jnp.zeros_like(acc)

    weight = joined(downs)
    half = own_ref.shape[0]
    for source, start in ((own_ref, 0), (other_ref, half)):
        incoming = dot_nn(source[...], weight)
        values = values_ref[start : start + half, :]
        slope = 0.5 * (1.0 + lax.erf(values * F32(ROOT_HALF))) + values * (
            jnp.exp(-0.5 * values * values) * F32(BELL)
        )
        grad_ref[start : start + half, :] = (incoming * slope).astype(BF16)
    acc[...] += dot_nt(grad_ref[...], joined(ups))

    @pl.when(step == pl.num_programs(0) - 1)
    def _():
        part_own_ref[...] = acc[:half, :]
        part_other_ref[...] = acc[half:, :].astype(BF16)


def feed_back(grads, values, pieces):
    own, other = grads
    half, wide = own.shape
    hidden = values.shape[1]
    steps = hidden // TILE
    rows = [min(p.shape[0], limit) for p, limit in pieces]
    arrays = [p for p, _ in pieces]
    return run(
        functools.partial(feed_back_kernel, len(pieces)),
        (steps,),
        [whole(own.shape), whole(other.shape), column(2 * half, lambda j: j)]
        + [column(r, lambda j: j) for r in rows]
        + [column(r, lambda j: j + steps) for r in rows],
        [column(2 * half, lambda j: j), whole((half, wide)), whole((half, wide))],
        [
            shaped(2 * half, hidden, dtype=BF16),
            shaped(half, wide, dtype=BF16),
            shaped(half, wide),
        ],
        [pltpu.VMEM((2 * half, wide), F32)],
        [own, other, values] + arrays + arrays,
        8,
    )


def weight_kernel(split, a_own, a_other, b_own, b_other, first_ref, second_ref, out_ref, turned):
    step = pl.program_id(0)
    half = a_own.shape[0]

    def turn(own, other):
        turned[:, :half] = own[...].T
        turned[:, half:] = other[...].T

    @pl.when(step == 0)
    def _():
        turn(a_own, a_other)

    @pl.when(step == split)
    def _():
        turn(b_own, b_other)

    @pl.when(step < split)
    def _():
        out_ref[...] = dot_nn(turned[...], first_ref[...]).astype(BF16)

    @pl.when(step >= split)
    def _():
        out_ref[...] = dot_nn(turned[...], second_ref[...]).astype(BF16)


def weight_grads(a, first, b, second, us, after):
    half, wide = a[0].shape
    split = first.shape[1] // TILE
    steps = split + second.shape[1] // TILE
    return run(
        functools.partial(weight_kernel, split),
        (steps,),
        [whole((half, wide))] * 4
        + [
            column(2 * half, lambda j: jnp.minimum(j, split - 1)),
            column(2 * half, lambda j: jnp.maximum(j - split, 0)),
        ],
        column(wide, lambda j: j),
        shaped(wide, steps * TILE, dtype=BF16),
        [pltpu.VMEM((wide, 2 * half), BF16)],
        [*a, *b, first, second],
        us,
        after=after,
    )


def finish_ff_kernel(part_ref, *refs):
    up_ref, down_ref = refs[-2:]
    hidden = up_ref.shape[2]
    up_ref[0] = part_ref[:, :hidden].astype(F32)
    down_ref[0] = part_ref[:, hidden:].astype(F32).T


def finish_at_kernel(part_ref, *refs):
    qkv_ref, out_ref = refs[-2:]
    width = qkv_ref.shape[3]
    for i in range(3):
        qkv_ref[0, i] = part_ref[:, i * width : (i + 1) * width].astype(F32)
    out_ref[0] = part_ref[:, 3 * width :].astype(F32).T


def finish(kernel, part, shapes, block, earlier):
    specs = [
        pl.BlockSpec((1,) + s[1:], functools.partial(lambda b, r, *_: (b,) + (0,) * (r - 1), block, len(s)))
        for s in shapes
    ]
    return run(
        kernel,
        (1,),
        [whole(part.shape)] + [pl.BlockSpec(memory_space=pl.ANY)] * len(earlier),
        specs,
        [shaped(*s) for s in shapes],
        [],
        [part, *earlier],
        2,
        aliases={1 + i: i for i in range(len(earlier))},
    )


def fetch_start(table_ref, sources, ring, buffer, sems, count):
    flen = buffer.shape[1]
    for j in range(count):
        if not ring:
            start = pl.multiple_of(table_ref[j] * flen, flen)
            pltpu.make_async_copy(sources[0].at[pl.ds(start, flen)], buffer.at[j], sems.at[j]).start()
            continue
        for k in range(8):

            @pl.when(table_ref[j] == k)
            def _(j=j, k=k):
                if k == 4:
                    cut = sources[4].shape[0]
                    pltpu.make_async_copy(sources[4], buffer.at[j, pl.ds(0, cut)], sems.at[j]).start()
                    pltpu.make_async_copy(
                        sources[5], buffer.at[j, pl.ds(cut, flen - cut)], sems.at[j]
                    ).start()
                else:
                    source = sources[k if k < 4 else k + 1]
                    pltpu.make_async_copy(source, buffer.at[j], sems.at[j]).start()


def fetch_wait(sources, buffer, sems, j):
    pltpu.make_async_copy(buffer.at[j], buffer.at[j], sems.at[j]).wait()


def attend_kernel(ring, n_kv, count, table_ref, lens_ref, facts_ref, q_ref, *refs):
    sources, pieces = refs[:n_kv], refs[n_kv : n_kv + count]
    out_ref, lse_ref, part_other_ref, part_own_ref = refs[n_kv + count : n_kv + count + 4]
    acc, sums, buffer, sems = refs[n_kv + count + 4 :]
    step = pl.program_id(0)
    steps = buffer.shape[0]
    rows, width = q_ref.shape
    heads = width // HEAD_DIM

    @pl.when(step == 0)
    def _():
        fetch_start(table_ref, sources, ring, buffer, sems, steps)
        acc[...] = jnp.zeros_like(acc)
        sums[...] = jnp.ones_like(sums)
        sums[:heads, :] = jnp.zeros((heads, rows), F32)

    fetch_wait(sources, buffer, sems, step)
    live = live_keys(buffer.shape[1], facts_ref[1], lens_ref[table_ref[step]])
    keys = buffer[step, :, :width]
    values_t = buffer[step, :, width:].T
    queries = q_ref[...]
    for head in range(heads):
        mine = jnp.where(head_mask(queries.shape, head), queries, 0) * BF16(SCALING)
        scores = dot_nt(keys, mine)
        powers = jnp.where(live, jnp.exp(scores), 0.0)
        sums[head : head + 1, :] += jnp.sum(powers, axis=0, keepdims=True)
        lanes = slice(head * HEAD_DIM, (head + 1) * HEAD_DIM)
        acc[lanes, :] += dot_nn(values_t[lanes, :], powers.astype(BF16))

    @pl.when(step == steps - 1)
    def _():
        lse_ref[...] = jnp.log(sums[...])
        for head in range(heads):
            lanes = slice(head * HEAD_DIM, (head + 1) * HEAD_DIM)
            acc[lanes, :] = acc[lanes, :] / sums[head : head + 1, :]
        out_ref[...] = acc[...].T.astype(BF16)
        weight = joined(pieces)
        half = rows // 2
        part_other_ref[...] = dot_nt(out_ref[half:, :], weight).astype(BF16)
        part_own_ref[...] = dot_nt(out_ref[:half, :], weight)


def attend(queries, sources, ring, pieces, table, lens, facts, wide):
    rows, width = queries.shape
    steps = table.shape[0]
    counts = [min(p.shape[0], limit) for p, limit in pieces]
    return run(
        functools.partial(attend_kernel, ring, len(sources), len(pieces)),
        (steps,),
        [whole(queries.shape)]
        + [pl.BlockSpec(memory_space=pl.ANY)] * len(sources)
        + [column(r, lambda j: 3) for r in counts],
        [whole((rows, width)), whole((8, rows)), whole((rows // 2, wide)), whole((rows // 2, wide))],
        [
            shaped(rows, width, dtype=BF16),
            shaped(8, rows),
            shaped(rows // 2, wide, dtype=BF16),
            shaped(rows // 2, wide),
        ],
        [
            pltpu.VMEM((width, rows), F32),
            pltpu.VMEM((8, rows), F32),
            pltpu.VMEM((steps, rows, 2 * width), BF16),
            pltpu.SemaphoreType.DMA((steps,)),
        ],
        [table, lens, facts, queries, *sources] + [p for p, _ in pieces],
        3 + 2 * steps,
        prefetch=3,
    )


def attend_back_kernel(ring, n_kv, count, n_out, table_ref, lens_ref, facts_ref, *refs):
    q_ref, o_ref, lse_ref, g_own_ref, g_other_ref = refs[:5]
    refs = refs[5:]
    sources, pieces = refs[:n_kv], refs[n_kv : n_kv + count]
    dq_ref = refs[n_kv + count]
    outs = refs[n_kv + count + 1 : n_kv + count + 1 + n_out]
    acc, delta, grads, buffer, sems = refs[n_kv + count + 1 + n_out :]
    step = pl.program_id(0)
    steps = buffer.shape[0]
    rows, width = q_ref.shape
    heads = width // HEAD_DIM
    half = rows // 2

    @pl.when(step == 0)
    def _():
        fetch_start(table_ref, sources, ring, buffer, sems, steps)
        acc[...] = jnp.zeros_like(acc)
        if ring:
            for out in outs:
                out[...] = jnp.zeros_like(out)
        weight = joined(pieces)
        grads[:half, :] = dot_nn(g_own_ref[...], weight).astype(BF16)
        grads[half:, :] = dot_nn(g_other_ref[...], weight).astype(BF16)
        turned = (grads[...].astype(F32) * o_ref[...].astype(F32)).T
        for head in range(heads):
            lanes = slice(head * HEAD_DIM, (head + 1) * HEAD_DIM)
            delta[head : head + 1, :] = jnp.sum(turned[lanes, :], axis=0, keepdims=True)

    fetch_wait(sources, buffer, sems, step)
    live = live_keys(buffer.shape[1], facts_ref[1], lens_ref[table_ref[step]])
    keys = buffer[step, :, :width]
    values = buffer[step, :, width:]
    keys_t = keys.T
    queries = q_ref[...]
    incoming = grads[...]
    grad_k = jnp.zeros(keys.shape, F32)
    grad_v = jnp.zeros(keys.shape, F32)
    for head in range(heads):
        inside = head_mask(queries.shape, head)
        mine = jnp.where(inside, queries, 0) * BF16(SCALING)
        mine_g = jnp.where(inside, incoming, 0)
        scores = dot_nt(keys, mine)
        full = jnp.where(live, jnp.exp(scores - lse_ref[head : head + 1, :]), 0.0)
        grad_probs = dot_nt(values, mine_g)
        steep = (full * (grad_probs - delta[head : head + 1, :])).astype(BF16)
        grad_v += dot_nn(full.astype(BF16), mine_g)
        grad_k += dot_nn(steep, mine)
        lanes = slice(head * HEAD_DIM, (head + 1) * HEAD_DIM)
        acc[lanes, :] += dot_nn(keys_t[lanes, :], steep)

    if not ring:
        outs[0][0, :, :width] = grad_k.astype(outs[0].dtype)
        outs[0][0, :, width:] = grad_v.astype(outs[0].dtype)
    else:
        for k in range(8):

            @pl.when(table_ref[step] == k)
            def _(k=k):
                if k == 4:
                    cut = outs[4].shape[0]
                    outs[4][:, :width] = grad_k[:cut].astype(BF16)
                    outs[4][:, width:] = grad_v[:cut].astype(BF16)
                    outs[5][:, :width] = grad_k[cut:].astype(BF16)
                    outs[5][:, width:] = grad_v[cut:].astype(BF16)
                else:
                    out = outs[k if k < 4 else k + 1]
                    out[:, :width] = grad_k.astype(BF16)
                    out[:, width:] = grad_v.astype(BF16)

    @pl.when(step == steps - 1)
    def _():
        dq_ref[...] = acc[...].T * F32(SCALING)


def attend_back(queries, grads, attended, lse, sources, ring, pieces, table, lens, facts, dtype):
    rows, width = queries.shape
    steps = table.shape[0]
    counts = [min(p.shape[0], limit) for p, limit in pieces]
    wide = grads[0].shape[1]
    if ring:
        out_specs = [whole(s.shape) for s in sources]
        out_shape = [shaped(*s.shape, dtype=BF16) for s in sources]
    else:
        out_specs = [pl.BlockSpec((1, rows, 2 * width), lambda j, *_: (j, 0, 0))]
        out_shape = [shaped(steps, rows, 2 * width, dtype=dtype)]
    return run(
        functools.partial(attend_back_kernel, ring, len(sources), len(pieces), len(out_specs)),
        (steps,),
        [
            whole((rows, width)),
            whole((rows, width)),
            whole((8, rows)),
            whole((rows // 2, wide)),
            whole((rows // 2, wide)),
        ]
        + [pl.BlockSpec(memory_space=pl.ANY)] * len(sources)
        + [column(r, lambda j: 3) for r in counts],
        [whole((rows, width))] + out_specs,
        [shaped(rows, width)] + out_shape,
        [
            pltpu.VMEM((width, rows), F32),
            pltpu.VMEM((8, rows), F32),
            pltpu.VMEM((rows, width), BF16),
            pltpu.VMEM((steps, rows, 2 * width), BF16),
            pltpu.SemaphoreType.DMA((steps,)),
        ],
        [table, lens, facts, queries, attended, lse, *grads, *sources] + [p for p, _ in pieces],
        4 + 4 * steps,
        prefetch=3,
    )


def per_device(
    block_input,
    cotangent,
    frame_lengths,
    frame_scenes,
    qkv_weight,
    out_weight,
    up_weight,
    down_weight,
    block_gains,
):
    quarter, wide = block_input.shape
    frames = lax.axis_size("frame")
    ring = on_ring()
    my_frame = lax.axis_index("frame")
    my_row = lax.axis_index("row")
    chip, core = my_row // 2, my_row % 2
    width = qkv_weight.shape[3]
    hidden = up_weight.shape[2]
    shard = wide // frames
    half = 2 * quarter
    facts = jnp.stack([chip, core, frame_lengths[my_frame]]).astype(jnp.int32)

    if ring:
        walk = jnp.array(RING, jnp.int32)
        at = jnp.argmax(walk == my_frame).astype(jnp.int32)
        order = lax.dynamic_slice_in_dim(jnp.concatenate([walk, walk]), at, frames)
        lane_order = RING
    else:
        order = jnp.arange(frames, dtype=jnp.int32)
        lane_order = tuple(range(wide // LANES))
    rel_lens = frame_lengths[order]
    other_scene = (frame_scenes[order] != frame_scenes[my_frame]).astype(jnp.int32)
    scene_table = jnp.argsort(other_scene, stable=True)[: frames // 2].astype(jnp.int32)
    frame_table = jnp.zeros((1,), jnp.int32)
    frame_lens = frame_lengths[my_frame].reshape(1)

    def enter(values, masked):
        return run(
            functools.partial(enter_kernel, masked, lane_order),
            (1,),
            [whole(values.shape)] * 2,
            whole((half, wide)),
            shaped(half, wide),
            [],
            [facts, values, row_take(values, 2)],
            1,
            prefetch=1,
        )

    big = whole((half, wide))

    qkv_shard = jnp.transpose(qkv_weight, (0, 2, 1, 3))
    if ring:
        pick = lambda s, b: pl.BlockSpec((1,) + s[1:], lambda *_: (b,) + (0,) * (len(s) - 1))

        def pack_at(block):
            return run(
                pack_at_kernel,
                (1,),
                [pick(qkv_shard.shape, block), pick(out_weight.shape, block)],
                whole((shard, 4 * width)),
                shaped(shard, 4 * width, dtype=BF16),
                [],
                [qkv_shard, out_weight],
                1,
            )

        def pack_ff(block, after=()):
            return run(
                pack_ff_kernel,
                (1,),
                [pick(up_weight.shape, block), pick(down_weight.shape, block)],
                whole((shard, 2 * hidden)),
                shaped(shard, 2 * hidden, dtype=BF16),
                [],
                [up_weight, down_weight],
                1,
                after=after,
            )

    else:

        def pack_at(block):
            return jnp.concatenate([*qkv_shard[block], out_weight[block].T], axis=1)

        def pack_ff(block, after=()):
            return jnp.concatenate([up_weight[block], down_weight[block].T], axis=1)

    def gather(packed):
        return [(lax.all_gather(packed, "frame", axis=0, tiled=True, axis_index_groups=frame_groups()), wide)]

    def scatter(grads):
        return lax.psum_scatter(
            grads, "frame", scatter_dimension=0, tiled=True, axis_index_groups=frame_groups()
        )

    at_zero, ff_zero, at_one = gather(pack_at(0)), gather(pack_ff(0)), gather(pack_at(1))
    weights = [(at_zero, ff_zero), None]
    if ring:
        rows = jnp.concatenate([block_gains[0], block_gains[1], jnp.zeros((4, shard), BF16)]).astype(F32)
        spread = lax.all_to_all(jnp.broadcast_to(rows[None], (frames, 16, shard)), "frame", 0, 0)
        gains_abs = jnp.swapaxes(spread, 0, 1).reshape(16, wide)
    else:
        gains_abs = lax.all_gather(block_gains, "frame", axis=2, tiled=True).astype(F32).reshape(12, wide)
        gains_abs = jnp.concatenate([gains_abs, jnp.zeros((4, wide), F32)])
    heads = lax.dynamic_slice_in_dim(gains_abs, my_row * width, width, 1)
    gains = jnp.concatenate([gains_abs[:, k * LANES : (k + 1) * LANES] for k in lane_order], axis=1)
    h = enter(block_input, False)
    normed = run(
        functools.partial(first_norm_kernel, 0),
        (1,),
        [big, whole(gains.shape)],
        big,
        shaped(half, wide, dtype=BF16),
        [],
        [h, gains],
        1,
    )

    gspec = whole(gains.shape)

    def reduce_rows(other, own):
        near = (own + row_take(other, 1).astype(F32)).astype(BF16)
        return near, row_take(near, 2)

    stored = []
    output = None
    for block in range(2):
        base = 6 * block
        at, ff = weights[block] or (at_one, None)
        normed = (normed, row_take(normed, 1))
        queries, kv, mixed = project(normed, at, heads, base + 4)
        if block == 0:
            sources, walking, table, lens = [kv], False, frame_table, frame_lens
        else:
            table, lens, walking = scene_table, rel_lens, ring
            sources = ring_gather(kv, half) if ring else [lax.all_gather(kv, "frame", axis=0, tiled=True)]
            ff = gather(pack_ff(1, [sources[2], sources[7]] if ring else ()))
            weights[1] = (at, ff)
        attended, lse, part_other, part_own = attend(
            queries, sources, walking, at, table, lens, facts, wide
        )
        branch = reduce_rows(part_other, part_own)
        middle, second = run(
            functools.partial(residual_kernel, base + 2, base + 1),
            (1,),
            [big, big, big, gspec],
            [big, big],
            [shaped(half, wide), shaped(half, wide, dtype=BF16)],
            [],
            [h, *branch, gains],
            2,
        )
        second = (second, row_take(second, 1))
        up_values, active, part_other, part_own = feed(second, ff, hidden)
        down = reduce_rows(part_other, part_own)
        stored.append(
            (h, normed, queries, mixed, (sources, walking, table, lens), attended, lse, branch)
            + (middle, second, up_values, active, down)
        )
        if block == 0:
            h, normed = run(
                functools.partial(residual_kernel, base + 3, base + 6),
                (1,),
                [big, big, big, gspec],
                [big, big],
                [shaped(half, wide), shaped(half, wide, dtype=BF16)],
                [],
                [middle, *down, gains],
                2,
            )
        else:
            output = run(
                functools.partial(output_kernel, base + 3, lane_order),
                (1,),
                [big, big, big, gspec],
                whole((quarter, wide)),
                shaped(quarter, wide, dtype=BF16),
                [pltpu.VMEM((half, wide), F32)],
                [facts, middle, *down, gains],
                1,
                prefetch=1,
            )

    grad = enter(cotangent, True)
    at_shapes = [(2, 3, shard, width), (2, width, shard)]
    ff_shapes = [(2, shard, hidden), (2, hidden, shard)]
    at_out, ff_out = [], []
    gain_sums = [None, None]
    input_grad = None
    after = []
    for block in (1, 0):
        base = 6 * block
        at, ff = weights[block]
        h, normed, queries, mixed, keys, attended, lse, branch, middle, second, up_values, active, down = stored[
            block
        ]
        sources, walking, table, lens = keys
        scaled, sum_three = run(
            functools.partial(seed_kernel, base + 3),
            (1,),
            [big, big, big, gspec],
            [big, whole((1, wide))],
            [shaped(half, wide, dtype=BF16), shaped(1, wide)],
            [],
            [grad, *down, gains],
            1,
        )
        grad_down = (scaled, row_take(scaled, 1))
        grad_up, part_other, part_own = feed_back(grad_down, up_values, ff)
        incoming = reduce_rows(part_other, part_own)
        ff_grads = weight_grads(second, grad_up, grad_down, active, 8, [*after, incoming[0]])
        ff_sum = scatter(ff_grads)
        after = [ff_sum]
        grad_middle, scaled, sums_middle = run(
            functools.partial(middle_back_kernel, base),
            (1,),
            [big] * 6 + [gspec],
            [big, big, whole((2, wide))],
            [shaped(half, wide), shaped(half, wide, dtype=BF16), shaped(2, wide)],
            [],
            [grad, *incoming, middle, *branch, gains],
            2,
            after=[ff_grads],
        )
        grad_branch = (scaled, row_take(scaled, 1))
        dq, *dkv_parts = attend_back(
            queries,
            grad_branch,
            attended,
            lse,
            sources,
            walking,
            at,
            table,
            lens,
            facts,
            F32 if block == 0 else BF16,
        )
        if block == 0:
            dkv = dkv_parts[0][0]
        elif ring:
            own, right, left = ring_scatter(dkv_parts)
            dkv = own.astype(F32) + right.astype(F32) + left.astype(F32)
        else:
            spread = jnp.zeros((frames,) + dkv_parts[0].shape[1:], BF16).at[table].set(dkv_parts[0])
            dkv = lax.psum_scatter(spread, "frame", scatter_dimension=0, tiled=False).astype(F32)
        grad_mixed, part_other, part_own, sums_heads, sum_zero = project_back(
            dq, dkv, mixed, at, heads, base + 4, normed, gains
        )
        gain_sums[block] = (sum_zero, sums_middle, sum_three, sums_heads)
        incoming = reduce_rows(part_other, part_own)
        at_grads = weight_grads(normed, grad_mixed, grad_branch, attended, 4, [*after, incoming[0]])
        if block == 1:
            grad = run(
                functools.partial(first_back_kernel, base),
                (1,),
                [big] * 4 + [gspec],
                big,
                shaped(half, wide),
                [],
                [grad_middle, *incoming, h, gains],
                2,
                after=[at_grads],
            )
        else:
            input_grad = run(
                functools.partial(last_back_kernel, lane_order),
                (1,),
                [big] * 4 + [gspec],
                whole((quarter, wide)),
                shaped(quarter, wide, dtype=BF16),
                [pltpu.VMEM((half, wide), F32)],
                [facts, grad_middle, *incoming, h, gains],
                2,
                prefetch=1,
                after=[at_grads, ff_sum],
            )
        at_sum = scatter(at_grads)
        after = [at_sum]
        if ring:
            ff_out = finish(finish_ff_kernel, ff_sum, ff_shapes, block, ff_out)
            at_out = finish(finish_at_kernel, at_sum, at_shapes, block, at_out)
        else:
            ff_sum, at_sum = ff_sum.astype(F32), at_sum.astype(F32)
            ff_out = [(ff_sum[:, :hidden], ff_sum[:, hidden:].T)] + ff_out
            qkv_sum = jnp.stack([at_sum[:, i * width : (i + 1) * width] for i in range(3)])
            at_out = [(qkv_sum, at_sum[:, 3 * width :].T)] + at_out
    if not ring:
        ff_out = [jnp.stack(both) for both in zip(*ff_out, strict=True)]
        at_out = [jnp.stack(both) for both in zip(*at_out, strict=True)]

    if ring:
        operands = [*gain_sums[0], *gain_sums[1]]
        sent = run(
            functools.partial(gain_sums_kernel, lane_order),
            (1,),
            [whole(v.shape) for v in operands],
            whole((frames, 16, LANES)),
            shaped(frames, 16, LANES),
            [],
            [facts, *operands],
            1,
            prefetch=1,
        )
        total = jnp.sum(lax.all_to_all(sent, "frame", 0, 0), axis=0)
        total = total + row_take(total, 1)
        total = total + row_take(total, 2)
        gains_grad = total[:12].reshape(2, 6, LANES)
    else:
        rows = [jnp.concatenate([sums[0], sums[1] * F32(0.5), sums[2] * F32(0.5)]) for sums in gain_sums]
        rows = jnp.stack(rows)
        per_head = lax.dynamic_update_slice_in_dim(
            jnp.zeros((2, 2, wide), F32),
            jnp.stack([gain_sums[0][3], gain_sums[1][3]]),
            my_row * width,
            2,
        )
        total = lax.psum(jnp.concatenate([rows, per_head], axis=1), ("frame", "row"))
        gains_grad = lax.dynamic_slice_in_dim(total, my_frame * shard, shard, 2)
    return (
        output,
        input_grad,
        jnp.transpose(at_out[0], (0, 2, 1, 3)),
        at_out[1],
        ff_out[0],
        ff_out[1],
        gains_grad,
    )


def solution(mesh):
    return jax.shard_map(
        per_device,
        mesh=mesh,
        in_specs=(
            P(("frame", "row"), None),
            P(("frame", "row"), None),
            P(),
            P(),
            P(None, "frame", None, "row"),
            P(None, "row", "frame"),
            P(None, "frame", "row"),
            P(None, "row", "frame"),
            P(None, None, "frame"),
        ),
        out_specs=(
            P(("frame", "row"), None),
            P(("frame", "row"), None),
            P(None, "frame", None, "row"),
            P(None, "row", "frame"),
            P(None, "frame", "row"),
            P(None, "row", "frame"),
            P(None, None, "frame"),
        ),
        check_vma=False,
    )
```

```python
import functools

import jax
import jax.numpy as jnp
from jax import lax
from jax.experimental import pallas as pl
from jax.experimental.pallas import tpu as pltpu
from jax.sharding import PartitionSpec as P

HEAD_DIM = 64
EPSILON = 1e-06
F32 = jnp.float32
BF16 = jnp.bfloat16
LANES = 128
TILE = 256
ROOT_HALF = 0.7071067811865476
BELL = 0.3989422804014327
SCALING = HEAD_DIM**-0.5

RING = (0, 2, 4, 6, 7, 5, 3, 1)


def on_ring():
    return lax.axis_size("frame") == len(RING)


def frame_groups():
    return [list(RING)] if on_ring() else None


def frame_order(frames):
    return RING if on_ring() else tuple(range(frames))


def ring_take(value, step):
    count = len(RING)
    return lax.ppermute(value, "frame", [(RING[(i + step) % count], RING[i]) for i in range(count)])


def row_take(value, bit):
    return lax.ppermute(value, "row", [(i ^ bit, i) for i in range(4)])


def ring_gather(shard, cut):
    ahead, behind = [shard], [shard]
    for _ in range(3):
        ahead.append(ring_take(ahead[-1], 1))
        behind.append(ring_take(behind[-1], -1))
    far_low = ring_take(ahead[3][:cut], 1)
    far_high = ring_take(behind[3][cut:], -1)
    return ahead + [far_low, far_high] + behind[3:0:-1]


def add_pair(a, b):
    return (a.astype(F32) + b.astype(F32)).astype(BF16)


def ring_scatter(pieces):
    ahead = pieces[1:4]
    far_low, far_high = pieces[4:6]
    behind = pieces[8:5:-1]
    cut = far_low.shape[0]
    low = ring_take(far_low, -1)
    high = ring_take(far_high, 1)
    right = jnp.concatenate([add_pair(ahead[2][:cut], low), ahead[2][cut:]])
    left = jnp.concatenate([behind[2][:cut], add_pair(behind[2][cut:], high)])
    for place in (1, 0):
        right = add_pair(ahead[place], ring_take(right, -1))
        left = add_pair(behind[place], ring_take(left, 1))
    return (pieces[0], ring_take(right, -1), ring_take(left, 1)), [right, left]


def dot_nt(a, b):
    return lax.dot_general(a, b, (((1,), (1,)), ((), ())), preferred_element_type=F32)


def dot_nn(a, b):
    return lax.dot_general(a, b, (((1,), (0,)), ((), ())), preferred_element_type=F32)


def whole(shape):
    return pl.BlockSpec(shape, lambda *_: (0,) * len(shape))


def column(rows, place):
    return pl.BlockSpec((rows, TILE), lambda j, *_: (0, place(j)))


WEIGH = 3.0


def cost(us):
    return pl.CostEstimate(
        flops=int(us * WEIGH * 1.0e9), bytes_accessed=int(us * WEIGH * 2.0e6), transcendentals=0
    )


def run(kernel, grid, in_specs, out_specs, out_shape, scratch, operands, us, prefetch=0, aliases=None, after=()):
    count = len(operands)

    def body(*refs):
        kernel(*refs[:count], *refs[count + len(after) :])

    in_specs = list(in_specs) + [pl.BlockSpec(memory_space=pl.ANY)] * len(after)
    operands = [*operands, *after]
    return pl.pallas_call(
        body,
        grid_spec=pltpu.PrefetchScalarGridSpec(
            num_scalar_prefetch=prefetch,
            grid=grid,
            in_specs=in_specs,
            out_specs=out_specs,
            scratch_shapes=scratch,
        ),
        out_shape=out_shape,
        input_output_aliases=aliases or {},
        compiler_params=pltpu.CompilerParams(vmem_limit_bytes=56 * 1024 * 1024),
        cost_estimate=cost(us),
    )(*operands)


def shaped(*shape, dtype=F32):
    return jax.ShapeDtypeStruct(shape, dtype)


def norm_parts(values):
    center = values - jnp.mean(values, axis=-1, keepdims=True)
    scale = lax.rsqrt(jnp.mean(center * center, axis=-1, keepdims=True) + EPSILON)
    return center * scale, scale


def norm_back(unit, scale, gain, grad):
    inner = grad * gain
    return scale * (
        inner
        - jnp.mean(inner, axis=-1, keepdims=True)
        - unit * jnp.mean(inner * unit, axis=-1, keepdims=True)
    )


def head_means(values):
    width = values.shape[-1]
    rows = lax.broadcasted_iota(jnp.int32, (width, width), 0) // HEAD_DIM
    cols = lax.broadcasted_iota(jnp.int32, (width, width), 1) // HEAD_DIM
    spread = jnp.where(rows == cols, F32(1.0 / HEAD_DIM), F32(0)).astype(BF16)
    high = values.astype(BF16)
    low = (values - high.astype(F32)).astype(BF16)
    return dot_nn(high, spread) + dot_nn(low, spread)


def head_parts(values):
    center = values - head_means(values)
    scale = lax.rsqrt(head_means(center * center) + EPSILON)
    return center * scale, scale


def head_back(unit, scale, gain, grad):
    inner = grad * gain
    return scale * (inner - head_means(inner) - unit * head_means(inner * unit))


def joined(refs):
    if len(refs) == 1:
        return refs[0][...]
    return jnp.concatenate([ref[...] for ref in refs], axis=0)


def head_mask(shape, head):
    lanes = lax.broadcasted_iota(jnp.int32, shape, 1)
    return (lanes // HEAD_DIM) == head


def live_keys(count, core, length):
    place = lax.broadcasted_iota(jnp.int32, (count, 1), 0)
    quarter = count // 4
    half = place // (2 * quarter)
    chip = (place // quarter) % 2
    slot = (chip * 2 + (half ^ core)) * quarter + place % quarter
    return slot < length


def pack_at_kernel(qkv_ref, out_ref, at_ref):
    rows = out_ref.shape[2]
    width = qkv_ref.shape[3]
    for i in range(3):
        at_ref[:rows, i * width : (i + 1) * width] = qkv_ref[0, i]
    at_ref[:rows, 3 * width :] = out_ref[0].T


def pack_ff_kernel(up_ref, down_ref, ff_ref):
    ff = up_ref.shape[2]
    ff_ref[:, :ff] = up_ref[0]
    ff_ref[:, ff:] = down_ref[0].T


def gain_sums_kernel(order, facts_ref, *refs):
    out_ref = refs[-1]
    out_ref[...] = jnp.zeros_like(out_ref)
    row = facts_ref[0] * 2 + facts_ref[1]
    for block in range(2):
        zero, middle, three, heads = refs[4 * block : 4 * block + 4]
        base = 6 * block
        for k in range(out_ref.shape[0]):
            lanes = slice(k * LANES, (k + 1) * LANES)
            place = order[k]
            out_ref[place, base : base + 1, :] = zero[:, lanes]
            out_ref[place, base + 1 : base + 3, :] = middle[:, lanes] * 0.5
            out_ref[place, base + 3 : base + 4, :] = three[:, lanes] * 0.5
        for k in range(2):
            lanes = slice(k * LANES, (k + 1) * LANES)
            out_ref[row * 2 + k, base + 4 : base + 6, :] = heads[:, lanes]


def enter_kernel(masked, order, facts_ref, own_ref, far_ref, out_ref):
    rows = own_ref.shape[0]
    chip, core, length = facts_ref[0], facts_ref[1], facts_ref[2]
    for k in range(len(order)):
        lanes = slice(order[k] * LANES, (order[k] + 1) * LANES)
        for source, place in ((own_ref, chip), (far_ref, 1 - chip)):
            values = source[:, lanes].astype(F32)
            if masked:
                slots = (place * 2 + core) * rows + lax.broadcasted_iota(jnp.int32, (rows, 1), 0)
                values = jnp.where(slots < length, values, 0.0)
            start = pl.multiple_of(place * rows, rows)
            out_ref[pl.ds(start, rows), k * LANES : (k + 1) * LANES] = values


def leave(values_ref, order, facts_ref, out_ref):
    rows = out_ref.shape[0]
    start = pl.multiple_of(facts_ref[0] * rows, rows)
    for k in range(len(order)):
        lanes = slice(order[k] * LANES, (order[k] + 1) * LANES)
        values = values_ref[pl.ds(start, rows), k * LANES : (k + 1) * LANES]
        out_ref[:, lanes] = values.astype(out_ref.dtype)


def first_norm_kernel(row, h_ref, gains_ref, normed_ref):
    unit, _ = norm_parts(h_ref[...])
    normed_ref[...] = (unit * gains_ref[row : row + 1, :]).astype(BF16)


def total_of(own_ref, far_ref):
    return own_ref[...].astype(F32) + far_ref[...].astype(F32)


def residual_kernel(scale_row, norm_row, h_ref, own_ref, far_ref, gains_ref, next_ref, normed_ref):
    value = h_ref[...] + gains_ref[scale_row : scale_row + 1, :] * total_of(own_ref, far_ref)
    next_ref[...] = value
    unit, _ = norm_parts(value)
    normed_ref[...] = (unit * gains_ref[norm_row : norm_row + 1, :]).astype(BF16)


def add_kernel(own_ref, other_ref, sum_ref):
    sum_ref[...] = (own_ref[...] + other_ref[...].astype(F32)).astype(BF16)


def output_kernel(scale_row, order, facts_ref, h_ref, own_ref, far_ref, gains_ref, grad_ref, out_ref, sums_ref, held):
    total = total_of(own_ref, far_ref)
    held[...] = h_ref[...] + gains_ref[scale_row : scale_row + 1, :] * total
    sums_ref[...] = jnp.sum(grad_ref[...] * total, axis=0, keepdims=True)
    leave(held, order, facts_ref, out_ref)


def scale_kernel(row, grad_ref, gains_ref, scaled_ref):
    scaled_ref[...] = (grad_ref[...] * gains_ref[row : row + 1, :]).astype(BF16)


def middle_back_kernel(
    base, grad_ref, own_ref, far_ref, middle_ref, b_own_ref, b_far_ref, gains_ref, next_ref, scaled_ref, sums_ref
):
    grad_in = total_of(own_ref, far_ref)
    unit, scale = norm_parts(middle_ref[...])
    sums_ref[0:1, :] = jnp.sum(grad_in * unit, axis=0, keepdims=True)
    grad = grad_ref[...] + norm_back(unit, scale, gains_ref[base + 1 : base + 2, :], grad_in)
    next_ref[...] = grad
    sums_ref[1:2, :] = jnp.sum(grad * total_of(b_own_ref, b_far_ref), axis=0, keepdims=True)
    scaled_ref[...] = (grad * gains_ref[base + 2 : base + 3, :]).astype(BF16)


def first_back(base, grad_ref, own_ref, far_ref, h_ref, gains_ref):
    unit, scale = norm_parts(h_ref[...])
    return grad_ref[...] + norm_back(unit, scale, gains_ref[base : base + 1, :], total_of(own_ref, far_ref))


def between_kernel(
    base, grad_ref, own_ref, far_ref, h_ref, gains_ref, d_own_ref, d_far_ref, next_ref, scaled_ref, sums_ref
):
    grad = first_back(base, grad_ref, own_ref, far_ref, h_ref, gains_ref)
    next_ref[...] = grad
    scaled_ref[...] = (grad * gains_ref[base - 3 : base - 2, :]).astype(BF16)
    sums_ref[...] = jnp.sum(grad * total_of(d_own_ref, d_far_ref), axis=0, keepdims=True)


def last_back_kernel(order, facts_ref, grad_ref, own_ref, far_ref, h_ref, gains_ref, out_ref, held):
    held[...] = first_back(0, grad_ref, own_ref, far_ref, h_ref, gains_ref)
    leave(held, order, facts_ref, out_ref)


def project_kernel(row_q, count, own_ref, other_ref, *refs):
    pieces = refs[:count]
    heads_ref, q_ref, kv_ref, mixed_ref = refs[count:]
    step = pl.program_id(0)
    weight = joined(pieces)
    half = own_ref.shape[0]
    mixed = jnp.concatenate([dot_nn(own_ref[...], weight), dot_nn(other_ref[...], weight)], axis=0)

    @pl.when(step < 2)
    def _():
        mixed_ref[...] = mixed
        unit, _ = head_parts(mixed)
        gain = jnp.where(step == 0, heads_ref[row_q : row_q + 1, :], heads_ref[row_q + 1 : row_q + 2, :])
        scaled = (unit * gain).astype(BF16)

        @pl.when(step == 0)
        def _():
            q_ref[...] = scaled

        @pl.when(step == 1)
        def _():
            kv_ref[...] = scaled

    @pl.when(step == 2)
    def _():
        kv_ref[...] = mixed.astype(BF16)


def project(normed, pieces, heads, row_q, after):
    own, other = normed
    half, wide = own.shape
    width = heads.shape[1]
    rows = [min(p.shape[0], limit) for p, limit in pieces]
    return run(
        functools.partial(project_kernel, row_q, len(pieces)),
        (3,),
        [whole(own.shape), whole(other.shape)]
        + [column(r, lambda j: j) for r in rows]
        + [whole(heads.shape)],
        [
            whole((2 * half, width)),
            column(2 * half, lambda j: jnp.maximum(j - 1, 0)),
            column(2 * half, lambda j: jnp.minimum(j, 1)),
        ],
        [
            shaped(2 * half, width, dtype=BF16),
            shaped(2 * half, 2 * width, dtype=BF16),
            shaped(2 * half, 2 * width),
        ],
        [],
        [own, other] + [p for p, _ in pieces] + [heads],
        5,
        after=after,
    )


def project_back_kernel(row_q, count, dq_ref, dkv_ref, mixed_ref, heads_ref, n_own_ref, n_other_ref, gains_ref, *refs):
    pieces = refs[:count]
    grad_ref, other_ref, own_ref, sums_ref, zero_ref, acc = refs[count:]
    step = pl.program_id(0)

    @pl.when(step == 0)
    def _():
        acc[...] = jnp.zeros_like(acc)

    def normed(incoming, row, place):
        unit, scale = head_parts(mixed_ref[...])
        sums_ref[place : place + 1, :] = jnp.sum(incoming * unit, axis=0, keepdims=True)
        grad_ref[...] = head_back(unit, scale, heads_ref[row : row + 1, :], incoming).astype(BF16)

    @pl.when(step == 0)
    def _():
        normed(dq_ref[...], row_q, 0)

    @pl.when(step == 1)
    def _():
        normed(dkv_ref[...].astype(F32), row_q + 1, 1)

    @pl.when(step == 2)
    def _():
        grad_ref[...] = dkv_ref[...].astype(BF16)

    acc[...] += dot_nt(grad_ref[...], joined(pieces))

    @pl.when(step == 2)
    def _():
        half = own_ref.shape[0]
        own_ref[...] = acc[:half, :]
        other_ref[...] = acc[half:, :].astype(BF16)
        products = acc[:half, :] * n_own_ref[...].astype(F32) + acc[half:, :] * n_other_ref[...].astype(F32)
        row_g = row_q - 4
        zero_ref[...] = jnp.sum(products, axis=0, keepdims=True) / gains_ref[row_g : row_g + 1, :]


def project_back(dq, dkv, mixed, pieces, heads, row_q, normed, gains, after):
    full, width = dq.shape
    wide = gains.shape[1]
    rows = [min(p.shape[0], limit) for p, limit in pieces]
    return run(
        functools.partial(project_back_kernel, row_q, len(pieces)),
        (3,),
        [
            whole(dq.shape),
            column(full, lambda j: jnp.maximum(j - 1, 0)),
            column(full, lambda j: jnp.minimum(j, 1)),
            whole(heads.shape),
            whole((full // 2, wide)),
            whole((full // 2, wide)),
            whole(gains.shape),
        ]
        + [column(r, lambda j: j) for r in rows],
        [
            column(full, lambda j: j),
            whole((full // 2, wide)),
            whole((full // 2, wide)),
            whole((2, width)),
            whole((1, wide)),
        ],
        [
            shaped(full, 3 * width, dtype=BF16),
            shaped(full // 2, wide, dtype=BF16),
            shaped(full // 2, wide),
            shaped(2, width),
            shaped(1, wide),
        ],
        [pltpu.VMEM((full, wide), F32)],
        [dq, dkv, mixed, heads, *normed, gains] + [p for p, _ in pieces],
        6,
        after=after,
    )


def feed_kernel(count, own_ref, other_ref, *refs):
    ups, downs = refs[:count], refs[count : 2 * count]
    values_ref, active_ref, part_other_ref, part_own_ref, acc = refs[2 * count :]
    step = pl.program_id(0)

    @pl.when(step == 0)
    def _():
        acc[...] = jnp.zeros_like(acc)

    weight = joined(ups)
    half = own_ref.shape[0]
    for source, start in ((own_ref, 0), (other_ref, half)):
        values = dot_nn(source[...], weight)
        values_ref[start : start + half, :] = values
        active_ref[start : start + half, :] = (
            0.5 * values * (1.0 + lax.erf(values * F32(ROOT_HALF)))
        ).astype(BF16)
    acc[...] += dot_nt(active_ref[...], joined(downs))

    @pl.when(step == pl.num_programs(0) - 1)
    def _():
        part_own_ref[...] = acc[:half, :]
        part_other_ref[...] = acc[half:, :].astype(BF16)


def feed(second, pieces, hidden):
    own, other = second
    half, wide = own.shape
    steps = hidden // TILE
    rows = [min(p.shape[0], limit) for p, limit in pieces]
    arrays = [p for p, _ in pieces]
    return run(
        functools.partial(feed_kernel, len(pieces)),
        (steps,),
        [whole(own.shape), whole(other.shape)]
        + [column(r, lambda j: j) for r in rows]
        + [column(r, lambda j: j + steps) for r in rows],
        [
            column(2 * half, lambda j: j),
            column(2 * half, lambda j: j),
            whole((half, wide)),
            whole((half, wide)),
        ],
        [
            shaped(2 * half, hidden),
            shaped(2 * half, hidden, dtype=BF16),
            shaped(half, wide, dtype=BF16),
            shaped(half, wide),
        ],
        [pltpu.VMEM((2 * half, wide), F32)],
        [own, other] + arrays + arrays,
        7,
    )


def feed_back_kernel(count, own_ref, other_ref, values_ref, *refs):
    ups, downs = refs[:count], refs[count : 2 * count]
    grad_ref, part_other_ref, part_own_ref, acc = refs[2 * count :]
    step = pl.program_id(0)

    @pl.when(step == 0)
    def _():
        acc[...] = jnp.zeros_like(acc)

    weight = joined(downs)
    half = own_ref.shape[0]
    for source, start in ((own_ref, 0), (other_ref, half)):
        incoming = dot_nn(source[...], weight)
        values = values_ref[start : start + half, :]
        slope = 0.5 * (1.0 + lax.erf(values * F32(ROOT_HALF))) + values * (
            jnp.exp(-0.5 * values * values) * F32(BELL)
        )
        grad_ref[start : start + half, :] = (incoming * slope).astype(BF16)
    acc[...] += dot_nt(grad_ref[...], joined(ups))

    @pl.when(step == pl.num_programs(0) - 1)
    def _():
        part_own_ref[...] = acc[:half, :]
        part_other_ref[...] = acc[half:, :].astype(BF16)


def feed_back(grads, values, pieces):
    own, other = grads
    half, wide = own.shape
    hidden = values.shape[1]
    steps = hidden // TILE
    rows = [min(p.shape[0], limit) for p, limit in pieces]
    arrays = [p for p, _ in pieces]
    return run(
        functools.partial(feed_back_kernel, len(pieces)),
        (steps,),
        [whole(own.shape), whole(other.shape), column(2 * half, lambda j: j)]
        + [column(r, lambda j: j) for r in rows]
        + [column(r, lambda j: j + steps) for r in rows],
        [column(2 * half, lambda j: j), whole((half, wide)), whole((half, wide))],
        [
            shaped(2 * half, hidden, dtype=BF16),
            shaped(half, wide, dtype=BF16),
            shaped(half, wide),
        ],
        [pltpu.VMEM((2 * half, wide), F32)],
        [own, other, values] + arrays + arrays,
        8,
    )


def weight_kernel(split, a_own, a_other, b_own, b_other, first_ref, second_ref, out_ref, turned):
    step = pl.program_id(0)
    half = a_own.shape[0]

    def turn(own, other):
        turned[:, :half] = own[...].T
        turned[:, half:] = other[...].T

    @pl.when(step == 0)
    def _():
        turn(a_own, a_other)

    @pl.when(step == split)
    def _():
        turn(b_own, b_other)

    @pl.when(step < split)
    def _():
        out_ref[...] = dot_nn(turned[...], first_ref[...]).astype(BF16)

    @pl.when(step >= split)
    def _():
        out_ref[...] = dot_nn(turned[...], second_ref[...]).astype(BF16)


def gate_kernel(*refs):
    pass


def gate(value, after):
    anywhere = pl.BlockSpec(memory_space=pl.ANY)
    return run(
        gate_kernel, (1,), [anywhere], anywhere, jax.ShapeDtypeStruct(value.shape, value.dtype), [], [value], 0.1,
        aliases={0: 0}, after=after,
    )


def one_weight_kernel(own, other, right_ref, out_ref, turned):
    half = own.shape[0]

    @pl.when(pl.program_id(0) == 0)
    def _():
        turned[:, :half] = own[...].T
        turned[:, half:] = other[...].T

    out_ref[...] = dot_nn(turned[...], right_ref[...]).astype(BF16)


def one_weight_grads(a, right, us, after):
    half, wide = a[0].shape
    return run(
        one_weight_kernel,
        (right.shape[1] // TILE,),
        [whole((half, wide))] * 2 + [column(2 * half, lambda j: j)],
        column(wide, lambda j: j),
        shaped(wide, right.shape[1], dtype=BF16),
        [pltpu.VMEM((wide, 2 * half), BF16)],
        [*a, right],
        us,
        after=after,
    )


def weight_grads(a, first, b, second, us, after):
    half, wide = a[0].shape
    split = first.shape[1] // TILE
    steps = split + second.shape[1] // TILE
    return run(
        functools.partial(weight_kernel, split),
        (steps,),
        [whole((half, wide))] * 4
        + [
            column(2 * half, lambda j: jnp.minimum(j, split - 1)),
            column(2 * half, lambda j: jnp.maximum(j - split, 0)),
        ],
        column(wide, lambda j: j),
        shaped(wide, steps * TILE, dtype=BF16),
        [pltpu.VMEM((wide, 2 * half), BF16)],
        [*a, *b, first, second],
        us,
        after=after,
    )


def finish_ff_kernel(part_ref, *refs):
    up_ref, down_ref = refs[-2:]
    hidden = up_ref.shape[2]
    up_ref[0] = part_ref[:, :hidden].astype(F32)
    down_ref[0] = part_ref[:, hidden:].astype(F32).T


def finish_two_kernel(up_part_ref, down_part_ref, up_ref, down_ref):
    up_ref[0] = up_part_ref[...].astype(F32)
    down_ref[0] = down_part_ref[...].astype(F32).T


def finish_at_kernel(part_ref, *refs):
    qkv_ref, out_ref = refs[-2:]
    width = qkv_ref.shape[3]
    for i in range(3):
        qkv_ref[0, i] = part_ref[:, i * width : (i + 1) * width].astype(F32)
    out_ref[0] = part_ref[:, 3 * width :].astype(F32).T


def finish(kernel, parts, shapes, block, earlier):
    specs = [
        pl.BlockSpec((1,) + s[1:], functools.partial(lambda b, r, *_: (b,) + (0,) * (r - 1), block, len(s)))
        for s in shapes
    ]
    return run(
        kernel,
        (1,),
        [whole(part.shape) for part in parts] + [pl.BlockSpec(memory_space=pl.ANY)] * len(earlier),
        specs,
        [shaped(*s) for s in shapes],
        [],
        [*parts, *earlier],
        2,
        aliases={len(parts) + i: i for i in range(len(earlier))},
    )


def fetch_start(table_ref, sources, ring, buffer, sems, count):
    flen = buffer.shape[1]
    for j in range(count):
        if not ring:
            start = pl.multiple_of(table_ref[j] * flen, flen)
            pltpu.make_async_copy(sources[0].at[pl.ds(start, flen)], buffer.at[j], sems.at[j]).start()
            continue
        for k in range(8):

            @pl.when(table_ref[j] == k)
            def _(j=j, k=k):
                if k == 4:
                    cut = sources[4].shape[0]
                    pltpu.make_async_copy(sources[4], buffer.at[j, pl.ds(0, cut)], sems.at[j]).start()
                    pltpu.make_async_copy(
                        sources[5], buffer.at[j, pl.ds(cut, flen - cut)], sems.at[j]
                    ).start()
                else:
                    source = sources[k if k < 4 else k + 1]
                    pltpu.make_async_copy(source, buffer.at[j], sems.at[j]).start()


def fetch_wait(sources, buffer, sems, j):
    pltpu.make_async_copy(buffer.at[j], buffer.at[j], sems.at[j]).wait()


def attend_kernel(ring, n_kv, count, table_ref, lens_ref, facts_ref, q_ref, *refs):
    sources, pieces = refs[:n_kv], refs[n_kv : n_kv + count]
    out_ref, lse_ref, part_other_ref, part_own_ref = refs[n_kv + count : n_kv + count + 4]
    acc, sums, buffer, sems = refs[n_kv + count + 4 :]
    step = pl.program_id(0)
    steps = buffer.shape[0]
    rows, width = q_ref.shape
    heads = width // HEAD_DIM

    @pl.when(step == 0)
    def _():
        fetch_start(table_ref, sources, ring, buffer, sems, steps)
        acc[...] = jnp.zeros_like(acc)
        sums[...] = jnp.ones_like(sums)
        sums[:heads, :] = jnp.zeros((heads, rows), F32)

    fetch_wait(sources, buffer, sems, step)
    live = live_keys(buffer.shape[1], facts_ref[1], lens_ref[table_ref[step]])
    keys = buffer[step, :, :width]
    values_t = buffer[step, :, width:].T
    queries = q_ref[...]
    for head in range(heads):
        mine = jnp.where(head_mask(queries.shape, head), queries, 0) * BF16(SCALING)
        scores = dot_nt(keys, mine)
        powers = jnp.where(live, jnp.exp(scores), 0.0)
        sums[head : head + 1, :] += jnp.sum(powers, axis=0, keepdims=True)
        lanes = slice(head * HEAD_DIM, (head + 1) * HEAD_DIM)
        acc[lanes, :] += dot_nn(values_t[lanes, :], powers.astype(BF16))

    @pl.when(step == steps - 1)
    def _():
        lse_ref[...] = jnp.log(sums[...])
        for head in range(heads):
            lanes = slice(head * HEAD_DIM, (head + 1) * HEAD_DIM)
            acc[lanes, :] = acc[lanes, :] / sums[head : head + 1, :]
        out_ref[...] = acc[...].T.astype(BF16)
        weight = joined(pieces)
        half = rows // 2
        part_other_ref[...] = dot_nt(out_ref[half:, :], weight).astype(BF16)
        part_own_ref[...] = dot_nt(out_ref[:half, :], weight)


def attend(queries, sources, ring, pieces, table, lens, facts, wide):
    rows, width = queries.shape
    steps = table.shape[0]
    counts = [min(p.shape[0], limit) for p, limit in pieces]
    return run(
        functools.partial(attend_kernel, ring, len(sources), len(pieces)),
        (steps,),
        [whole(queries.shape)]
        + [pl.BlockSpec(memory_space=pl.ANY)] * len(sources)
        + [column(r, lambda j: 3) for r in counts],
        [whole((rows, width)), whole((8, rows)), whole((rows // 2, wide)), whole((rows // 2, wide))],
        [
            shaped(rows, width, dtype=BF16),
            shaped(8, rows),
            shaped(rows // 2, wide, dtype=BF16),
            shaped(rows // 2, wide),
        ],
        [
            pltpu.VMEM((width, rows), F32),
            pltpu.VMEM((8, rows), F32),
            pltpu.VMEM((steps, rows, 2 * width), BF16),
            pltpu.SemaphoreType.DMA((steps,)),
        ],
        [table, lens, facts, queries, *sources] + [p for p, _ in pieces],
        3 + 2 * steps,
        prefetch=3,
    )


def attend_back_kernel(ring, n_kv, count, n_out, table_ref, lens_ref, facts_ref, *refs):
    q_ref, o_ref, lse_ref, g_own_ref, g_other_ref = refs[:5]
    refs = refs[5:]
    sources, pieces = refs[:n_kv], refs[n_kv : n_kv + count]
    dq_ref = refs[n_kv + count]
    outs = refs[n_kv + count + 1 : n_kv + count + 1 + n_out]
    acc, delta, grads, buffer, sems = refs[n_kv + count + 1 + n_out :]
    step = pl.program_id(0)
    steps = buffer.shape[0]
    rows, width = q_ref.shape
    heads = width // HEAD_DIM
    half = rows // 2

    @pl.when(step == 0)
    def _():
        fetch_start(table_ref, sources, ring, buffer, sems, steps)
        acc[...] = jnp.zeros_like(acc)
        if ring:
            for out in outs:
                out[...] = jnp.zeros_like(out)
        weight = joined(pieces)
        grads[:half, :] = dot_nn(g_own_ref[...], weight).astype(BF16)
        grads[half:, :] = dot_nn(g_other_ref[...], weight).astype(BF16)
        turned = (grads[...].astype(F32) * o_ref[...].astype(F32)).T
        for head in range(heads):
            lanes = slice(head * HEAD_DIM, (head + 1) * HEAD_DIM)
            delta[head : head + 1, :] = jnp.sum(turned[lanes, :], axis=0, keepdims=True)

    fetch_wait(sources, buffer, sems, step)
    live = live_keys(buffer.shape[1], facts_ref[1], lens_ref[table_ref[step]])
    keys = buffer[step, :, :width]
    values = buffer[step, :, width:]
    keys_t = keys.T
    queries = q_ref[...]
    incoming = grads[...]
    grad_k = jnp.zeros(keys.shape, F32)
    grad_v = jnp.zeros(keys.shape, F32)
    for head in range(heads):
        inside = head_mask(queries.shape, head)
        mine = jnp.where(inside, queries, 0) * BF16(SCALING)
        mine_g = jnp.where(inside, incoming, 0)
        scores = dot_nt(keys, mine)
        full = jnp.where(live, jnp.exp(scores - lse_ref[head : head + 1, :]), 0.0)
        grad_probs = dot_nt(values, mine_g)
        steep = (full * (grad_probs - delta[head : head + 1, :])).astype(BF16)
        grad_v += dot_nn(full.astype(BF16), mine_g)
        grad_k += dot_nn(steep, mine)
        lanes = slice(head * HEAD_DIM, (head + 1) * HEAD_DIM)
        acc[lanes, :] += dot_nn(keys_t[lanes, :], steep)

    if not ring:
        outs[0][0, :, :width] = grad_k.astype(outs[0].dtype)
        outs[0][0, :, width:] = grad_v.astype(outs[0].dtype)
    else:
        for k in range(8):

            @pl.when(table_ref[step] == k)
            def _(k=k):
                if k == 4:
                    cut = outs[4].shape[0]
                    outs[4][:, :width] = grad_k[:cut].astype(BF16)
                    outs[4][:, width:] = grad_v[:cut].astype(BF16)
                    outs[5][:, :width] = grad_k[cut:].astype(BF16)
                    outs[5][:, width:] = grad_v[cut:].astype(BF16)
                else:
                    out = outs[k if k < 4 else k + 1]
                    out[:, :width] = grad_k.astype(BF16)
                    out[:, width:] = grad_v.astype(BF16)

    @pl.when(step == steps - 1)
    def _():
        dq_ref[...] = acc[...].T * F32(SCALING)


def attend_back(queries, grads, attended, lse, sources, ring, pieces, table, lens, facts, dtype):
    rows, width = queries.shape
    steps = table.shape[0]
    counts = [min(p.shape[0], limit) for p, limit in pieces]
    wide = grads[0].shape[1]
    if ring:
        out_specs = [whole(s.shape) for s in sources]
        out_shape = [shaped(*s.shape, dtype=BF16) for s in sources]
    else:
        out_specs = [pl.BlockSpec((1, rows, 2 * width), lambda j, *_: (j, 0, 0))]
        out_shape = [shaped(steps, rows, 2 * width, dtype=dtype)]
    return run(
        functools.partial(attend_back_kernel, ring, len(sources), len(pieces), len(out_specs)),
        (steps,),
        [
            whole((rows, width)),
            whole((rows, width)),
            whole((8, rows)),
            whole((rows // 2, wide)),
            whole((rows // 2, wide)),
        ]
        + [pl.BlockSpec(memory_space=pl.ANY)] * len(sources)
        + [column(r, lambda j: 3) for r in counts],
        [whole((rows, width))] + out_specs,
        [shaped(rows, width)] + out_shape,
        [
            pltpu.VMEM((width, rows), F32),
            pltpu.VMEM((8, rows), F32),
            pltpu.VMEM((rows, width), BF16),
            pltpu.VMEM((steps, rows, 2 * width), BF16),
            pltpu.SemaphoreType.DMA((steps,)),
        ],
        [table, lens, facts, queries, attended, lse, *grads, *sources] + [p for p, _ in pieces],
        4 + 4 * steps,
        prefetch=3,
    )


def per_device(
    block_input,
    cotangent,
    frame_lengths,
    frame_scenes,
    qkv_weight,
    out_weight,
    up_weight,
    down_weight,
    block_gains,
):
    quarter, wide = block_input.shape
    frames = lax.axis_size("frame")
    ring = on_ring()
    my_frame = lax.axis_index("frame")
    my_row = lax.axis_index("row")
    chip, core = my_row // 2, my_row % 2
    width = qkv_weight.shape[3]
    hidden = up_weight.shape[2]
    shard = wide // frames
    half = 2 * quarter
    facts = jnp.stack([chip, core, frame_lengths[my_frame]]).astype(jnp.int32)

    if ring:
        walk = jnp.array(RING, jnp.int32)
        at = jnp.argmax(walk == my_frame).astype(jnp.int32)
        order = lax.dynamic_slice_in_dim(jnp.concatenate([walk, walk]), at, frames)
        lane_order = RING
    else:
        order = jnp.arange(frames, dtype=jnp.int32)
        lane_order = tuple(range(wide // LANES))
    rel_lens = frame_lengths[order]
    other_scene = (frame_scenes[order] != frame_scenes[my_frame]).astype(jnp.int32)
    scene_table = jnp.argsort(other_scene, stable=True)[: frames // 2].astype(jnp.int32)
    frame_table = jnp.zeros((1,), jnp.int32)
    frame_lens = frame_lengths[my_frame].reshape(1)

    def enter(values, masked):
        return run(
            functools.partial(enter_kernel, masked, lane_order),
            (1,),
            [whole(values.shape)] * 2,
            whole((half, wide)),
            shaped(half, wide),
            [],
            [facts, values, row_take(values, 2)],
            1,
            prefetch=1,
        )

    big = whole((half, wide))

    qkv_shard = jnp.transpose(qkv_weight, (0, 2, 1, 3))
    if ring:
        pick = lambda s, b: pl.BlockSpec((1,) + s[1:], lambda *_: (b,) + (0,) * (len(s) - 1))

        def pack_at(block):
            return run(
                pack_at_kernel,
                (1,),
                [pick(qkv_shard.shape, block), pick(out_weight.shape, block)],
                whole((shard, 4 * width)),
                shaped(shard, 4 * width, dtype=BF16),
                [],
                [qkv_shard, out_weight],
                1,
            )

        def pack_ff(block, after=()):
            return run(
                pack_ff_kernel,
                (1,),
                [pick(up_weight.shape, block), pick(down_weight.shape, block)],
                whole((shard, 2 * hidden)),
                shaped(shard, 2 * hidden, dtype=BF16),
                [],
                [up_weight, down_weight],
                1,
                after=after,
            )

    else:

        def pack_at(block):
            return jnp.concatenate([*qkv_shard[block], out_weight[block].T], axis=1)

        def pack_ff(block, after=()):
            return jnp.concatenate([up_weight[block], down_weight[block].T], axis=1)

    def gather(packed):
        return [(lax.all_gather(packed, "frame", axis=0, tiled=True, axis_index_groups=frame_groups()), wide)]

    def scatter(grads):
        return lax.psum_scatter(
            grads, "frame", scatter_dimension=0, tiled=True, axis_index_groups=frame_groups()
        )

    at_zero, ff_zero, at_one = gather(pack_at(0)), gather(pack_ff(0)), gather(pack_at(1))
    weights = [(at_zero, ff_zero), None]
    if ring:
        rows = jnp.concatenate([block_gains[0], block_gains[1], jnp.zeros((4, shard), BF16)]).astype(F32)
        spread = lax.all_to_all(jnp.broadcast_to(rows[None], (frames, 16, shard)), "frame", 0, 0)
        gains_abs = jnp.swapaxes(spread, 0, 1).reshape(16, wide)
    else:
        gains_abs = lax.all_gather(block_gains, "frame", axis=2, tiled=True).astype(F32).reshape(12, wide)
        gains_abs = jnp.concatenate([gains_abs, jnp.zeros((4, wide), F32)])
    heads = lax.dynamic_slice_in_dim(gains_abs, my_row * width, width, 1)
    gains = jnp.concatenate([gains_abs[:, k * LANES : (k + 1) * LANES] for k in lane_order], axis=1)
    h = enter(block_input, False)
    normed = run(
        functools.partial(first_norm_kernel, 0),
        (1,),
        [big, whole(gains.shape)],
        big,
        shaped(half, wide, dtype=BF16),
        [],
        [h, gains],
        1,
    )

    gspec = whole(gains.shape)

    def reduce_rows(other, own):
        near = (own + row_take(other, 1).astype(F32)).astype(BF16)
        return near, row_take(near, 2)

    stored = []
    grad = enter(cotangent, True)
    scaled = run(
        functools.partial(scale_kernel, 9),
        (1,),
        [big, gspec],
        big,
        shaped(half, wide, dtype=BF16),
        [],
        [grad, gains],
        1,
    )
    grad_down = (scaled, row_take(scaled, 1))
    for block in range(2):
        base = 6 * block
        at, ff = weights[block] or (at_one, None)
        normed = (normed, row_take(normed, 1))
        early = [*grad_down, scene_table, rel_lens] if block == 0 else []
        queries, kv, mixed = project(normed, at, heads, base + 4, early)
        if block == 0:
            sources, walking, table, lens = [kv], False, frame_table, frame_lens
        else:
            table, lens, walking = scene_table, rel_lens, ring
            sources = ring_gather(kv, half) if ring else [lax.all_gather(kv, "frame", axis=0, tiled=True)]
            ff = gather(pack_ff(1, sources[4:6] if ring else ()))
            weights[1] = (at, ff)
        attended, lse, part_other, part_own = attend(
            queries, sources, walking, at, table, lens, facts, wide
        )
        branch = reduce_rows(part_other, part_own)
        middle, second = run(
            functools.partial(residual_kernel, base + 2, base + 1),
            (1,),
            [big, big, big, gspec],
            [big, big],
            [shaped(half, wide), shaped(half, wide, dtype=BF16)],
            [],
            [h, *branch, gains],
            2,
        )
        second = (second, row_take(second, 1))
        up_values, active, part_other, part_own = feed(second, ff, hidden)
        stored.append(
            (h, normed, queries, mixed, (sources, walking, table, lens), attended, lse, branch)
            + (middle, second, up_values, active)
        )
        if block == 0:
            down_zero = reduce_rows(part_other, part_own)
            h, normed = run(
                functools.partial(residual_kernel, base + 3, base + 6),
                (1,),
                [big, big, big, gspec],
                [big, big],
                [shaped(half, wide), shaped(half, wide, dtype=BF16)],
                [],
                [middle, *down_zero, gains],
                2,
            )

    last_other, last_own = row_take(part_other, 1), part_own
    at_shapes = [(2, 3, shard, width), (2, width, shard)]
    ff_shapes = [(2, shard, hidden), (2, hidden, shard)]
    at_out, ff_out = [], []
    gain_sums = [None, None]
    input_grad = None
    for block in (1, 0):
        base = 6 * block
        at, ff = weights[block]
        h, normed, queries, mixed, keys, attended, lse, branch, middle, second, up_values, active = stored[block]
        sources, walking, table, lens = keys
        grad_up, part_other, part_own = feed_back(grad_down, up_values, ff)
        incoming = reduce_rows(part_other, part_own)
        if block == 1:
            up_grads = one_weight_grads(second, grad_up, 5, [incoming[0]])
            ff_grads = one_weight_grads(grad_down, active, 5, [incoming[0]])
            up_sum = scatter(up_grads)
        else:
            ff_grads = weight_grads(second, grad_up, grad_down, active, 8, [incoming[0]])
            ff_grads = gate(ff_grads, [at_sum, incoming[1]])
            ff_sum = scatter(ff_grads)
            if ring:
                ff_out = finish(finish_ff_kernel, [ff_sum], ff_shapes, block, ff_out)
        grad_middle, scaled, sums_middle = run(
            functools.partial(middle_back_kernel, base),
            (1,),
            [big] * 6 + [gspec],
            [big, big, whole((2, wide))],
            [shaped(half, wide), shaped(half, wide, dtype=BF16), shaped(2, wide)],
            [],
            [grad, *incoming, middle, *branch, gains],
            2,
            after=[up_grads, ff_grads] if block == 1 else [ff_grads, *(at_out[:1] if ring else [])],
        )
        grad_branch = (scaled, row_take(scaled, 1))
        if block == 1:
            near = run(
                add_kernel, (1,), [big, big], big, shaped(half, wide, dtype=BF16), [], [last_own, last_other], 1,
                after=[incoming[1]],
            )
            output, sum_three = run(
                functools.partial(output_kernel, base + 3, lane_order),
                (1,),
                [big, big, big, gspec, big],
                [whole((quarter, wide)), whole((1, wide))],
                [shaped(quarter, wide, dtype=BF16), shaped(1, wide)],
                [pltpu.VMEM((half, wide), F32)],
                [facts, middle, near, row_take(near, 2), gains, grad],
                1,
                prefetch=1,
            )
        dq, *dkv_parts = attend_back(
            queries,
            grad_branch,
            attended,
            lse,
            sources,
            walking,
            at,
            table,
            lens,
            facts,
            F32 if block == 0 else BF16,
        )
        if block == 0:
            dkv = dkv_parts[0][0]
        elif ring:
            (own, right, left), sent_last = ring_scatter(dkv_parts)
            dkv = own.astype(F32) + right.astype(F32) + left.astype(F32)
        else:
            spread = jnp.zeros((frames,) + dkv_parts[0].shape[1:], BF16).at[table].set(dkv_parts[0])
            dkv = lax.psum_scatter(spread, "frame", scatter_dimension=0, tiled=False).astype(F32)
        if block == 1:
            down_sum = scatter(gate(ff_grads, [*(sent_last if ring else [dkv]), up_sum]))
            ff_sum = down_sum
            if ring:
                ff_out = finish(finish_two_kernel, [up_sum, down_sum], ff_shapes, 1, ff_out)
        grad_mixed, part_other, part_own, sums_heads, sum_zero = project_back(
            dq, dkv, mixed, at, heads, base + 4, normed, gains, [output] if block == 1 else ()
        )
        gain_sums[block] = (sum_zero, sums_middle, sum_three, sums_heads)
        incoming = reduce_rows(part_other, part_own)
        at_grads = weight_grads(normed, grad_mixed, grad_branch, attended, 4, [incoming[0]])
        at_grads = gate(at_grads, [ff_sum, incoming[1]])
        if block == 1:
            grad, scaled, sum_three = run(
                functools.partial(between_kernel, base),
                (1,),
                [big] * 4 + [gspec, big, big],
                [big, big, whole((1, wide))],
                [shaped(half, wide), shaped(half, wide, dtype=BF16), shaped(1, wide)],
                [],
                [grad_middle, *incoming, h, gains, *down_zero],
                3,
                after=[at_grads],
            )
            grad_down = (scaled, row_take(scaled, 1))
        else:
            input_grad = run(
                functools.partial(last_back_kernel, lane_order),
                (1,),
                [big] * 4 + [gspec],
                whole((quarter, wide)),
                shaped(quarter, wide, dtype=BF16),
                [pltpu.VMEM((half, wide), F32)],
                [facts, grad_middle, *incoming, h, gains],
                2,
                prefetch=1,
                after=[],
            )
        at_sum = scatter(at_grads)
        if ring:
            at_out = finish(finish_at_kernel, [at_sum], at_shapes, block, at_out)
        else:
            ff_parts = [up_sum, down_sum] if block == 1 else [ff_sum[:, :hidden], ff_sum[:, hidden:]]
            ff_out = [(ff_parts[0].astype(F32), ff_parts[1].astype(F32).T)] + ff_out
            at_last = at_sum.astype(F32)
            qkv_sum = jnp.stack([at_last[:, i * width : (i + 1) * width] for i in range(3)])
            at_out = [(qkv_sum, at_last[:, 3 * width :].T)] + at_out
    if not ring:
        ff_out = [jnp.stack(both) for both in zip(*ff_out, strict=True)]
        at_out = [jnp.stack(both) for both in zip(*at_out, strict=True)]

    if ring:
        operands = [*gain_sums[0], *gain_sums[1]]
        sent = run(
            functools.partial(gain_sums_kernel, lane_order),
            (1,),
            [whole(v.shape) for v in operands],
            whole((frames, 16, LANES)),
            shaped(frames, 16, LANES),
            [],
            [facts, *operands],
            1,
            prefetch=1,
            after=[input_grad],
        )
        total = jnp.sum(lax.all_to_all(sent, "frame", 0, 0), axis=0)
        total = total + row_take(total, 1)
        total = total + row_take(total, 2)
        gains_grad = total[:12].reshape(2, 6, LANES)
    else:
        rows = [jnp.concatenate([sums[0], sums[1] * F32(0.5), sums[2] * F32(0.5)]) for sums in gain_sums]
        rows = jnp.stack(rows)
        per_head = lax.dynamic_update_slice_in_dim(
            jnp.zeros((2, 2, wide), F32),
            jnp.stack([gain_sums[0][3], gain_sums[1][3]]),
            my_row * width,
            2,
        )
        total = lax.psum(jnp.concatenate([rows, per_head], axis=1), ("frame", "row"))
        gains_grad = lax.dynamic_slice_in_dim(total, my_frame * shard, shard, 2)
    return (
        output,
        input_grad,
        jnp.transpose(at_out[0], (0, 2, 1, 3)),
        at_out[1],
        ff_out[0],
        ff_out[1],
        gains_grad,
    )


def solution(mesh):
    return jax.shard_map(
        per_device,
        mesh=mesh,
        in_specs=(
            P(("frame", "row"), None),
            P(("frame", "row"), None),
            P(),
            P(),
            P(None, "frame", None, "row"),
            P(None, "row", "frame"),
            P(None, "frame", "row"),
            P(None, "row", "frame"),
            P(None, None, "frame"),
        ),
        out_specs=(
            P(("frame", "row"), None),
            P(("frame", "row"), None),
            P(None, "frame", None, "row"),
            P(None, "row", "frame"),
            P(None, "frame", "row"),
            P(None, "row", "frame"),
            P(None, None, "frame"),
        ),
        check_vma=False,
    )
```

```python
import functools

import jax
import jax.numpy as jnp
from jax import lax
from jax.experimental import pallas as pl
from jax.experimental.pallas import tpu as pltpu
from jax.sharding import PartitionSpec as P

HEAD_DIM = 64
EPSILON = 1e-06
F32 = jnp.float32
BF16 = jnp.bfloat16
LANES = 128
TILE = 256
ROOT_HALF = 0.7071067811865476
BELL = 0.3989422804014327
SCALING = HEAD_DIM**-0.5

RING = (0, 2, 4, 6, 7, 5, 3, 1)


def on_ring():
    return lax.axis_size("frame") == len(RING)


def frame_groups():
    return [list(RING)] if on_ring() else None


def frame_order(frames):
    return RING if on_ring() else tuple(range(frames))


def ring_take(value, step):
    count = len(RING)
    return lax.ppermute(value, "frame", [(RING[(i + step) % count], RING[i]) for i in range(count)])


def row_take(value, bit):
    return lax.ppermute(value, "row", [(i ^ bit, i) for i in range(4)])


def ring_gather(shard, cut):
    ahead, behind = [shard], [shard]
    for _ in range(3):
        ahead.append(ring_take(ahead[-1], 1))
        behind.append(ring_take(behind[-1], -1))
    far_low = ring_take(ahead[3][:cut], 1)
    far_high = ring_take(behind[3][cut:], -1)
    return ahead + [far_low, far_high] + behind[3:0:-1]


def add_pair(a, b):
    return (a.astype(F32) + b.astype(F32)).astype(BF16)


def ring_scatter(pieces):
    ahead = pieces[1:4]
    far_low, far_high = pieces[4:6]
    behind = pieces[8:5:-1]
    cut = far_low.shape[0]
    low = ring_take(far_low, -1)
    high = ring_take(far_high, 1)
    right = jnp.concatenate([add_pair(ahead[2][:cut], low), ahead[2][cut:]])
    left = jnp.concatenate([behind[2][:cut], add_pair(behind[2][cut:], high)])
    for place in (1, 0):
        right = add_pair(ahead[place], ring_take(right, -1))
        left = add_pair(behind[place], ring_take(left, 1))
    return (pieces[0], ring_take(right, -1), ring_take(left, 1)), [right, left]


def dot_nt(a, b):
    return lax.dot_general(a, b, (((1,), (1,)), ((), ())), preferred_element_type=F32)


def dot_nn(a, b):
    return lax.dot_general(a, b, (((1,), (0,)), ((), ())), preferred_element_type=F32)


def whole(shape):
    return pl.BlockSpec(shape, lambda *_: (0,) * len(shape))


def column(rows, place):
    return pl.BlockSpec((rows, TILE), lambda j, *_: (0, place(j)))


WEIGH = 3.0


def cost(us):
    return pl.CostEstimate(
        flops=int(us * WEIGH * 1.0e9), bytes_accessed=int(us * WEIGH * 2.0e6), transcendentals=0
    )


def run(kernel, grid, in_specs, out_specs, out_shape, scratch, operands, us, prefetch=0, aliases=None, after=()):
    count = len(operands)

    def body(*refs):
        kernel(*refs[:count], *refs[count + len(after) :])

    in_specs = list(in_specs) + [pl.BlockSpec(memory_space=pl.ANY)] * len(after)
    operands = [*operands, *after]
    return pl.pallas_call(
        body,
        grid_spec=pltpu.PrefetchScalarGridSpec(
            num_scalar_prefetch=prefetch,
            grid=grid,
            in_specs=in_specs,
            out_specs=out_specs,
            scratch_shapes=scratch,
        ),
        out_shape=out_shape,
        input_output_aliases=aliases or {},
        compiler_params=pltpu.CompilerParams(vmem_limit_bytes=56 * 1024 * 1024),
        cost_estimate=cost(us),
    )(*operands)


def shaped(*shape, dtype=F32):
    return jax.ShapeDtypeStruct(shape, dtype)


def norm_parts(values):
    center = values - jnp.mean(values, axis=-1, keepdims=True)
    scale = lax.rsqrt(jnp.mean(center * center, axis=-1, keepdims=True) + EPSILON)
    return center * scale, scale


def norm_back(unit, scale, gain, grad):
    inner = grad * gain
    return scale * (
        inner
        - jnp.mean(inner, axis=-1, keepdims=True)
        - unit * jnp.mean(inner * unit, axis=-1, keepdims=True)
    )


def head_means(values):
    width = values.shape[-1]
    rows = lax.broadcasted_iota(jnp.int32, (width, width), 0) // HEAD_DIM
    cols = lax.broadcasted_iota(jnp.int32, (width, width), 1) // HEAD_DIM
    spread = jnp.where(rows == cols, F32(1.0 / HEAD_DIM), F32(0)).astype(BF16)
    high = values.astype(BF16)
    low = (values - high.astype(F32)).astype(BF16)
    return dot_nn(high, spread) + dot_nn(low, spread)


def head_parts(values):
    center = values - head_means(values)
    scale = lax.rsqrt(head_means(center * center) + EPSILON)
    return center * scale, scale


def head_back(unit, scale, gain, grad):
    inner = grad * gain
    return scale * (inner - head_means(inner) - unit * head_means(inner * unit))


def joined(refs):
    if len(refs) == 1:
        return refs[0][...]
    return jnp.concatenate([ref[...] for ref in refs], axis=0)


def head_mask(shape, head):
    lanes = lax.broadcasted_iota(jnp.int32, shape, 1)
    return (lanes // HEAD_DIM) == head


def live_keys(count, core, length):
    place = lax.broadcasted_iota(jnp.int32, (count, 1), 0)
    quarter = count // 4
    half = place // (2 * quarter)
    chip = (place // quarter) % 2
    slot = (chip * 2 + (half ^ core)) * quarter + place % quarter
    return slot < length


def pack_at_kernel(qkv_ref, out_ref, at_ref):
    rows = out_ref.shape[2]
    width = qkv_ref.shape[3]
    for i in range(3):
        at_ref[:rows, i * width : (i + 1) * width] = qkv_ref[0, i]
    at_ref[:rows, 3 * width :] = out_ref[0].T


def pack_ff_kernel(up_ref, down_ref, ff_ref):
    ff = up_ref.shape[2]
    ff_ref[:, :ff] = up_ref[0]
    ff_ref[:, ff:] = down_ref[0].T


def gain_sums_kernel(order, facts_ref, *refs):
    out_ref = refs[-1]
    out_ref[...] = jnp.zeros_like(out_ref)
    row = facts_ref[0] * 2 + facts_ref[1]
    for block in range(2):
        zero, middle, three, heads = refs[4 * block : 4 * block + 4]
        base = 6 * block
        for k in range(out_ref.shape[0]):
            lanes = slice(k * LANES, (k + 1) * LANES)
            place = order[k]
            out_ref[place, base : base + 1, :] = zero[:, lanes]
            out_ref[place, base + 1 : base + 3, :] = middle[:, lanes] * 0.5
            out_ref[place, base + 3 : base + 4, :] = three[:, lanes] * 0.5
        for k in range(2):
            lanes = slice(k * LANES, (k + 1) * LANES)
            out_ref[row * 2 + k, base + 4 : base + 6, :] = heads[:, lanes]


def enter_kernel(masked, order, facts_ref, own_ref, far_ref, out_ref):
    rows = own_ref.shape[0]
    chip, core, length = facts_ref[0], facts_ref[1], facts_ref[2]
    for k in range(len(order)):
        lanes = slice(order[k] * LANES, (order[k] + 1) * LANES)
        for source, place in ((own_ref, chip), (far_ref, 1 - chip)):
            values = source[:, lanes].astype(F32)
            if masked:
                slots = (place * 2 + core) * rows + lax.broadcasted_iota(jnp.int32, (rows, 1), 0)
                values = jnp.where(slots < length, values, 0.0)
            start = pl.multiple_of(place * rows, rows)
            out_ref[pl.ds(start, rows), k * LANES : (k + 1) * LANES] = values


def leave(values_ref, order, facts_ref, out_ref):
    rows = out_ref.shape[0]
    start = pl.multiple_of(facts_ref[0] * rows, rows)
    for k in range(len(order)):
        lanes = slice(order[k] * LANES, (order[k] + 1) * LANES)
        values = values_ref[pl.ds(start, rows), k * LANES : (k + 1) * LANES]
        out_ref[:, lanes] = values.astype(out_ref.dtype)


def first_norm_kernel(row, h_ref, gains_ref, normed_ref):
    unit, _ = norm_parts(h_ref[...])
    normed_ref[...] = (unit * gains_ref[row : row + 1, :]).astype(BF16)


def total_of(own_ref, far_ref):
    return own_ref[...].astype(F32) + far_ref[...].astype(F32)


def residual_kernel(scale_row, norm_row, h_ref, own_ref, far_ref, gains_ref, next_ref, normed_ref):
    value = h_ref[...] + gains_ref[scale_row : scale_row + 1, :] * total_of(own_ref, far_ref)
    next_ref[...] = value
    unit, _ = norm_parts(value)
    normed_ref[...] = (unit * gains_ref[norm_row : norm_row + 1, :]).astype(BF16)


def add_kernel(own_ref, other_ref, sum_ref):
    sum_ref[...] = (own_ref[...] + other_ref[...].astype(F32)).astype(BF16)


def output_kernel(scale_row, order, facts_ref, h_ref, own_ref, far_ref, gains_ref, grad_ref, out_ref, sums_ref, held):
    total = total_of(own_ref, far_ref)
    held[...] = h_ref[...] + gains_ref[scale_row : scale_row + 1, :] * total
    sums_ref[...] = jnp.sum(grad_ref[...] * total, axis=0, keepdims=True)
    leave(held, order, facts_ref, out_ref)


def scale_kernel(row, grad_ref, gains_ref, scaled_ref):
    scaled_ref[...] = (grad_ref[...] * gains_ref[row : row + 1, :]).astype(BF16)


def middle_back_kernel(
    base, grad_ref, own_ref, far_ref, middle_ref, b_own_ref, b_far_ref, gains_ref, next_ref, scaled_ref, sums_ref
):
    grad_in = total_of(own_ref, far_ref)
    unit, scale = norm_parts(middle_ref[...])
    sums_ref[0:1, :] = jnp.sum(grad_in * unit, axis=0, keepdims=True)
    grad = grad_ref[...] + norm_back(unit, scale, gains_ref[base + 1 : base + 2, :], grad_in)
    next_ref[...] = grad
    sums_ref[1:2, :] = jnp.sum(grad * total_of(b_own_ref, b_far_ref), axis=0, keepdims=True)
    scaled_ref[...] = (grad * gains_ref[base + 2 : base + 3, :]).astype(BF16)


def first_back(base, grad_ref, own_ref, far_ref, h_ref, gains_ref):
    unit, scale = norm_parts(h_ref[...])
    return grad_ref[...] + norm_back(unit, scale, gains_ref[base : base + 1, :], total_of(own_ref, far_ref))


def between_kernel(
    base, grad_ref, own_ref, far_ref, h_ref, gains_ref, d_own_ref, d_far_ref, next_ref, scaled_ref, sums_ref
):
    grad = first_back(base, grad_ref, own_ref, far_ref, h_ref, gains_ref)
    next_ref[...] = grad
    scaled_ref[...] = (grad * gains_ref[base - 3 : base - 2, :]).astype(BF16)
    sums_ref[...] = jnp.sum(grad * total_of(d_own_ref, d_far_ref), axis=0, keepdims=True)


def last_back_kernel(order, facts_ref, grad_ref, own_ref, far_ref, h_ref, gains_ref, out_ref, held):
    held[...] = first_back(0, grad_ref, own_ref, far_ref, h_ref, gains_ref)
    leave(held, order, facts_ref, out_ref)


def project_kernel(row_q, count, own_ref, other_ref, *refs):
    pieces = refs[:count]
    heads_ref, q_ref, kv_ref, mixed_ref = refs[count:]
    step = pl.program_id(0)
    weight = joined(pieces)
    half = own_ref.shape[0]
    mixed = jnp.concatenate([dot_nn(own_ref[...], weight), dot_nn(other_ref[...], weight)], axis=0)

    @pl.when(step < 2)
    def _():
        mixed_ref[...] = mixed
        unit, _ = head_parts(mixed)
        gain = jnp.where(step == 0, heads_ref[row_q : row_q + 1, :], heads_ref[row_q + 1 : row_q + 2, :])
        scaled = (unit * gain).astype(BF16)

        @pl.when(step == 0)
        def _():
            q_ref[...] = scaled

        @pl.when(step == 1)
        def _():
            kv_ref[...] = scaled

    @pl.when(step == 2)
    def _():
        kv_ref[...] = mixed.astype(BF16)


def project(normed, pieces, heads, row_q, after):
    own, other = normed
    half, wide = own.shape
    width = heads.shape[1]
    rows = [min(p.shape[0], limit) for p, limit in pieces]
    return run(
        functools.partial(project_kernel, row_q, len(pieces)),
        (3,),
        [whole(own.shape), whole(other.shape)]
        + [column(r, lambda j: j) for r in rows]
        + [whole(heads.shape)],
        [
            whole((2 * half, width)),
            column(2 * half, lambda j: jnp.maximum(j - 1, 0)),
            column(2 * half, lambda j: jnp.minimum(j, 1)),
        ],
        [
            shaped(2 * half, width, dtype=BF16),
            shaped(2 * half, 2 * width, dtype=BF16),
            shaped(2 * half, 2 * width),
        ],
        [],
        [own, other] + [p for p, _ in pieces] + [heads],
        5,
        after=after,
    )


def project_back_kernel(row_q, count, dq_ref, dkv_ref, mixed_ref, heads_ref, n_own_ref, n_other_ref, gains_ref, *refs):
    pieces = refs[:count]
    grad_ref, other_ref, own_ref, sums_ref, zero_ref, acc = refs[count:]
    step = pl.program_id(0)

    @pl.when(step == 0)
    def _():
        acc[...] = jnp.zeros_like(acc)

    def normed(incoming, row, place):
        unit, scale = head_parts(mixed_ref[...])
        sums_ref[place : place + 1, :] = jnp.sum(incoming * unit, axis=0, keepdims=True)
        grad_ref[...] = head_back(unit, scale, heads_ref[row : row + 1, :], incoming).astype(BF16)

    @pl.when(step == 0)
    def _():
        normed(dq_ref[...], row_q, 0)

    @pl.when(step == 1)
    def _():
        normed(dkv_ref[...].astype(F32), row_q + 1, 1)

    @pl.when(step == 2)
    def _():
        grad_ref[...] = dkv_ref[...].astype(BF16)

    acc[...] += dot_nt(grad_ref[...], joined(pieces))

    @pl.when(step == 2)
    def _():
        half = own_ref.shape[0]
        own_ref[...] = acc[:half, :]
        other_ref[...] = acc[half:, :].astype(BF16)
        products = acc[:half, :] * n_own_ref[...].astype(F32) + acc[half:, :] * n_other_ref[...].astype(F32)
        row_g = row_q - 4
        zero_ref[...] = jnp.sum(products, axis=0, keepdims=True) / gains_ref[row_g : row_g + 1, :]


def project_back(dq, dkv, mixed, pieces, heads, row_q, normed, gains, after):
    full, width = dq.shape
    wide = gains.shape[1]
    rows = [min(p.shape[0], limit) for p, limit in pieces]
    return run(
        functools.partial(project_back_kernel, row_q, len(pieces)),
        (3,),
        [
            whole(dq.shape),
            column(full, lambda j: jnp.maximum(j - 1, 0)),
            column(full, lambda j: jnp.minimum(j, 1)),
            whole(heads.shape),
            whole((full // 2, wide)),
            whole((full // 2, wide)),
            whole(gains.shape),
        ]
        + [column(r, lambda j: j) for r in rows],
        [
            column(full, lambda j: j),
            whole((full // 2, wide)),
            whole((full // 2, wide)),
            whole((2, width)),
            whole((1, wide)),
        ],
        [
            shaped(full, 3 * width, dtype=BF16),
            shaped(full // 2, wide, dtype=BF16),
            shaped(full // 2, wide),
            shaped(2, width),
            shaped(1, wide),
        ],
        [pltpu.VMEM((full, wide), F32)],
        [dq, dkv, mixed, heads, *normed, gains] + [p for p, _ in pieces],
        6,
        after=after,
    )


def feed_kernel(count, own_ref, other_ref, *refs):
    ups, downs = refs[:count], refs[count : 2 * count]
    values_ref, active_ref, part_other_ref, part_own_ref, acc = refs[2 * count :]
    step = pl.program_id(0)

    @pl.when(step == 0)
    def _():
        acc[...] = jnp.zeros_like(acc)

    weight = joined(ups)
    half = own_ref.shape[0]
    for source, start in ((own_ref, 0), (other_ref, half)):
        values = dot_nn(source[...], weight)
        values_ref[start : start + half, :] = values
        active_ref[start : start + half, :] = (
            0.5 * values * (1.0 + lax.erf(values * F32(ROOT_HALF)))
        ).astype(BF16)
    acc[...] += dot_nt(active_ref[...], joined(downs))

    @pl.when(step == pl.num_programs(0) - 1)
    def _():
        part_own_ref[...] = acc[:half, :]
        part_other_ref[...] = acc[half:, :].astype(BF16)


def feed(second, pieces, hidden):
    own, other = second
    half, wide = own.shape
    steps = hidden // TILE
    rows = [min(p.shape[0], limit) for p, limit in pieces]
    arrays = [p for p, _ in pieces]
    return run(
        functools.partial(feed_kernel, len(pieces)),
        (steps,),
        [whole(own.shape), whole(other.shape)]
        + [column(r, lambda j: j) for r in rows]
        + [column(r, lambda j: j + steps) for r in rows],
        [
            column(2 * half, lambda j: j),
            column(2 * half, lambda j: j),
            whole((half, wide)),
            whole((half, wide)),
        ],
        [
            shaped(2 * half, hidden),
            shaped(2 * half, hidden, dtype=BF16),
            shaped(half, wide, dtype=BF16),
            shaped(half, wide),
        ],
        [pltpu.VMEM((2 * half, wide), F32)],
        [own, other] + arrays + arrays,
        7,
    )


def feed_back_kernel(count, own_ref, other_ref, values_ref, *refs):
    ups, downs = refs[:count], refs[count : 2 * count]
    grad_ref, part_other_ref, part_own_ref, acc = refs[2 * count :]
    step = pl.program_id(0)

    @pl.when(step == 0)
    def _():
        acc[...] = jnp.zeros_like(acc)

    weight = joined(downs)
    half = own_ref.shape[0]
    for source, start in ((own_ref, 0), (other_ref, half)):
        incoming = dot_nn(source[...], weight)
        values = values_ref[start : start + half, :]
        slope = 0.5 * (1.0 + lax.erf(values * F32(ROOT_HALF))) + values * (
            jnp.exp(-0.5 * values * values) * F32(BELL)
        )
        grad_ref[start : start + half, :] = (incoming * slope).astype(BF16)
    acc[...] += dot_nt(grad_ref[...], joined(ups))

    @pl.when(step == pl.num_programs(0) - 1)
    def _():
        part_own_ref[...] = acc[:half, :]
        part_other_ref[...] = acc[half:, :].astype(BF16)


def feed_back(grads, values, pieces):
    own, other = grads
    half, wide = own.shape
    hidden = values.shape[1]
    steps = hidden // TILE
    rows = [min(p.shape[0], limit) for p, limit in pieces]
    arrays = [p for p, _ in pieces]
    return run(
        functools.partial(feed_back_kernel, len(pieces)),
        (steps,),
        [whole(own.shape), whole(other.shape), column(2 * half, lambda j: j)]
        + [column(r, lambda j: j) for r in rows]
        + [column(r, lambda j: j + steps) for r in rows],
        [column(2 * half, lambda j: j), whole((half, wide)), whole((half, wide))],
        [
            shaped(2 * half, hidden, dtype=BF16),
            shaped(half, wide, dtype=BF16),
            shaped(half, wide),
        ],
        [pltpu.VMEM((2 * half, wide), F32)],
        [own, other, values] + arrays + arrays,
        3,
    )


def weight_kernel(split, a_own, a_other, b_own, b_other, first_ref, second_ref, out_ref, turned):
    step = pl.program_id(0)
    half = a_own.shape[0]

    def turn(own, other):
        turned[:, :half] = own[...].T
        turned[:, half:] = other[...].T

    @pl.when(step == 0)
    def _():
        turn(a_own, a_other)

    @pl.when(step == split)
    def _():
        turn(b_own, b_other)

    @pl.when(step < split)
    def _():
        out_ref[...] = dot_nn(turned[...], first_ref[...]).astype(BF16)

    @pl.when(step >= split)
    def _():
        out_ref[...] = dot_nn(turned[...], second_ref[...]).astype(BF16)


def gate_kernel(*refs):
    pass


def gate(value, after):
    anywhere = pl.BlockSpec(memory_space=pl.ANY)
    return run(
        gate_kernel, (1,), [anywhere], anywhere, jax.ShapeDtypeStruct(value.shape, value.dtype), [], [value], 0.1,
        aliases={0: 0}, after=after,
    )


def one_weight_kernel(own, other, right_ref, out_ref, turned):
    half = own.shape[0]

    @pl.when(pl.program_id(0) == 0)
    def _():
        turned[:, :half] = own[...].T
        turned[:, half:] = other[...].T

    out_ref[...] = dot_nn(turned[...], right_ref[...]).astype(BF16)


def one_weight_grads(a, right, us, after):
    half, wide = a[0].shape
    return run(
        one_weight_kernel,
        (right.shape[1] // TILE,),
        [whole((half, wide))] * 2 + [column(2 * half, lambda j: j)],
        column(wide, lambda j: j),
        shaped(wide, right.shape[1], dtype=BF16),
        [pltpu.VMEM((wide, 2 * half), BF16)],
        [*a, right],
        us,
        after=after,
    )


def weight_grads(a, first, b, second, us, after):
    half, wide = a[0].shape
    split = first.shape[1] // TILE
    steps = split + second.shape[1] // TILE
    return run(
        functools.partial(weight_kernel, split),
        (steps,),
        [whole((half, wide))] * 4
        + [
            column(2 * half, lambda j: jnp.minimum(j, split - 1)),
            column(2 * half, lambda j: jnp.maximum(j - split, 0)),
        ],
        column(wide, lambda j: j),
        shaped(wide, steps * TILE, dtype=BF16),
        [pltpu.VMEM((wide, 2 * half), BF16)],
        [*a, *b, first, second],
        us,
        after=after,
    )


def finish_ff_kernel(part_ref, *refs):
    up_ref, down_ref = refs[-2:]
    hidden = up_ref.shape[2]
    up_ref[0] = part_ref[:, :hidden].astype(F32)
    down_ref[0] = part_ref[:, hidden:].astype(F32).T


def finish_two_kernel(up_part_ref, down_part_ref, up_ref, down_ref):
    up_ref[0] = up_part_ref[...].astype(F32)
    down_ref[0] = down_part_ref[...].astype(F32).T


def finish_at_kernel(part_ref, *refs):
    qkv_ref, out_ref = refs[-2:]
    width = qkv_ref.shape[3]
    for i in range(3):
        qkv_ref[0, i] = part_ref[:, i * width : (i + 1) * width].astype(F32)
    out_ref[0] = part_ref[:, 3 * width :].astype(F32).T


def finish(kernel, parts, shapes, block, earlier):
    specs = [
        pl.BlockSpec((1,) + s[1:], functools.partial(lambda b, r, *_: (b,) + (0,) * (r - 1), block, len(s)))
        for s in shapes
    ]
    return run(
        kernel,
        (1,),
        [whole(part.shape) for part in parts] + [pl.BlockSpec(memory_space=pl.ANY)] * len(earlier),
        specs,
        [shaped(*s) for s in shapes],
        [],
        [*parts, *earlier],
        2,
        aliases={len(parts) + i: i for i in range(len(earlier))},
    )


def fetch_start(table_ref, sources, ring, buffer, sems, count):
    flen = buffer.shape[1]
    for j in range(count):
        if not ring:
            start = pl.multiple_of(table_ref[j] * flen, flen)
            pltpu.make_async_copy(sources[0].at[pl.ds(start, flen)], buffer.at[j], sems.at[j]).start()
            continue
        for k in range(8):

            @pl.when(table_ref[j] == k)
            def _(j=j, k=k):
                if k == 4:
                    cut = sources[4].shape[0]
                    pltpu.make_async_copy(sources[4], buffer.at[j, pl.ds(0, cut)], sems.at[j]).start()
                    pltpu.make_async_copy(
                        sources[5], buffer.at[j, pl.ds(cut, flen - cut)], sems.at[j]
                    ).start()
                else:
                    source = sources[k if k < 4 else k + 1]
                    pltpu.make_async_copy(source, buffer.at[j], sems.at[j]).start()


def fetch_wait(sources, buffer, sems, j):
    pltpu.make_async_copy(buffer.at[j], buffer.at[j], sems.at[j]).wait()


def attend_kernel(ring, n_kv, count, table_ref, lens_ref, facts_ref, q_ref, *refs):
    sources, pieces = refs[:n_kv], refs[n_kv : n_kv + count]
    out_ref, lse_ref, part_other_ref, part_own_ref = refs[n_kv + count : n_kv + count + 4]
    acc, sums, buffer, sems = refs[n_kv + count + 4 :]
    step = pl.program_id(0)
    steps = buffer.shape[0]
    rows, width = q_ref.shape
    heads = width // HEAD_DIM

    @pl.when(step == 0)
    def _():
        fetch_start(table_ref, sources, ring, buffer, sems, steps)
        acc[...] = jnp.zeros_like(acc)
        sums[...] = jnp.ones_like(sums)
        sums[:heads, :] = jnp.zeros((heads, rows), F32)

    fetch_wait(sources, buffer, sems, step)
    live = live_keys(buffer.shape[1], facts_ref[1], lens_ref[table_ref[step]])
    keys = buffer[step, :, :width]
    values_t = buffer[step, :, width:].T
    queries = q_ref[...]
    for head in range(heads):
        mine = jnp.where(head_mask(queries.shape, head), queries, 0) * BF16(SCALING)
        scores = dot_nt(keys, mine)
        powers = jnp.where(live, jnp.exp(scores), 0.0)
        sums[head : head + 1, :] += jnp.sum(powers, axis=0, keepdims=True)
        lanes = slice(head * HEAD_DIM, (head + 1) * HEAD_DIM)
        acc[lanes, :] += dot_nn(values_t[lanes, :], powers.astype(BF16))

    @pl.when(step == steps - 1)
    def _():
        lse_ref[...] = jnp.log(sums[...])
        for head in range(heads):
            lanes = slice(head * HEAD_DIM, (head + 1) * HEAD_DIM)
            acc[lanes, :] = acc[lanes, :] / sums[head : head + 1, :]
        out_ref[...] = acc[...].T.astype(BF16)
        weight = joined(pieces)
        half = rows // 2
        part_other_ref[...] = dot_nt(out_ref[half:, :], weight).astype(BF16)
        part_own_ref[...] = dot_nt(out_ref[:half, :], weight)


def attend(queries, sources, ring, pieces, table, lens, facts, wide):
    rows, width = queries.shape
    steps = table.shape[0]
    counts = [min(p.shape[0], limit) for p, limit in pieces]
    return run(
        functools.partial(attend_kernel, ring, len(sources), len(pieces)),
        (steps,),
        [whole(queries.shape)]
        + [pl.BlockSpec(memory_space=pl.ANY)] * len(sources)
        + [column(r, lambda j: 3) for r in counts],
        [whole((rows, width)), whole((8, rows)), whole((rows // 2, wide)), whole((rows // 2, wide))],
        [
            shaped(rows, width, dtype=BF16),
            shaped(8, rows),
            shaped(rows // 2, wide, dtype=BF16),
            shaped(rows // 2, wide),
        ],
        [
            pltpu.VMEM((width, rows), F32),
            pltpu.VMEM((8, rows), F32),
            pltpu.VMEM((steps, rows, 2 * width), BF16),
            pltpu.SemaphoreType.DMA((steps,)),
        ],
        [table, lens, facts, queries, *sources] + [p for p, _ in pieces],
        3 + 2 * steps,
        prefetch=3,
    )


def attend_back_kernel(ring, n_kv, count, n_out, table_ref, lens_ref, facts_ref, *refs):
    q_ref, o_ref, lse_ref, g_own_ref, g_other_ref = refs[:5]
    refs = refs[5:]
    sources, pieces = refs[:n_kv], refs[n_kv : n_kv + count]
    dq_ref = refs[n_kv + count]
    outs = refs[n_kv + count + 1 : n_kv + count + 1 + n_out]
    acc, lines, stack_q, stack_g, buffer, sems = refs[n_kv + count + 1 + n_out :]
    step = pl.program_id(0)
    steps = buffer.shape[0]
    rows, width = q_ref.shape
    heads = width // HEAD_DIM

    @pl.when(step == 0)
    def _():
        fetch_start(table_ref, sources, ring, buffer, sems, steps)
        acc[...] = jnp.zeros_like(acc)
        if ring:
            for out in outs:
                out[...] = jnp.zeros_like(out)
        weight = joined(pieces)
        grads = jnp.concatenate([dot_nn(ref[...], weight).astype(BF16) for ref in (g_own_ref, g_other_ref)], axis=0)
        turned = (grads.astype(F32) * o_ref[...].astype(F32)).T
        for head in range(heads):
            lanes = slice(head * HEAD_DIM, (head + 1) * HEAD_DIM)
            columns = slice(head * rows, (head + 1) * rows)
            lines[0:1, columns] = lse_ref[head : head + 1, :]
            lines[1:2, columns] = jnp.sum(turned[lanes, :], axis=0, keepdims=True)
            inside = head_mask((rows, width), head)
            stack_q[columns, :] = jnp.where(inside, q_ref[...], 0) * BF16(SCALING)
            stack_g[columns, :] = jnp.where(inside, grads, 0)

    fetch_wait(sources, buffer, sems, step)
    live = live_keys(buffer.shape[1], facts_ref[1], lens_ref[table_ref[step]])
    keys = buffer[step, :, :width]
    keys_t = keys.T
    scores = dot_nt(keys, stack_q[...])
    full = jnp.where(live, jnp.exp(scores - lines[0:1, :]), 0.0)
    grad_probs = dot_nt(buffer[step, :, width:], stack_g[...])
    steep = (full * (grad_probs - lines[1:2, :])).astype(BF16)
    grad_v = dot_nn(full.astype(BF16), stack_g[...])
    grad_k = dot_nn(steep, stack_q[...])
    for head in range(heads):
        lanes = slice(head * HEAD_DIM, (head + 1) * HEAD_DIM)
        acc[lanes, :] += dot_nn(keys_t[lanes, :], steep[:, head * rows : (head + 1) * rows])

    if not ring:
        outs[0][0, :, :width] = grad_k.astype(outs[0].dtype)
        outs[0][0, :, width:] = grad_v.astype(outs[0].dtype)
    else:
        for k in range(8):

            @pl.when(table_ref[step] == k)
            def _(k=k):
                if k == 4:
                    cut = outs[4].shape[0]
                    outs[4][:, :width] = grad_k[:cut].astype(BF16)
                    outs[4][:, width:] = grad_v[:cut].astype(BF16)
                    outs[5][:, :width] = grad_k[cut:].astype(BF16)
                    outs[5][:, width:] = grad_v[cut:].astype(BF16)
                else:
                    out = outs[k if k < 4 else k + 1]
                    out[:, :width] = grad_k.astype(BF16)
                    out[:, width:] = grad_v.astype(BF16)

    @pl.when(step == steps - 1)
    def _():
        dq_ref[...] = acc[...].T * F32(SCALING)


def attend_back(queries, grads, attended, lse, sources, ring, pieces, table, lens, facts, dtype):
    rows, width = queries.shape
    steps = table.shape[0]
    counts = [min(p.shape[0], limit) for p, limit in pieces]
    wide = grads[0].shape[1]
    if ring:
        out_specs = [whole(s.shape) for s in sources]
        out_shape = [shaped(*s.shape, dtype=BF16) for s in sources]
    else:
        out_specs = [pl.BlockSpec((1, rows, 2 * width), lambda j, *_: (j, 0, 0))]
        out_shape = [shaped(steps, rows, 2 * width, dtype=dtype)]
    return run(
        functools.partial(attend_back_kernel, ring, len(sources), len(pieces), len(out_specs)),
        (steps,),
        [
            whole((rows, width)),
            whole((rows, width)),
            whole((8, rows)),
            whole((rows // 2, wide)),
            whole((rows // 2, wide)),
        ]
        + [pl.BlockSpec(memory_space=pl.ANY)] * len(sources)
        + [column(r, lambda j: 3) for r in counts],
        [whole((rows, width))] + out_specs,
        [shaped(rows, width)] + out_shape,
        [
            pltpu.VMEM((width, rows), F32),
            pltpu.VMEM((8, rows * width // HEAD_DIM), F32),
            pltpu.VMEM((rows * width // HEAD_DIM, width), BF16),
            pltpu.VMEM((rows * width // HEAD_DIM, width), BF16),
            pltpu.VMEM((steps, rows, 2 * width), BF16),
            pltpu.SemaphoreType.DMA((steps,)),
        ],
        [table, lens, facts, queries, attended, lse, *grads, *sources] + [p for p, _ in pieces],
        1 + 0.5 * steps,
        prefetch=3,
    )


def per_device(
    block_input,
    cotangent,
    frame_lengths,
    frame_scenes,
    qkv_weight,
    out_weight,
    up_weight,
    down_weight,
    block_gains,
):
    quarter, wide = block_input.shape
    frames = lax.axis_size("frame")
    ring = on_ring()
    my_frame = lax.axis_index("frame")
    my_row = lax.axis_index("row")
    chip, core = my_row // 2, my_row % 2
    width = qkv_weight.shape[3]
    hidden = up_weight.shape[2]
    shard = wide // frames
    half = 2 * quarter
    facts = jnp.stack([chip, core, frame_lengths[my_frame]]).astype(jnp.int32)

    if ring:
        walk = jnp.array(RING, jnp.int32)
        at = jnp.argmax(walk == my_frame).astype(jnp.int32)
        order = lax.dynamic_slice_in_dim(jnp.concatenate([walk, walk]), at, frames)
        lane_order = RING
    else:
        order = jnp.arange(frames, dtype=jnp.int32)
        lane_order = tuple(range(wide // LANES))
    rel_lens = frame_lengths[order]
    other_scene = (frame_scenes[order] != frame_scenes[my_frame]).astype(jnp.int32)
    scene_table = jnp.argsort(other_scene, stable=True)[: frames // 2].astype(jnp.int32)
    frame_table = jnp.zeros((1,), jnp.int32)
    frame_lens = frame_lengths[my_frame].reshape(1)

    def enter(values, masked):
        return run(
            functools.partial(enter_kernel, masked, lane_order),
            (1,),
            [whole(values.shape)] * 2,
            whole((half, wide)),
            shaped(half, wide),
            [],
            [facts, values, row_take(values, 2)],
            1,
            prefetch=1,
        )

    big = whole((half, wide))

    qkv_shard = jnp.transpose(qkv_weight, (0, 2, 1, 3))
    if ring:
        pick = lambda s, b: pl.BlockSpec((1,) + s[1:], lambda *_: (b,) + (0,) * (len(s) - 1))

        def pack_at(block):
            return run(
                pack_at_kernel,
                (1,),
                [pick(qkv_shard.shape, block), pick(out_weight.shape, block)],
                whole((shard, 4 * width)),
                shaped(shard, 4 * width, dtype=BF16),
                [],
                [qkv_shard, out_weight],
                1,
            )

        def pack_ff(block, after=()):
            return run(
                pack_ff_kernel,
                (1,),
                [pick(up_weight.shape, block), pick(down_weight.shape, block)],
                whole((shard, 2 * hidden)),
                shaped(shard, 2 * hidden, dtype=BF16),
                [],
                [up_weight, down_weight],
                1,
                after=after,
            )

    else:

        def pack_at(block):
            return jnp.concatenate([*qkv_shard[block], out_weight[block].T], axis=1)

        def pack_ff(block, after=()):
            return jnp.concatenate([up_weight[block], down_weight[block].T], axis=1)

    def gather(packed):
        return [(lax.all_gather(packed, "frame", axis=0, tiled=True, axis_index_groups=frame_groups()), wide)]

    def scatter(grads):
        return lax.psum_scatter(
            grads, "frame", scatter_dimension=0, tiled=True, axis_index_groups=frame_groups()
        )

    at_zero, ff_zero, at_one = gather(pack_at(0)), gather(pack_ff(0)), gather(pack_at(1))
    weights = [(at_zero, ff_zero), None]
    if ring:
        rows = jnp.concatenate([block_gains[0], block_gains[1], jnp.zeros((4, shard), BF16)]).astype(F32)
        spread = lax.all_to_all(jnp.broadcast_to(rows[None], (frames, 16, shard)), "frame", 0, 0)
        gains_abs = jnp.swapaxes(spread, 0, 1).reshape(16, wide)
    else:
        gains_abs = lax.all_gather(block_gains, "frame", axis=2, tiled=True).astype(F32).reshape(12, wide)
        gains_abs = jnp.concatenate([gains_abs, jnp.zeros((4, wide), F32)])
    heads = lax.dynamic_slice_in_dim(gains_abs, my_row * width, width, 1)
    gains = jnp.concatenate([gains_abs[:, k * LANES : (k + 1) * LANES] for k in lane_order], axis=1)
    h = enter(block_input, False)
    normed = run(
        functools.partial(first_norm_kernel, 0),
        (1,),
        [big, whole(gains.shape)],
        big,
        shaped(half, wide, dtype=BF16),
        [],
        [h, gains],
        1,
    )

    gspec = whole(gains.shape)

    def reduce_rows(other, own):
        near = (own + row_take(other, 1).astype(F32)).astype(BF16)
        return near, row_take(near, 2)

    stored = []
    grad = enter(cotangent, True)
    scaled = run(
        functools.partial(scale_kernel, 9),
        (1,),
        [big, gspec],
        big,
        shaped(half, wide, dtype=BF16),
        [],
        [grad, gains],
        1,
    )
    grad_down = (scaled, row_take(scaled, 1))
    for block in range(2):
        base = 6 * block
        at, ff = weights[block] or (at_one, None)
        normed = (normed, row_take(normed, 1))
        early = [*grad_down, scene_table, rel_lens] if block == 0 else []
        queries, kv, mixed = project(normed, at, heads, base + 4, early)
        if block == 0:
            sources, walking, table, lens = [kv], False, frame_table, frame_lens
        else:
            table, lens, walking = scene_table, rel_lens, ring
            sources = ring_gather(kv, half) if ring else [lax.all_gather(kv, "frame", axis=0, tiled=True)]
            ff = gather(pack_ff(1, [sources[3], sources[6]] if ring else ()))
            weights[1] = (at, ff)
        attended, lse, part_other, part_own = attend(
            queries, sources, walking, at, table, lens, facts, wide
        )
        branch = reduce_rows(part_other, part_own)
        middle, second = run(
            functools.partial(residual_kernel, base + 2, base + 1),
            (1,),
            [big, big, big, gspec],
            [big, big],
            [shaped(half, wide), shaped(half, wide, dtype=BF16)],
            [],
            [h, *branch, gains],
            2,
        )
        second = (second, row_take(second, 1))
        up_values, active, part_other, part_own = feed(second, ff, hidden)
        stored.append(
            (h, normed, queries, mixed, (sources, walking, table, lens), attended, lse, branch)
            + (middle, second, up_values, active)
        )
        if block == 0:
            down_zero = reduce_rows(part_other, part_own)
            h, normed = run(
                functools.partial(residual_kernel, base + 3, base + 6),
                (1,),
                [big, big, big, gspec],
                [big, big],
                [shaped(half, wide), shaped(half, wide, dtype=BF16)],
                [],
                [middle, *down_zero, gains],
                2,
            )

    last_other, last_own = row_take(part_other, 1), part_own
    at_shapes = [(2, 3, shard, width), (2, width, shard)]
    ff_shapes = [(2, shard, hidden), (2, hidden, shard)]
    at_out, ff_out = [], []
    gain_sums = [None, None]
    input_grad = None
    for block in (1, 0):
        base = 6 * block
        at, ff = weights[block]
        h, normed, queries, mixed, keys, attended, lse, branch, middle, second, up_values, active = stored[block]
        sources, walking, table, lens = keys
        grad_up, part_other, part_own = feed_back(grad_down, up_values, ff)
        incoming = reduce_rows(part_other, part_own)
        if block == 1:
            up_grads = one_weight_grads(second, grad_up, 5, [incoming[0]])
            ff_grads = one_weight_grads(grad_down, active, 5, [incoming[0]])
            up_sum = scatter(up_grads)
        else:
            ff_grads = weight_grads(second, grad_up, grad_down, active, 3, [incoming[0]])
            ff_grads = gate(ff_grads, [at_sum, incoming[1]])
            ff_sum = scatter(ff_grads)
            if ring:
                ff_out = finish(finish_ff_kernel, [ff_sum], ff_shapes, block, ff_out)
        grad_middle, scaled, sums_middle = run(
            functools.partial(middle_back_kernel, base),
            (1,),
            [big] * 6 + [gspec],
            [big, big, whole((2, wide))],
            [shaped(half, wide), shaped(half, wide, dtype=BF16), shaped(2, wide)],
            [],
            [grad, *incoming, middle, *branch, gains],
            2,
            after=[up_grads, ff_grads] if block == 1 else [ff_grads, *(at_out[:1] if ring else [])],
        )
        grad_branch = (scaled, row_take(scaled, 1))
        if block == 1:
            near = run(
                add_kernel, (1,), [big, big], big, shaped(half, wide, dtype=BF16), [], [last_own, last_other], 1,
                after=[incoming[1]],
            )
            output, sum_three = run(
                functools.partial(output_kernel, base + 3, lane_order),
                (1,),
                [big, big, big, gspec, big],
                [whole((quarter, wide)), whole((1, wide))],
                [shaped(quarter, wide, dtype=BF16), shaped(1, wide)],
                [pltpu.VMEM((half, wide), F32)],
                [facts, middle, near, row_take(near, 2), gains, grad],
                1,
                prefetch=1,
            )
        dq, *dkv_parts = attend_back(
            queries,
            grad_branch,
            attended,
            lse,
            sources,
            walking,
            at,
            table,
            lens,
            facts,
            F32 if block == 0 else BF16,
        )
        if block == 0:
            dkv = dkv_parts[0][0]
        elif ring:
            (own, right, left), sent_last = ring_scatter(dkv_parts)
            dkv = own.astype(F32) + right.astype(F32) + left.astype(F32)
        else:
            spread = jnp.zeros((frames,) + dkv_parts[0].shape[1:], BF16).at[table].set(dkv_parts[0])
            dkv = lax.psum_scatter(spread, "frame", scatter_dimension=0, tiled=False).astype(F32)
        if block == 1:
            down_sum = scatter(gate(ff_grads, [*(sent_last if ring else [dkv]), up_sum]))
            ff_sum = down_sum
            if ring:
                ff_out = finish(finish_two_kernel, [up_sum, down_sum], ff_shapes, 1, ff_out)
        grad_mixed, part_other, part_own, sums_heads, sum_zero = project_back(
            dq, dkv, mixed, at, heads, base + 4, normed, gains, [output] if block == 1 else ()
        )
        gain_sums[block] = (sum_zero, sums_middle, sum_three, sums_heads)
        incoming = reduce_rows(part_other, part_own)
        at_grads = weight_grads(normed, grad_mixed, grad_branch, attended, 4, [incoming[0]])
        at_grads = gate(at_grads, [ff_sum, incoming[1]])
        if block == 1:
            grad, scaled, sum_three = run(
                functools.partial(between_kernel, base),
                (1,),
                [big] * 4 + [gspec, big, big],
                [big, big, whole((1, wide))],
                [shaped(half, wide), shaped(half, wide, dtype=BF16), shaped(1, wide)],
                [],
                [grad_middle, *incoming, h, gains, *down_zero],
                3,
                after=[at_grads],
            )
            grad_down = (scaled, row_take(scaled, 1))
        else:
            input_grad = run(
                functools.partial(last_back_kernel, lane_order),
                (1,),
                [big] * 4 + [gspec],
                whole((quarter, wide)),
                shaped(quarter, wide, dtype=BF16),
                [pltpu.VMEM((half, wide), F32)],
                [facts, grad_middle, *incoming, h, gains],
                2,
                prefetch=1,
                after=[],
            )
        at_sum = scatter(at_grads)
        if ring:
            at_out = finish(finish_at_kernel, [at_sum], at_shapes, block, at_out)
        else:
            ff_parts = [up_sum, down_sum] if block == 1 else [ff_sum[:, :hidden], ff_sum[:, hidden:]]
            ff_out = [(ff_parts[0].astype(F32), ff_parts[1].astype(F32).T)] + ff_out
            at_last = at_sum.astype(F32)
            qkv_sum = jnp.stack([at_last[:, i * width : (i + 1) * width] for i in range(3)])
            at_out = [(qkv_sum, at_last[:, 3 * width :].T)] + at_out
    if not ring:
        ff_out = [jnp.stack(both) for both in zip(*ff_out, strict=True)]
        at_out = [jnp.stack(both) for both in zip(*at_out, strict=True)]

    if ring:
        operands = [*gain_sums[0], *gain_sums[1]]
        sent = run(
            functools.partial(gain_sums_kernel, lane_order),
            (1,),
            [whole(v.shape) for v in operands],
            whole((frames, 16, LANES)),
            shaped(frames, 16, LANES),
            [],
            [facts, *operands],
            1,
            prefetch=1,
            after=[input_grad],
        )
        total = jnp.sum(lax.all_to_all(sent, "frame", 0, 0), axis=0)
        total = total + row_take(total, 1)
        total = total + row_take(total, 2)
        gains_grad = total[:12].reshape(2, 6, LANES)
    else:
        rows = [jnp.concatenate([sums[0], sums[1] * F32(0.5), sums[2] * F32(0.5)]) for sums in gain_sums]
        rows = jnp.stack(rows)
        per_head = lax.dynamic_update_slice_in_dim(
            jnp.zeros((2, 2, wide), F32),
            jnp.stack([gain_sums[0][3], gain_sums[1][3]]),
            my_row * width,
            2,
        )
        total = lax.psum(jnp.concatenate([rows, per_head], axis=1), ("frame", "row"))
        gains_grad = lax.dynamic_slice_in_dim(total, my_frame * shard, shard, 2)
    return (
        output,
        input_grad,
        jnp.transpose(at_out[0], (0, 2, 1, 3)),
        at_out[1],
        ff_out[0],
        ff_out[1],
        gains_grad,
    )


def solution(mesh):
    return jax.shard_map(
        per_device,
        mesh=mesh,
        in_specs=(
            P(("frame", "row"), None),
            P(("frame", "row"), None),
            P(),
            P(),
            P(None, "frame", None, "row"),
            P(None, "row", "frame"),
            P(None, "frame", "row"),
            P(None, "row", "frame"),
            P(None, None, "frame"),
        ),
        out_specs=(
            P(("frame", "row"), None),
            P(("frame", "row"), None),
            P(None, "frame", None, "row"),
            P(None, "row", "frame"),
            P(None, "frame", "row"),
            P(None, "row", "frame"),
            P(None, None, "frame"),
        ),
        check_vma=False,
    )
```

```python
import functools

import jax
import jax.numpy as jnp
from jax import lax
from jax.experimental import pallas as pl
from jax.experimental.pallas import tpu as pltpu
from jax.sharding import PartitionSpec as P

HEAD_DIM = 64
EPSILON = 1e-06
F32 = jnp.float32
BF16 = jnp.bfloat16
LANES = 128
TILE = 256
ROOT_HALF = 0.7071067811865476
BELL = 0.3989422804014327
SCALING = HEAD_DIM**-0.5

RING = (0, 2, 4, 6, 7, 5, 3, 1)


def on_ring():
    return lax.axis_size("frame") == len(RING)


def frame_groups():
    return [list(RING)] if on_ring() else None


def frame_order(frames):
    return RING if on_ring() else tuple(range(frames))


def ring_take(value, step):
    count = len(RING)
    return lax.ppermute(value, "frame", [(RING[(i + step) % count], RING[i]) for i in range(count)])


def row_take(value, bit):
    return lax.ppermute(value, "row", [(i ^ bit, i) for i in range(4)])


def ring_gather(shard, cut):
    ahead, behind = [shard], [shard]
    for _ in range(3):
        ahead.append(ring_take(ahead[-1], 1))
        behind.append(ring_take(behind[-1], -1))
    far_low = ring_take(ahead[3][:cut], 1)
    far_high = ring_take(behind[3][cut:], -1)
    return ahead + [far_low, far_high] + behind[3:0:-1]


def add_pair(a, b):
    return (a.astype(F32) + b.astype(F32)).astype(BF16)


def ring_scatter(pieces):
    ahead = pieces[1:4]
    far_low, far_high = pieces[4:6]
    behind = pieces[8:5:-1]
    cut = far_low.shape[0]
    low = ring_take(far_low, -1)
    high = ring_take(far_high, 1)
    right = jnp.concatenate([add_pair(ahead[2][:cut], low), ahead[2][cut:]])
    left = jnp.concatenate([behind[2][:cut], add_pair(behind[2][cut:], high)])
    for place in (1, 0):
        right = add_pair(ahead[place], ring_take(right, -1))
        left = add_pair(behind[place], ring_take(left, 1))
    return (pieces[0], ring_take(right, -1), ring_take(left, 1)), [right, left]


def dot_nt(a, b):
    return lax.dot_general(a, b, (((1,), (1,)), ((), ())), preferred_element_type=F32)


def dot_nn(a, b):
    return lax.dot_general(a, b, (((1,), (0,)), ((), ())), preferred_element_type=F32)


def whole(shape):
    return pl.BlockSpec(shape, lambda *_: (0,) * len(shape))


def column(rows, place):
    return pl.BlockSpec((rows, TILE), lambda j, *_: (0, place(j)))


WEIGH = 3.0


def cost(us):
    return pl.CostEstimate(
        flops=int(us * WEIGH * 1.0e9), bytes_accessed=int(us * WEIGH * 2.0e6), transcendentals=0
    )


def run(kernel, grid, in_specs, out_specs, out_shape, scratch, operands, us, prefetch=0, aliases=None, after=()):
    count = len(operands)

    def body(*refs):
        kernel(*refs[:count], *refs[count + len(after) :])

    in_specs = list(in_specs) + [pl.BlockSpec(memory_space=pl.ANY)] * len(after)
    operands = [*operands, *after]
    return pl.pallas_call(
        body,
        grid_spec=pltpu.PrefetchScalarGridSpec(
            num_scalar_prefetch=prefetch,
            grid=grid,
            in_specs=in_specs,
            out_specs=out_specs,
            scratch_shapes=scratch,
        ),
        out_shape=out_shape,
        input_output_aliases=aliases or {},
        compiler_params=pltpu.CompilerParams(vmem_limit_bytes=56 * 1024 * 1024),
        cost_estimate=cost(us),
    )(*operands)


def shaped(*shape, dtype=F32):
    return jax.ShapeDtypeStruct(shape, dtype)


def norm_parts(values):
    center = values - jnp.mean(values, axis=-1, keepdims=True)
    scale = lax.rsqrt(jnp.mean(center * center, axis=-1, keepdims=True) + EPSILON)
    return center * scale, scale


def norm_back(unit, scale, gain, grad):
    inner = grad * gain
    return scale * (
        inner
        - jnp.mean(inner, axis=-1, keepdims=True)
        - unit * jnp.mean(inner * unit, axis=-1, keepdims=True)
    )


def head_means(values):
    width = values.shape[-1]
    rows = lax.broadcasted_iota(jnp.int32, (width, width), 0) // HEAD_DIM
    cols = lax.broadcasted_iota(jnp.int32, (width, width), 1) // HEAD_DIM
    spread = jnp.where(rows == cols, F32(1.0 / HEAD_DIM), F32(0)).astype(BF16)
    high = values.astype(BF16)
    low = (values - high.astype(F32)).astype(BF16)
    return dot_nn(high, spread) + dot_nn(low, spread)


def head_parts(values):
    center = values - head_means(values)
    scale = lax.rsqrt(head_means(center * center) + EPSILON)
    return center * scale, scale


def head_back(unit, scale, gain, grad):
    inner = grad * gain
    return scale * (inner - head_means(inner) - unit * head_means(inner * unit))


def joined(refs):
    if len(refs) == 1:
        return refs[0][...]
    return jnp.concatenate([ref[...] for ref in refs], axis=0)


def head_mask(shape, head):
    lanes = lax.broadcasted_iota(jnp.int32, shape, 1)
    return (lanes // HEAD_DIM) == head


def live_keys(count, core, length):
    place = lax.broadcasted_iota(jnp.int32, (count, 1), 0)
    quarter = count // 4
    half = place // (2 * quarter)
    chip = (place // quarter) % 2
    slot = (chip * 2 + (half ^ core)) * quarter + place % quarter
    return slot < length


def pack_at_kernel(qkv_ref, out_ref, at_ref):
    rows = out_ref.shape[2]
    width = qkv_ref.shape[3]
    for i in range(3):
        at_ref[:rows, i * width : (i + 1) * width] = qkv_ref[0, i]
    at_ref[:rows, 3 * width :] = out_ref[0].T


def pack_ff_kernel(up_ref, down_ref, ff_ref):
    ff = up_ref.shape[2]
    ff_ref[:, :ff] = up_ref[0]
    ff_ref[:, ff:] = down_ref[0].T


def gain_sums_kernel(order, facts_ref, *refs):
    out_ref = refs[-1]
    out_ref[...] = jnp.zeros_like(out_ref)
    row = facts_ref[0] * 2 + facts_ref[1]
    for block in range(2):
        zero, middle, three, heads = refs[4 * block : 4 * block + 4]
        base = 6 * block
        for k in range(out_ref.shape[0]):
            lanes = slice(k * LANES, (k + 1) * LANES)
            place = order[k]
            out_ref[place, base : base + 1, :] = zero[:, lanes]
            out_ref[place, base + 1 : base + 3, :] = middle[:, lanes] * 0.5
            out_ref[place, base + 3 : base + 4, :] = three[:, lanes] * 0.5
        for k in range(2):
            lanes = slice(k * LANES, (k + 1) * LANES)
            out_ref[row * 2 + k, base + 4 : base + 6, :] = heads[:, lanes]


def enter_kernel(masked, order, facts_ref, own_ref, far_ref, out_ref):
    rows = own_ref.shape[0]
    chip, core, length = facts_ref[0], facts_ref[1], facts_ref[2]
    for k in range(len(order)):
        lanes = slice(order[k] * LANES, (order[k] + 1) * LANES)
        for source, place in ((own_ref, chip), (far_ref, 1 - chip)):
            values = source[:, lanes].astype(F32)
            if masked:
                slots = (place * 2 + core) * rows + lax.broadcasted_iota(jnp.int32, (rows, 1), 0)
                values = jnp.where(slots < length, values, 0.0)
            start = pl.multiple_of(place * rows, rows)
            out_ref[pl.ds(start, rows), k * LANES : (k + 1) * LANES] = values


def leave(values_ref, order, facts_ref, out_ref):
    rows = out_ref.shape[0]
    start = pl.multiple_of(facts_ref[0] * rows, rows)
    for k in range(len(order)):
        lanes = slice(order[k] * LANES, (order[k] + 1) * LANES)
        values = values_ref[pl.ds(start, rows), k * LANES : (k + 1) * LANES]
        out_ref[:, lanes] = values.astype(out_ref.dtype)


def first_norm_kernel(row, h_ref, gains_ref, normed_ref):
    unit, _ = norm_parts(h_ref[...])
    normed_ref[...] = (unit * gains_ref[row : row + 1, :]).astype(BF16)


def total_of(own_ref, far_ref):
    return own_ref[...].astype(F32) + far_ref[...].astype(F32)


def residual_kernel(scale_row, norm_row, h_ref, own_ref, far_ref, gains_ref, next_ref, normed_ref):
    value = h_ref[...] + gains_ref[scale_row : scale_row + 1, :] * total_of(own_ref, far_ref)
    next_ref[...] = value
    unit, _ = norm_parts(value)
    normed_ref[...] = (unit * gains_ref[norm_row : norm_row + 1, :]).astype(BF16)


def add_kernel(own_ref, other_ref, sum_ref):
    sum_ref[...] = (own_ref[...] + other_ref[...].astype(F32)).astype(BF16)


def output_kernel(scale_row, order, facts_ref, h_ref, own_ref, far_ref, gains_ref, grad_ref, out_ref, sums_ref, held):
    total = total_of(own_ref, far_ref)
    held[...] = h_ref[...] + gains_ref[scale_row : scale_row + 1, :] * total
    sums_ref[...] = jnp.sum(grad_ref[...] * total, axis=0, keepdims=True)
    leave(held, order, facts_ref, out_ref)


def scale_kernel(row, grad_ref, gains_ref, scaled_ref):
    scaled_ref[...] = (grad_ref[...] * gains_ref[row : row + 1, :]).astype(BF16)


def middle_back_kernel(
    base, grad_ref, own_ref, far_ref, middle_ref, b_own_ref, b_far_ref, gains_ref, next_ref, scaled_ref, sums_ref
):
    grad_in = total_of(own_ref, far_ref)
    unit, scale = norm_parts(middle_ref[...])
    sums_ref[0:1, :] = jnp.sum(grad_in * unit, axis=0, keepdims=True)
    grad = grad_ref[...] + norm_back(unit, scale, gains_ref[base + 1 : base + 2, :], grad_in)
    next_ref[...] = grad
    sums_ref[1:2, :] = jnp.sum(grad * total_of(b_own_ref, b_far_ref), axis=0, keepdims=True)
    scaled_ref[...] = (grad * gains_ref[base + 2 : base + 3, :]).astype(BF16)


def first_back(base, grad_ref, own_ref, far_ref, h_ref, gains_ref):
    unit, scale = norm_parts(h_ref[...])
    return grad_ref[...] + norm_back(unit, scale, gains_ref[base : base + 1, :], total_of(own_ref, far_ref))


def between_kernel(
    base, grad_ref, own_ref, far_ref, h_ref, gains_ref, d_own_ref, d_far_ref, next_ref, scaled_ref, sums_ref
):
    grad = first_back(base, grad_ref, own_ref, far_ref, h_ref, gains_ref)
    next_ref[...] = grad
    scaled_ref[...] = (grad * gains_ref[base - 3 : base - 2, :]).astype(BF16)
    sums_ref[...] = jnp.sum(grad * total_of(d_own_ref, d_far_ref), axis=0, keepdims=True)


def last_back_kernel(order, facts_ref, grad_ref, own_ref, far_ref, h_ref, gains_ref, out_ref, held):
    held[...] = first_back(0, grad_ref, own_ref, far_ref, h_ref, gains_ref)
    leave(held, order, facts_ref, out_ref)


def project_kernel(row_q, count, own_ref, other_ref, *refs):
    pieces = refs[:count]
    heads_ref, q_ref, kv_ref, mixed_ref = refs[count:]
    step = pl.program_id(0)
    weight = joined(pieces)
    half = own_ref.shape[0]
    mixed = jnp.concatenate([dot_nn(own_ref[...], weight), dot_nn(other_ref[...], weight)], axis=0)

    @pl.when(step < 2)
    def _():
        mixed_ref[...] = mixed
        unit, _ = head_parts(mixed)
        gain = jnp.where(step == 0, heads_ref[row_q : row_q + 1, :], heads_ref[row_q + 1 : row_q + 2, :])
        scaled = (unit * gain).astype(BF16)

        @pl.when(step == 0)
        def _():
            q_ref[...] = scaled

        @pl.when(step == 1)
        def _():
            kv_ref[...] = scaled

    @pl.when(step == 2)
    def _():
        kv_ref[...] = mixed.astype(BF16)


def project(normed, pieces, heads, row_q, after):
    own, other = normed
    half, wide = own.shape
    width = heads.shape[1]
    rows = [min(p.shape[0], limit) for p, limit in pieces]
    return run(
        functools.partial(project_kernel, row_q, len(pieces)),
        (3,),
        [whole(own.shape), whole(other.shape)]
        + [column(r, lambda j: j) for r in rows]
        + [whole(heads.shape)],
        [
            whole((2 * half, width)),
            column(2 * half, lambda j: jnp.maximum(j - 1, 0)),
            column(2 * half, lambda j: jnp.minimum(j, 1)),
        ],
        [
            shaped(2 * half, width, dtype=BF16),
            shaped(2 * half, 2 * width, dtype=BF16),
            shaped(2 * half, 2 * width),
        ],
        [],
        [own, other] + [p for p, _ in pieces] + [heads],
        5,
        after=after,
    )


def project_back_kernel(row_q, count, dq_ref, dkv_ref, mixed_ref, heads_ref, n_own_ref, n_other_ref, gains_ref, *refs):
    pieces = refs[:count]
    grad_ref, other_ref, own_ref, sums_ref, zero_ref, acc = refs[count:]
    step = pl.program_id(0)

    @pl.when(step == 0)
    def _():
        acc[...] = jnp.zeros_like(acc)

    def normed(incoming, row, place):
        unit, scale = head_parts(mixed_ref[...])
        sums_ref[place : place + 1, :] = jnp.sum(incoming * unit, axis=0, keepdims=True)
        grad_ref[...] = head_back(unit, scale, heads_ref[row : row + 1, :], incoming).astype(BF16)

    @pl.when(step == 0)
    def _():
        normed(dq_ref[...], row_q, 0)

    @pl.when(step == 1)
    def _():
        normed(dkv_ref[...].astype(F32), row_q + 1, 1)

    @pl.when(step == 2)
    def _():
        grad_ref[...] = dkv_ref[...].astype(BF16)

    acc[...] += dot_nt(grad_ref[...], joined(pieces))

    @pl.when(step == 2)
    def _():
        half = own_ref.shape[0]
        own_ref[...] = acc[:half, :]
        other_ref[...] = acc[half:, :].astype(BF16)
        products = acc[:half, :] * n_own_ref[...].astype(F32) + acc[half:, :] * n_other_ref[...].astype(F32)
        row_g = row_q - 4
        zero_ref[...] = jnp.sum(products, axis=0, keepdims=True) / gains_ref[row_g : row_g + 1, :]


def project_back(dq, dkv, mixed, pieces, heads, row_q, normed, gains, after):
    full, width = dq.shape
    wide = gains.shape[1]
    rows = [min(p.shape[0], limit) for p, limit in pieces]
    return run(
        functools.partial(project_back_kernel, row_q, len(pieces)),
        (3,),
        [
            whole(dq.shape),
            column(full, lambda j: jnp.maximum(j - 1, 0)),
            column(full, lambda j: jnp.minimum(j, 1)),
            whole(heads.shape),
            whole((full // 2, wide)),
            whole((full // 2, wide)),
            whole(gains.shape),
        ]
        + [column(r, lambda j: j) for r in rows],
        [
            column(full, lambda j: j),
            whole((full // 2, wide)),
            whole((full // 2, wide)),
            whole((2, width)),
            whole((1, wide)),
        ],
        [
            shaped(full, 3 * width, dtype=BF16),
            shaped(full // 2, wide, dtype=BF16),
            shaped(full // 2, wide),
            shaped(2, width),
            shaped(1, wide),
        ],
        [pltpu.VMEM((full, wide), F32)],
        [dq, dkv, mixed, heads, *normed, gains] + [p for p, _ in pieces],
        6,
        after=after,
    )


def feed_kernel(count, own_ref, other_ref, *refs):
    ups, downs = refs[:count], refs[count : 2 * count]
    values_ref, active_ref, part_other_ref, part_own_ref, acc = refs[2 * count :]
    step = pl.program_id(0)

    @pl.when(step == 0)
    def _():
        acc[...] = jnp.zeros_like(acc)

    weight = joined(ups)
    half = own_ref.shape[0]
    for source, start in ((own_ref, 0), (other_ref, half)):
        values = dot_nn(source[...], weight)
        values_ref[start : start + half, :] = values
        active_ref[start : start + half, :] = (
            0.5 * values * (1.0 + lax.erf(values * F32(ROOT_HALF)))
        ).astype(BF16)
    acc[...] += dot_nt(active_ref[...], joined(downs))

    @pl.when(step == pl.num_programs(0) - 1)
    def _():
        part_own_ref[...] = acc[:half, :]
        part_other_ref[...] = acc[half:, :].astype(BF16)


def feed(second, pieces, hidden):
    own, other = second
    half, wide = own.shape
    steps = hidden // TILE
    rows = [min(p.shape[0], limit) for p, limit in pieces]
    arrays = [p for p, _ in pieces]
    return run(
        functools.partial(feed_kernel, len(pieces)),
        (steps,),
        [whole(own.shape), whole(other.shape)]
        + [column(r, lambda j: j) for r in rows]
        + [column(r, lambda j: j + steps) for r in rows],
        [
            column(2 * half, lambda j: j),
            column(2 * half, lambda j: j),
            whole((half, wide)),
            whole((half, wide)),
        ],
        [
            shaped(2 * half, hidden),
            shaped(2 * half, hidden, dtype=BF16),
            shaped(half, wide, dtype=BF16),
            shaped(half, wide),
        ],
        [pltpu.VMEM((2 * half, wide), F32)],
        [own, other] + arrays + arrays,
        7,
    )


def feed_back_kernel(count, own_ref, other_ref, values_ref, *refs):
    ups, downs = refs[:count], refs[count : 2 * count]
    grad_ref, part_other_ref, part_own_ref, acc = refs[2 * count :]
    step = pl.program_id(0)

    @pl.when(step == 0)
    def _():
        acc[...] = jnp.zeros_like(acc)

    weight = joined(downs)
    half = own_ref.shape[0]
    for source, start in ((own_ref, 0), (other_ref, half)):
        incoming = dot_nn(source[...], weight)
        values = values_ref[start : start + half, :]
        slope = 0.5 * (1.0 + lax.erf(values * F32(ROOT_HALF))) + values * (
            jnp.exp(-0.5 * values * values) * F32(BELL)
        )
        grad_ref[start : start + half, :] = (incoming * slope).astype(BF16)
    acc[...] += dot_nt(grad_ref[...], joined(ups))

    @pl.when(step == pl.num_programs(0) - 1)
    def _():
        part_own_ref[...] = acc[:half, :]
        part_other_ref[...] = acc[half:, :].astype(BF16)


def feed_back(grads, values, pieces):
    own, other = grads
    half, wide = own.shape
    hidden = values.shape[1]
    steps = hidden // TILE
    rows = [min(p.shape[0], limit) for p, limit in pieces]
    arrays = [p for p, _ in pieces]
    return run(
        functools.partial(feed_back_kernel, len(pieces)),
        (steps,),
        [whole(own.shape), whole(other.shape), column(2 * half, lambda j: j)]
        + [column(r, lambda j: j) for r in rows]
        + [column(r, lambda j: j + steps) for r in rows],
        [column(2 * half, lambda j: j), whole((half, wide)), whole((half, wide))],
        [
            shaped(2 * half, hidden, dtype=BF16),
            shaped(half, wide, dtype=BF16),
            shaped(half, wide),
        ],
        [pltpu.VMEM((2 * half, wide), F32)],
        [own, other, values] + arrays + arrays,
        3,
    )


def feed_both_kernel(own_ref, other_ref, g_own_ref, g_other_ref, up_ref, down_ref, *refs):
    active_ref, grad_ref, part_other_ref, part_own_ref, back_other_ref, back_own_ref, acc, back = refs
    step = pl.program_id(0)

    @pl.when(step == 0)
    def _():
        acc[...] = jnp.zeros_like(acc)
        back[...] = jnp.zeros_like(back)

    up, down = up_ref[...], down_ref[...]
    half = own_ref.shape[0]
    for source, g_source, start in ((own_ref, g_own_ref, 0), (other_ref, g_other_ref, half)):
        values = dot_nn(source[...], up)
        gate_part = 0.5 * (1.0 + lax.erf(values * F32(ROOT_HALF)))
        active_ref[start : start + half, :] = (values * gate_part).astype(BF16)
        slope = gate_part + values * (jnp.exp(-0.5 * values * values) * F32(BELL))
        grad_ref[start : start + half, :] = (dot_nn(g_source[...], down) * slope).astype(BF16)
    acc[...] += dot_nt(active_ref[...], down)
    back[...] += dot_nt(grad_ref[...], up)

    @pl.when(step == pl.num_programs(0) - 1)
    def _():
        part_own_ref[...] = acc[:half, :]
        part_other_ref[...] = acc[half:, :].astype(BF16)
        back_own_ref[...] = back[:half, :]
        back_other_ref[...] = back[half:, :].astype(BF16)


def feed_both(second, grads, weight, hidden):
    half, wide = second[0].shape
    steps = hidden // TILE
    return run(
        feed_both_kernel,
        (steps,),
        [whole((half, wide))] * 4 + [column(wide, lambda j: j), column(wide, lambda j: j + steps)],
        [column(2 * half, lambda j: j)] * 2 + [whole((half, wide))] * 4,
        [shaped(2 * half, hidden, dtype=BF16)] * 2 + [shaped(half, wide, dtype=BF16), shaped(half, wide)] * 2,
        [pltpu.VMEM((2 * half, wide), F32)] * 2,
        [*second, *grads, weight, weight],
        10,
    )


def weight_kernel(split, a_own, a_other, b_own, b_other, first_ref, second_ref, out_ref, turned):
    step = pl.program_id(0)
    half = a_own.shape[0]

    def turn(own, other):
        turned[:, :half] = own[...].T
        turned[:, half:] = other[...].T

    @pl.when(step == 0)
    def _():
        turn(a_own, a_other)

    @pl.when(step == split)
    def _():
        turn(b_own, b_other)

    @pl.when(step < split)
    def _():
        out_ref[...] = dot_nn(turned[...], first_ref[...]).astype(BF16)

    @pl.when(step >= split)
    def _():
        out_ref[...] = dot_nn(turned[...], second_ref[...]).astype(BF16)


def gate_kernel(*refs):
    pass


def gate(value, after):
    anywhere = pl.BlockSpec(memory_space=pl.ANY)
    return run(
        gate_kernel, (1,), [anywhere], anywhere, jax.ShapeDtypeStruct(value.shape, value.dtype), [], [value], 0.1,
        aliases={0: 0}, after=after,
    )


def one_weight_kernel(own, other, right_ref, out_ref, turned):
    half = own.shape[0]

    @pl.when(pl.program_id(0) == 0)
    def _():
        turned[:, :half] = own[...].T
        turned[:, half:] = other[...].T

    out_ref[...] = dot_nn(turned[...], right_ref[...]).astype(BF16)


def one_weight_grads(a, right, us, after):
    half, wide = a[0].shape
    return run(
        one_weight_kernel,
        (right.shape[1] // TILE,),
        [whole((half, wide))] * 2 + [column(2 * half, lambda j: j)],
        column(wide, lambda j: j),
        shaped(wide, right.shape[1], dtype=BF16),
        [pltpu.VMEM((wide, 2 * half), BF16)],
        [*a, right],
        us,
        after=after,
    )


def weight_grads(a, first, b, second, us, after):
    half, wide = a[0].shape
    split = first.shape[1] // TILE
    steps = split + second.shape[1] // TILE
    return run(
        functools.partial(weight_kernel, split),
        (steps,),
        [whole((half, wide))] * 4
        + [
            column(2 * half, lambda j: jnp.minimum(j, split - 1)),
            column(2 * half, lambda j: jnp.maximum(j - split, 0)),
        ],
        column(wide, lambda j: j),
        shaped(wide, steps * TILE, dtype=BF16),
        [pltpu.VMEM((wide, 2 * half), BF16)],
        [*a, *b, first, second],
        us,
        after=after,
    )


def finish_ff_kernel(part_ref, *refs):
    up_ref, down_ref = refs[-2:]
    hidden = up_ref.shape[2]
    up_ref[0] = part_ref[:, :hidden].astype(F32)
    down_ref[0] = part_ref[:, hidden:].astype(F32).T


def finish_two_kernel(up_part_ref, down_part_ref, up_ref, down_ref):
    up_ref[0] = up_part_ref[...].astype(F32)
    down_ref[0] = down_part_ref[...].astype(F32).T


def finish_at_kernel(part_ref, *refs):
    qkv_ref, out_ref = refs[-2:]
    width = qkv_ref.shape[3]
    for i in range(3):
        qkv_ref[0, i] = part_ref[:, i * width : (i + 1) * width].astype(F32)
    out_ref[0] = part_ref[:, 3 * width :].astype(F32).T


def finish(kernel, parts, shapes, block, earlier):
    specs = [
        pl.BlockSpec((1,) + s[1:], functools.partial(lambda b, r, *_: (b,) + (0,) * (r - 1), block, len(s)))
        for s in shapes
    ]
    return run(
        kernel,
        (1,),
        [whole(part.shape) for part in parts] + [pl.BlockSpec(memory_space=pl.ANY)] * len(earlier),
        specs,
        [shaped(*s) for s in shapes],
        [],
        [*parts, *earlier],
        2,
        aliases={len(parts) + i: i for i in range(len(earlier))},
    )


def fetch_start(table_ref, sources, ring, buffer, sems, count):
    flen = buffer.shape[1]
    for j in range(count):
        if not ring:
            start = pl.multiple_of(table_ref[j] * flen, flen)
            pltpu.make_async_copy(sources[0].at[pl.ds(start, flen)], buffer.at[j], sems.at[j]).start()
            continue
        for k in range(8):

            @pl.when(table_ref[j] == k)
            def _(j=j, k=k):
                if k == 4:
                    cut = sources[4].shape[0]
                    pltpu.make_async_copy(sources[4], buffer.at[j, pl.ds(0, cut)], sems.at[j]).start()
                    pltpu.make_async_copy(
                        sources[5], buffer.at[j, pl.ds(cut, flen - cut)], sems.at[j]
                    ).start()
                else:
                    source = sources[k if k < 4 else k + 1]
                    pltpu.make_async_copy(source, buffer.at[j], sems.at[j]).start()


def fetch_wait(sources, buffer, sems, j):
    pltpu.make_async_copy(buffer.at[j], buffer.at[j], sems.at[j]).wait()


def attend_kernel(ring, n_kv, count, table_ref, lens_ref, facts_ref, q_ref, *refs):
    sources, pieces = refs[:n_kv], refs[n_kv : n_kv + count]
    out_ref, lse_ref, part_other_ref, part_own_ref = refs[n_kv + count : n_kv + count + 4]
    acc, sums, stack, buffer, sems = refs[n_kv + count + 4 :]
    step = pl.program_id(0)
    steps = buffer.shape[0]
    rows, width = q_ref.shape
    heads = width // HEAD_DIM

    @pl.when(step == 0)
    def _():
        fetch_start(table_ref, sources, ring, buffer, sems, steps)
        acc[...] = jnp.zeros_like(acc)
        sums[...] = jnp.zeros_like(sums)
        for head in range(heads):
            mine = jnp.where(head_mask((rows, width), head), q_ref[...], 0) * BF16(SCALING)
            stack[head * rows : (head + 1) * rows, :] = mine

    fetch_wait(sources, buffer, sems, step)
    live = live_keys(buffer.shape[1], facts_ref[1], lens_ref[table_ref[step]])
    values_t = buffer[step, :, width:].T
    powers = jnp.where(live, jnp.exp(dot_nt(buffer[step, :, :width], stack[...])), 0.0)
    sums[0:1, :] += jnp.sum(powers, axis=0, keepdims=True)
    low = powers.astype(BF16)
    for head in range(heads):
        lanes = slice(head * HEAD_DIM, (head + 1) * HEAD_DIM)
        acc[lanes, :] += dot_nn(values_t[lanes, :], low[:, head * rows : (head + 1) * rows])

    @pl.when(step == steps - 1)
    def _():
        lse_ref[...] = jnp.zeros_like(lse_ref)
        for head in range(heads):
            lanes = slice(head * HEAD_DIM, (head + 1) * HEAD_DIM)
            total = sums[0:1, head * rows : (head + 1) * rows]
            lse_ref[head : head + 1, :] = jnp.log(total)
            acc[lanes, :] = acc[lanes, :] / total
        out_ref[...] = acc[...].T.astype(BF16)
        weight = joined(pieces)
        half = rows // 2
        part_other_ref[...] = dot_nt(out_ref[half:, :], weight).astype(BF16)
        part_own_ref[...] = dot_nt(out_ref[:half, :], weight)


def attend(queries, sources, ring, pieces, table, lens, facts, wide):
    rows, width = queries.shape
    steps = table.shape[0]
    counts = [min(p.shape[0], limit) for p, limit in pieces]
    return run(
        functools.partial(attend_kernel, ring, len(sources), len(pieces)),
        (steps,),
        [whole(queries.shape)]
        + [pl.BlockSpec(memory_space=pl.ANY)] * len(sources)
        + [column(r, lambda j: 3) for r in counts],
        [whole((rows, width)), whole((8, rows)), whole((rows // 2, wide)), whole((rows // 2, wide))],
        [
            shaped(rows, width, dtype=BF16),
            shaped(8, rows),
            shaped(rows // 2, wide, dtype=BF16),
            shaped(rows // 2, wide),
        ],
        [
            pltpu.VMEM((width, rows), F32),
            pltpu.VMEM((8, rows * width // HEAD_DIM), F32),
            pltpu.VMEM((rows * width // HEAD_DIM, width), BF16),
            pltpu.VMEM((steps, rows, 2 * width), BF16),
            pltpu.SemaphoreType.DMA((steps,)),
        ],
        [table, lens, facts, queries, *sources] + [p for p, _ in pieces],
        3 + 2 * steps,
        prefetch=3,
    )


def attend_back_kernel(ring, n_kv, count, n_out, table_ref, lens_ref, facts_ref, *refs):
    q_ref, o_ref, lse_ref, g_own_ref, g_other_ref = refs[:5]
    refs = refs[5:]
    sources, pieces = refs[:n_kv], refs[n_kv : n_kv + count]
    dq_ref = refs[n_kv + count]
    outs = refs[n_kv + count + 1 : n_kv + count + 1 + n_out]
    acc, lines, stack_q, stack_g, buffer, sems = refs[n_kv + count + 1 + n_out :]
    step = pl.program_id(0)
    steps = buffer.shape[0]
    rows, width = q_ref.shape
    heads = width // HEAD_DIM

    @pl.when(step == 0)
    def _():
        fetch_start(table_ref, sources, ring, buffer, sems, steps)
        acc[...] = jnp.zeros_like(acc)
        if ring:
            for out in outs:
                out[...] = jnp.zeros_like(out)
        weight = joined(pieces)
        grads = jnp.concatenate([dot_nn(ref[...], weight).astype(BF16) for ref in (g_own_ref, g_other_ref)], axis=0)
        turned = (grads.astype(F32) * o_ref[...].astype(F32)).T
        for head in range(heads):
            lanes = slice(head * HEAD_DIM, (head + 1) * HEAD_DIM)
            columns = slice(head * rows, (head + 1) * rows)
            lines[0:1, columns] = lse_ref[head : head + 1, :]
            lines[1:2, columns] = jnp.sum(turned[lanes, :], axis=0, keepdims=True)
            inside = head_mask((rows, width), head)
            stack_q[columns, :] = jnp.where(inside, q_ref[...], 0) * BF16(SCALING)
            stack_g[columns, :] = jnp.where(inside, grads, 0)

    fetch_wait(sources, buffer, sems, step)
    live = live_keys(buffer.shape[1], facts_ref[1], lens_ref[table_ref[step]])
    keys = buffer[step, :, :width]
    keys_t = keys.T
    scores = dot_nt(keys, stack_q[...])
    full = jnp.where(live, jnp.exp(scores - lines[0:1, :]), 0.0)
    grad_probs = dot_nt(buffer[step, :, width:], stack_g[...])
    steep = (full * (grad_probs - lines[1:2, :])).astype(BF16)
    grad_v = dot_nn(full.astype(BF16), stack_g[...])
    grad_k = dot_nn(steep, stack_q[...])
    for head in range(heads):
        lanes = slice(head * HEAD_DIM, (head + 1) * HEAD_DIM)
        acc[lanes, :] += dot_nn(keys_t[lanes, :], steep[:, head * rows : (head + 1) * rows])

    if not ring:
        outs[0][0, :, :width] = grad_k.astype(outs[0].dtype)
        outs[0][0, :, width:] = grad_v.astype(outs[0].dtype)
    else:
        for k in range(8):

            @pl.when(table_ref[step] == k)
            def _(k=k):
                if k == 4:
                    cut = outs[4].shape[0]
                    outs[4][:, :width] = grad_k[:cut].astype(BF16)
                    outs[4][:, width:] = grad_v[:cut].astype(BF16)
                    outs[5][:, :width] = grad_k[cut:].astype(BF16)
                    outs[5][:, width:] = grad_v[cut:].astype(BF16)
                else:
                    out = outs[k if k < 4 else k + 1]
                    out[:, :width] = grad_k.astype(BF16)
                    out[:, width:] = grad_v.astype(BF16)

    @pl.when(step == steps - 1)
    def _():
        dq_ref[...] = acc[...].T * F32(SCALING)


def attend_back(queries, grads, attended, lse, sources, ring, pieces, table, lens, facts, dtype):
    rows, width = queries.shape
    steps = table.shape[0]
    counts = [min(p.shape[0], limit) for p, limit in pieces]
    wide = grads[0].shape[1]
    if ring:
        out_specs = [whole(s.shape) for s in sources]
        out_shape = [shaped(*s.shape, dtype=BF16) for s in sources]
    else:
        out_specs = [pl.BlockSpec((1, rows, 2 * width), lambda j, *_: (j, 0, 0))]
        out_shape = [shaped(steps, rows, 2 * width, dtype=dtype)]
    return run(
        functools.partial(attend_back_kernel, ring, len(sources), len(pieces), len(out_specs)),
        (steps,),
        [
            whole((rows, width)),
            whole((rows, width)),
            whole((8, rows)),
            whole((rows // 2, wide)),
            whole((rows // 2, wide)),
        ]
        + [pl.BlockSpec(memory_space=pl.ANY)] * len(sources)
        + [column(r, lambda j: 3) for r in counts],
        [whole((rows, width))] + out_specs,
        [shaped(rows, width)] + out_shape,
        [
            pltpu.VMEM((width, rows), F32),
            pltpu.VMEM((8, rows * width // HEAD_DIM), F32),
            pltpu.VMEM((rows * width // HEAD_DIM, width), BF16),
            pltpu.VMEM((rows * width // HEAD_DIM, width), BF16),
            pltpu.VMEM((steps, rows, 2 * width), BF16),
            pltpu.SemaphoreType.DMA((steps,)),
        ],
        [table, lens, facts, queries, attended, lse, *grads, *sources] + [p for p, _ in pieces],
        1 + 0.5 * steps,
        prefetch=3,
    )


def per_device(
    block_input,
    cotangent,
    frame_lengths,
    frame_scenes,
    qkv_weight,
    out_weight,
    up_weight,
    down_weight,
    block_gains,
):
    quarter, wide = block_input.shape
    frames = lax.axis_size("frame")
    ring = on_ring()
    my_frame = lax.axis_index("frame")
    my_row = lax.axis_index("row")
    chip, core = my_row // 2, my_row % 2
    width = qkv_weight.shape[3]
    hidden = up_weight.shape[2]
    shard = wide // frames
    half = 2 * quarter
    facts = jnp.stack([chip, core, frame_lengths[my_frame]]).astype(jnp.int32)

    if ring:
        walk = jnp.array(RING, jnp.int32)
        at = jnp.argmax(walk == my_frame).astype(jnp.int32)
        order = lax.dynamic_slice_in_dim(jnp.concatenate([walk, walk]), at, frames)
        lane_order = RING
    else:
        order = jnp.arange(frames, dtype=jnp.int32)
        lane_order = tuple(range(wide // LANES))
    rel_lens = frame_lengths[order]
    other_scene = (frame_scenes[order] != frame_scenes[my_frame]).astype(jnp.int32)
    scene_table = jnp.argsort(other_scene, stable=True)[: frames // 2].astype(jnp.int32)
    frame_table = jnp.zeros((1,), jnp.int32)
    frame_lens = frame_lengths[my_frame].reshape(1)

    def enter(values, masked):
        return run(
            functools.partial(enter_kernel, masked, lane_order),
            (1,),
            [whole(values.shape)] * 2,
            whole((half, wide)),
            shaped(half, wide),
            [],
            [facts, values, row_take(values, 2)],
            1,
            prefetch=1,
        )

    big = whole((half, wide))

    qkv_shard = jnp.transpose(qkv_weight, (0, 2, 1, 3))
    if ring:
        pick = lambda s, b: pl.BlockSpec((1,) + s[1:], lambda *_: (b,) + (0,) * (len(s) - 1))

        def pack_at(block):
            return run(
                pack_at_kernel,
                (1,),
                [pick(qkv_shard.shape, block), pick(out_weight.shape, block)],
                whole((shard, 4 * width)),
                shaped(shard, 4 * width, dtype=BF16),
                [],
                [qkv_shard, out_weight],
                1,
            )

        def pack_ff(block, after=()):
            return run(
                pack_ff_kernel,
                (1,),
                [pick(up_weight.shape, block), pick(down_weight.shape, block)],
                whole((shard, 2 * hidden)),
                shaped(shard, 2 * hidden, dtype=BF16),
                [],
                [up_weight, down_weight],
                1,
                after=after,
            )

    else:

        def pack_at(block):
            return jnp.concatenate([*qkv_shard[block], out_weight[block].T], axis=1)

        def pack_ff(block, after=()):
            return jnp.concatenate([up_weight[block], down_weight[block].T], axis=1)

    def gather(packed):
        return [(lax.all_gather(packed, "frame", axis=0, tiled=True, axis_index_groups=frame_groups()), wide)]

    def scatter(grads):
        return lax.psum_scatter(
            grads, "frame", scatter_dimension=0, tiled=True, axis_index_groups=frame_groups()
        )

    at_zero, ff_zero, at_one = gather(pack_at(0)), gather(pack_ff(0)), gather(pack_at(1))
    ff_one = pack_ff(1)
    weights = [(at_zero, ff_zero), None]
    if ring:
        rows = jnp.concatenate([block_gains[0], block_gains[1], jnp.zeros((4, shard), BF16)]).astype(F32)
        spread = lax.all_to_all(jnp.broadcast_to(rows[None], (frames, 16, shard)), "frame", 0, 0)
        gains_abs = jnp.swapaxes(spread, 0, 1).reshape(16, wide)
    else:
        gains_abs = lax.all_gather(block_gains, "frame", axis=2, tiled=True).astype(F32).reshape(12, wide)
        gains_abs = jnp.concatenate([gains_abs, jnp.zeros((4, wide), F32)])
    heads = lax.dynamic_slice_in_dim(gains_abs, my_row * width, width, 1)
    gains = jnp.concatenate([gains_abs[:, k * LANES : (k + 1) * LANES] for k in lane_order], axis=1)
    h = enter(block_input, False)
    normed = run(
        functools.partial(first_norm_kernel, 0),
        (1,),
        [big, whole(gains.shape)],
        big,
        shaped(half, wide, dtype=BF16),
        [],
        [h, gains],
        1,
    )

    gspec = whole(gains.shape)

    def reduce_rows(other, own):
        near = (own + row_take(other, 1).astype(F32)).astype(BF16)
        return near, row_take(near, 2)

    stored = []
    grad = enter(cotangent, True)
    scaled = run(
        functools.partial(scale_kernel, 9),
        (1,),
        [big, gspec],
        big,
        shaped(half, wide, dtype=BF16),
        [],
        [grad, gains],
        1,
    )
    grad_down = (scaled, row_take(scaled, 1))
    for block in range(2):
        base = 6 * block
        at, ff = weights[block] or (at_one, None)
        normed = (normed, row_take(normed, 1))
        early = [*grad_down, scene_table, rel_lens] if block == 0 else []
        queries, kv, mixed = project(normed, at, heads, base + 4, early)
        if block == 0:
            sources, walking, table, lens = [kv], False, frame_table, frame_lens
        else:
            table, lens, walking = scene_table, rel_lens, ring
            sources = ring_gather(kv, half) if ring else [lax.all_gather(kv, "frame", axis=0, tiled=True)]
            ff = gather(gate(ff_one, [sources[3], sources[6]]) if ring else ff_one)
            weights[1] = (at, ff)
        attended, lse, part_other, part_own = attend(
            queries, sources, walking, at, table, lens, facts, wide
        )
        branch = reduce_rows(part_other, part_own)
        middle, second = run(
            functools.partial(residual_kernel, base + 2, base + 1),
            (1,),
            [big, big, big, gspec],
            [big, big],
            [shaped(half, wide), shaped(half, wide, dtype=BF16)],
            [],
            [h, *branch, gains],
            2,
        )
        second = (second, row_take(second, 1))
        if block == 0:
            up_values, active, part_other, part_own = feed(second, ff, hidden)
        else:
            both = feed_both(second, grad_down, ff[0][0], hidden)
            active, grad_up, part_other, part_own, back_other, back_own = both
            up_values = None
        stored.append(
            (h, normed, queries, mixed, (sources, walking, table, lens), attended, lse, branch)
            + (middle, second, up_values, active)
        )
        if block == 0:
            down_zero = reduce_rows(part_other, part_own)
            h, normed = run(
                functools.partial(residual_kernel, base + 3, base + 6),
                (1,),
                [big, big, big, gspec],
                [big, big],
                [shaped(half, wide), shaped(half, wide, dtype=BF16)],
                [],
                [middle, *down_zero, gains],
                2,
            )

    last_other, last_own = row_take(part_other, 1), part_own
    at_shapes = [(2, 3, shard, width), (2, width, shard)]
    ff_shapes = [(2, shard, hidden), (2, hidden, shard)]
    at_out, ff_out = [], []
    gain_sums = [None, None]
    input_grad = None
    for block in (1, 0):
        base = 6 * block
        at, ff = weights[block]
        h, normed, queries, mixed, keys, attended, lse, branch, middle, second, up_values, active = stored[block]
        sources, walking, table, lens = keys
        if block == 1:
            part_other, part_own = back_other, back_own
        else:
            grad_up, part_other, part_own = feed_back(grad_down, up_values, ff)
        incoming = reduce_rows(part_other, part_own)
        if block == 1:
            up_grads = one_weight_grads(second, grad_up, 5, [incoming[0]])
            ff_grads = one_weight_grads(grad_down, active, 5, [incoming[0]])
            up_sum = scatter(up_grads)
        else:
            ff_grads = weight_grads(second, grad_up, grad_down, active, 3, [incoming[0]])
            ff_grads = gate(ff_grads, [at_sum, incoming[1]])
            ff_sum = scatter(ff_grads)
            if ring:
                ff_out = finish(finish_ff_kernel, [ff_sum], ff_shapes, block, ff_out)
        grad_middle, scaled, sums_middle = run(
            functools.partial(middle_back_kernel, base),
            (1,),
            [big] * 6 + [gspec],
            [big, big, whole((2, wide))],
            [shaped(half, wide), shaped(half, wide, dtype=BF16), shaped(2, wide)],
            [],
            [grad, *incoming, middle, *branch, gains],
            2,
            after=[up_grads, ff_grads] if block == 1 else [ff_grads, *(at_out[:1] if ring else [])],
        )
        grad_branch = (scaled, row_take(scaled, 1))
        if block == 1:
            near = run(
                add_kernel, (1,), [big, big], big, shaped(half, wide, dtype=BF16), [], [last_own, last_other], 1,
                after=[incoming[1]],
            )
            output, sum_three = run(
                functools.partial(output_kernel, base + 3, lane_order),
                (1,),
                [big, big, big, gspec, big],
                [whole((quarter, wide)), whole((1, wide))],
                [shaped(quarter, wide, dtype=BF16), shaped(1, wide)],
                [pltpu.VMEM((half, wide), F32)],
                [facts, middle, near, row_take(near, 2), gains, grad],
                1,
                prefetch=1,
            )
        dq, *dkv_parts = attend_back(
            queries,
            grad_branch,
            attended,
            lse,
            sources,
            walking,
            at,
            table,
            lens,
            facts,
            F32 if block == 0 else BF16,
        )
        if block == 0:
            dkv = dkv_parts[0][0]
        elif ring:
            (own, right, left), sent_last = ring_scatter(dkv_parts)
            dkv = own.astype(F32) + right.astype(F32) + left.astype(F32)
        else:
            spread = jnp.zeros((frames,) + dkv_parts[0].shape[1:], BF16).at[table].set(dkv_parts[0])
            dkv = lax.psum_scatter(spread, "frame", scatter_dimension=0, tiled=False).astype(F32)
        if block == 1:
            down_sum = scatter(gate(ff_grads, [*(sent_last if ring else [dkv]), up_sum]))
            ff_sum = down_sum
            if ring:
                ff_out = finish(finish_two_kernel, [up_sum, down_sum], ff_shapes, 1, ff_out)
        grad_mixed, part_other, part_own, sums_heads, sum_zero = project_back(
            dq, dkv, mixed, at, heads, base + 4, normed, gains, [output] if block == 1 else ()
        )
        gain_sums[block] = (sum_zero, sums_middle, sum_three, sums_heads)
        incoming = reduce_rows(part_other, part_own)
        at_grads = weight_grads(normed, grad_mixed, grad_branch, attended, 4, [incoming[0]])
        at_grads = gate(at_grads, [ff_sum, incoming[1]])
        if block == 1:
            grad, scaled, sum_three = run(
                functools.partial(between_kernel, base),
                (1,),
                [big] * 4 + [gspec, big, big],
                [big, big, whole((1, wide))],
                [shaped(half, wide), shaped(half, wide, dtype=BF16), shaped(1, wide)],
                [],
                [grad_middle, *incoming, h, gains, *down_zero],
                3,
                after=[at_grads],
            )
            grad_down = (scaled, row_take(scaled, 1))
        else:
            input_grad = run(
                functools.partial(last_back_kernel, lane_order),
                (1,),
                [big] * 4 + [gspec],
                whole((quarter, wide)),
                shaped(quarter, wide, dtype=BF16),
                [pltpu.VMEM((half, wide), F32)],
                [facts, grad_middle, *incoming, h, gains],
                2,
                prefetch=1,
                after=[],
            )
        at_sum = scatter(at_grads)
        if ring:
            at_out = finish(finish_at_kernel, [at_sum], at_shapes, block, at_out)
        else:
            ff_parts = [up_sum, down_sum] if block == 1 else [ff_sum[:, :hidden], ff_sum[:, hidden:]]
            ff_out = [(ff_parts[0].astype(F32), ff_parts[1].astype(F32).T)] + ff_out
            at_last = at_sum.astype(F32)
            qkv_sum = jnp.stack([at_last[:, i * width : (i + 1) * width] for i in range(3)])
            at_out = [(qkv_sum, at_last[:, 3 * width :].T)] + at_out
    if not ring:
        ff_out = [jnp.stack(both) for both in zip(*ff_out, strict=True)]
        at_out = [jnp.stack(both) for both in zip(*at_out, strict=True)]

    if ring:
        operands = [*gain_sums[0], *gain_sums[1]]
        sent = run(
            functools.partial(gain_sums_kernel, lane_order),
            (1,),
            [whole(v.shape) for v in operands],
            whole((frames, 16, LANES)),
            shaped(frames, 16, LANES),
            [],
            [facts, *operands],
            1,
            prefetch=1,
            after=[input_grad],
        )
        total = jnp.sum(lax.all_to_all(sent, "frame", 0, 0), axis=0)
        total = total + row_take(total, 1)
        total = total + row_take(total, 2)
        gains_grad = total[:12].reshape(2, 6, LANES)
    else:
        rows = [jnp.concatenate([sums[0], sums[1] * F32(0.5), sums[2] * F32(0.5)]) for sums in gain_sums]
        rows = jnp.stack(rows)
        per_head = lax.dynamic_update_slice_in_dim(
            jnp.zeros((2, 2, wide), F32),
            jnp.stack([gain_sums[0][3], gain_sums[1][3]]),
            my_row * width,
            2,
        )
        total = lax.psum(jnp.concatenate([rows, per_head], axis=1), ("frame", "row"))
        gains_grad = lax.dynamic_slice_in_dim(total, my_frame * shard, shard, 2)
    return (
        output,
        input_grad,
        jnp.transpose(at_out[0], (0, 2, 1, 3)),
        at_out[1],
        ff_out[0],
        ff_out[1],
        gains_grad,
    )


def solution(mesh):
    return jax.shard_map(
        per_device,
        mesh=mesh,
        in_specs=(
            P(("frame", "row"), None),
            P(("frame", "row"), None),
            P(),
            P(),
            P(None, "frame", None, "row"),
            P(None, "row", "frame"),
            P(None, "frame", "row"),
            P(None, "row", "frame"),
            P(None, None, "frame"),
        ),
        out_specs=(
            P(("frame", "row"), None),
            P(("frame", "row"), None),
            P(None, "frame", None, "row"),
            P(None, "row", "frame"),
            P(None, "frame", "row"),
            P(None, "row", "frame"),
            P(None, None, "frame"),
        ),
        check_vma=False,
    )
```

```python
import functools

import jax
import jax.numpy as jnp
from jax import lax
from jax.experimental import pallas as pl
from jax.experimental.pallas import tpu as pltpu
from jax.sharding import PartitionSpec as P

HEAD_DIM = 64
EPSILON = 1e-06
F32 = jnp.float32
BF16 = jnp.bfloat16
LANES = 128
TILE = 256
ROOT_HALF = 0.7071067811865476
BELL = 0.3989422804014327
SCALING = HEAD_DIM**-0.5

RING = (0, 2, 4, 6, 7, 5, 3, 1)


def on_ring():
    return lax.axis_size("frame") == len(RING)


def frame_groups():
    return [list(RING)] if on_ring() else None


def frame_order(frames):
    return RING if on_ring() else tuple(range(frames))


def ring_take(value, step):
    count = len(RING)
    return lax.ppermute(value, "frame", [(RING[(i + step) % count], RING[i]) for i in range(count)])


def row_take(value, bit):
    return lax.ppermute(value, "row", [(i ^ bit, i) for i in range(4)])


def ring_gather(shard, cut):
    ahead, behind = [shard], [shard]
    for _ in range(3):
        ahead.append(ring_take(ahead[-1], 1))
        behind.append(ring_take(behind[-1], -1))
    far_low = ring_take(ahead[3][:cut], 1)
    far_high = ring_take(behind[3][cut:], -1)
    return ahead + [far_low, far_high] + behind[3:0:-1]


def add_pair(a, b):
    return (a.astype(F32) + b.astype(F32)).astype(BF16)


def ring_scatter(pieces):
    ahead = pieces[1:4]
    far_low, far_high = pieces[4:6]
    behind = pieces[8:5:-1]
    cut = far_low.shape[0]
    low = ring_take(far_low, -1)
    high = ring_take(far_high, 1)
    right = jnp.concatenate([add_pair(ahead[2][:cut], low), ahead[2][cut:]])
    left = jnp.concatenate([behind[2][:cut], add_pair(behind[2][cut:], high)])
    for place in (1, 0):
        right = add_pair(ahead[place], ring_take(right, -1))
        left = add_pair(behind[place], ring_take(left, 1))
    return (pieces[0], ring_take(right, -1), ring_take(left, 1)), [right, left]


def dot_nt(a, b):
    return lax.dot_general(a, b, (((1,), (1,)), ((), ())), preferred_element_type=F32)


def dot_nn(a, b):
    return lax.dot_general(a, b, (((1,), (0,)), ((), ())), preferred_element_type=F32)


def whole(shape):
    return pl.BlockSpec(shape, lambda *_: (0,) * len(shape))


def column(rows, place):
    return pl.BlockSpec((rows, TILE), lambda j, *_: (0, place(j)))


WEIGH = 3.0


def cost(us):
    return pl.CostEstimate(
        flops=int(us * WEIGH * 1.0e9), bytes_accessed=int(us * WEIGH * 2.0e6), transcendentals=0
    )


def run(kernel, grid, in_specs, out_specs, out_shape, scratch, operands, us, prefetch=0, aliases=None, after=()):
    count = len(operands)

    def body(*refs):
        kernel(*refs[:count], *refs[count + len(after) :])

    in_specs = list(in_specs) + [pl.BlockSpec(memory_space=pl.ANY)] * len(after)
    operands = [*operands, *after]
    return pl.pallas_call(
        body,
        grid_spec=pltpu.PrefetchScalarGridSpec(
            num_scalar_prefetch=prefetch,
            grid=grid,
            in_specs=in_specs,
            out_specs=out_specs,
            scratch_shapes=scratch,
        ),
        out_shape=out_shape,
        input_output_aliases=aliases or {},
        compiler_params=pltpu.CompilerParams(vmem_limit_bytes=56 * 1024 * 1024),
        cost_estimate=cost(us),
    )(*operands)


def shaped(*shape, dtype=F32):
    return jax.ShapeDtypeStruct(shape, dtype)


def norm_parts(values):
    center = values - jnp.mean(values, axis=-1, keepdims=True)
    scale = lax.rsqrt(jnp.mean(center * center, axis=-1, keepdims=True) + EPSILON)
    return center * scale, scale


def norm_back(unit, scale, gain, grad):
    inner = grad * gain
    return scale * (
        inner
        - jnp.mean(inner, axis=-1, keepdims=True)
        - unit * jnp.mean(inner * unit, axis=-1, keepdims=True)
    )


def head_means(values):
    width = values.shape[-1]
    rows = lax.broadcasted_iota(jnp.int32, (width, width), 0) // HEAD_DIM
    cols = lax.broadcasted_iota(jnp.int32, (width, width), 1) // HEAD_DIM
    spread = jnp.where(rows == cols, F32(1.0 / HEAD_DIM), F32(0)).astype(BF16)
    high = values.astype(BF16)
    low = (values - high.astype(F32)).astype(BF16)
    return dot_nn(high, spread) + dot_nn(low, spread)


def head_parts(values):
    center = values - head_means(values)
    scale = lax.rsqrt(head_means(center * center) + EPSILON)
    return center * scale, scale


def head_back(unit, scale, gain, grad):
    inner = grad * gain
    return scale * (inner - head_means(inner) - unit * head_means(inner * unit))


def joined(refs):
    if len(refs) == 1:
        return refs[0][...]
    return jnp.concatenate([ref[...] for ref in refs], axis=0)


def head_mask(shape, head):
    lanes = lax.broadcasted_iota(jnp.int32, shape, 1)
    return (lanes // HEAD_DIM) == head


def live_keys(count, core, length):
    place = lax.broadcasted_iota(jnp.int32, (count, 1), 0)
    quarter = count // 4
    half = place // (2 * quarter)
    chip = (place // quarter) % 2
    slot = (chip * 2 + (half ^ core)) * quarter + place % quarter
    return slot < length


def pack_at_kernel(qkv_ref, out_ref, at_ref):
    rows = out_ref.shape[2]
    width = qkv_ref.shape[3]
    for i in range(3):
        at_ref[:rows, i * width : (i + 1) * width] = qkv_ref[0, i]
    at_ref[:rows, 3 * width :] = out_ref[0].T


def pack_ff_kernel(up_ref, down_ref, ff_ref):
    ff = up_ref.shape[2]
    ff_ref[:, :ff] = up_ref[0]
    ff_ref[:, ff:] = down_ref[0].T


def gain_sums_kernel(order, facts_ref, *refs):
    out_ref = refs[-1]
    out_ref[...] = jnp.zeros_like(out_ref)
    row = facts_ref[0] * 2 + facts_ref[1]
    for block in range(2):
        zero, middle, three, heads = refs[4 * block : 4 * block + 4]
        base = 6 * block
        for k in range(out_ref.shape[0]):
            lanes = slice(k * LANES, (k + 1) * LANES)
            place = order[k]
            out_ref[place, base : base + 1, :] = zero[:, lanes]
            out_ref[place, base + 1 : base + 3, :] = middle[:, lanes] * 0.5
            out_ref[place, base + 3 : base + 4, :] = three[:, lanes] * 0.5
        for k in range(2):
            lanes = slice(k * LANES, (k + 1) * LANES)
            out_ref[row * 2 + k, base + 4 : base + 6, :] = heads[:, lanes]


def enter_kernel(masked, order, facts_ref, own_ref, far_ref, out_ref):
    rows = own_ref.shape[0]
    chip, core, length = facts_ref[0], facts_ref[1], facts_ref[2]
    for k in range(len(order)):
        lanes = slice(order[k] * LANES, (order[k] + 1) * LANES)
        for source, place in ((own_ref, chip), (far_ref, 1 - chip)):
            values = source[:, lanes].astype(F32)
            if masked:
                slots = (place * 2 + core) * rows + lax.broadcasted_iota(jnp.int32, (rows, 1), 0)
                values = jnp.where(slots < length, values, 0.0)
            start = pl.multiple_of(place * rows, rows)
            out_ref[pl.ds(start, rows), k * LANES : (k + 1) * LANES] = values


def leave(values_ref, order, facts_ref, out_ref):
    rows = out_ref.shape[0]
    start = pl.multiple_of(facts_ref[0] * rows, rows)
    for k in range(len(order)):
        lanes = slice(order[k] * LANES, (order[k] + 1) * LANES)
        values = values_ref[pl.ds(start, rows), k * LANES : (k + 1) * LANES]
        out_ref[:, lanes] = values.astype(out_ref.dtype)


def first_norm_kernel(row, h_ref, gains_ref, normed_ref):
    unit, _ = norm_parts(h_ref[...])
    normed_ref[...] = (unit * gains_ref[row : row + 1, :]).astype(BF16)


def add_up(ref, value):
    ref[...] = jnp.where(pl.program_id(0) == 0, value, ref[...] + value)


def total_of(own_ref, far_ref):
    return own_ref[...].astype(F32) + far_ref[...].astype(F32)


def residual_kernel(scale_row, norm_row, h_ref, own_ref, far_ref, gains_ref, next_ref, normed_ref):
    value = h_ref[...] + gains_ref[scale_row : scale_row + 1, :] * total_of(own_ref, far_ref)
    next_ref[...] = value
    unit, _ = norm_parts(value)
    normed_ref[...] = (unit * gains_ref[norm_row : norm_row + 1, :]).astype(BF16)


def add_kernel(own_ref, other_ref, sum_ref):
    sum_ref[...] = (own_ref[...] + other_ref[...].astype(F32)).astype(BF16)


def output_kernel(scale_row, order, facts_ref, h_ref, own_ref, far_ref, gains_ref, grad_ref, out_ref, sums_ref, held):
    total = total_of(own_ref, far_ref)
    held[...] = h_ref[...] + gains_ref[scale_row : scale_row + 1, :] * total
    sums_ref[...] = jnp.sum(grad_ref[...] * total, axis=0, keepdims=True)
    leave(held, order, facts_ref, out_ref)


def scale_kernel(row, grad_ref, gains_ref, scaled_ref):
    scaled_ref[...] = (grad_ref[...] * gains_ref[row : row + 1, :]).astype(BF16)


def middle_back_kernel(
    base, grad_ref, own_ref, far_ref, middle_ref, b_own_ref, b_far_ref, gains_ref, next_ref, scaled_ref, sums_ref
):
    grad_in = total_of(own_ref, far_ref)
    unit, scale = norm_parts(middle_ref[...])
    first = jnp.sum(grad_in * unit, axis=0, keepdims=True)
    grad = grad_ref[...] + norm_back(unit, scale, gains_ref[base + 1 : base + 2, :], grad_in)
    next_ref[...] = grad
    second = jnp.sum(grad * total_of(b_own_ref, b_far_ref), axis=0, keepdims=True)
    add_up(sums_ref, jnp.concatenate([first, second], axis=0))
    scaled_ref[...] = (grad * gains_ref[base + 2 : base + 3, :]).astype(BF16)


def first_back(base, grad_ref, own_ref, far_ref, h_ref, gains_ref):
    unit, scale = norm_parts(h_ref[...])
    return grad_ref[...] + norm_back(unit, scale, gains_ref[base : base + 1, :], total_of(own_ref, far_ref))


def between_kernel(
    base, grad_ref, own_ref, far_ref, h_ref, gains_ref, d_own_ref, d_far_ref, next_ref, scaled_ref, sums_ref
):
    grad = first_back(base, grad_ref, own_ref, far_ref, h_ref, gains_ref)
    next_ref[...] = grad
    scaled_ref[...] = (grad * gains_ref[base - 3 : base - 2, :]).astype(BF16)
    add_up(sums_ref, jnp.sum(grad * total_of(d_own_ref, d_far_ref), axis=0, keepdims=True))


def last_back_kernel(order, facts_ref, grad_ref, own_ref, far_ref, h_ref, gains_ref, out_ref, held):
    held[...] = first_back(0, grad_ref, own_ref, far_ref, h_ref, gains_ref)
    leave(held, order, facts_ref, out_ref)


def project_kernel(row_q, count, own_ref, other_ref, *refs):
    pieces = refs[:count]
    heads_ref, q_ref, kv_ref, mixed_ref = refs[count:]
    step = pl.program_id(0)
    weight = joined(pieces)
    half = own_ref.shape[0]
    mixed = jnp.concatenate([dot_nn(own_ref[...], weight), dot_nn(other_ref[...], weight)], axis=0)

    @pl.when(step < 2)
    def _():
        mixed_ref[...] = mixed
        unit, _ = head_parts(mixed)
        gain = jnp.where(step == 0, heads_ref[row_q : row_q + 1, :], heads_ref[row_q + 1 : row_q + 2, :])
        scaled = (unit * gain).astype(BF16)

        @pl.when(step == 0)
        def _():
            q_ref[...] = scaled

        @pl.when(step == 1)
        def _():
            kv_ref[...] = scaled

    @pl.when(step == 2)
    def _():
        kv_ref[...] = mixed.astype(BF16)


def project(normed, pieces, heads, row_q, after):
    own, other = normed
    half, wide = own.shape
    width = heads.shape[1]
    rows = [min(p.shape[0], limit) for p, limit in pieces]
    return run(
        functools.partial(project_kernel, row_q, len(pieces)),
        (3,),
        [whole(own.shape), whole(other.shape)]
        + [column(r, lambda j: j) for r in rows]
        + [whole(heads.shape)],
        [
            whole((2 * half, width)),
            column(2 * half, lambda j: jnp.maximum(j - 1, 0)),
            column(2 * half, lambda j: jnp.minimum(j, 1)),
        ],
        [
            shaped(2 * half, width, dtype=BF16),
            shaped(2 * half, 2 * width, dtype=BF16),
            shaped(2 * half, 2 * width),
        ],
        [],
        [own, other] + [p for p, _ in pieces] + [heads],
        5,
        after=after,
    )


def project_back_kernel(row_q, count, dq_ref, dkv_ref, mixed_ref, heads_ref, n_own_ref, n_other_ref, gains_ref, *refs):
    pieces = refs[:count]
    grad_ref, other_ref, own_ref, sums_ref, zero_ref, acc = refs[count:]
    step = pl.program_id(0)

    @pl.when(step == 0)
    def _():
        acc[...] = jnp.zeros_like(acc)

    def normed(incoming, row, place):
        unit, scale = head_parts(mixed_ref[...])
        sums_ref[place : place + 1, :] = jnp.sum(incoming * unit, axis=0, keepdims=True)
        grad_ref[...] = head_back(unit, scale, heads_ref[row : row + 1, :], incoming).astype(BF16)

    @pl.when(step == 0)
    def _():
        normed(dq_ref[...], row_q, 0)

    @pl.when(step == 1)
    def _():
        normed(dkv_ref[...].astype(F32), row_q + 1, 1)

    @pl.when(step == 2)
    def _():
        grad_ref[...] = dkv_ref[...].astype(BF16)

    acc[...] += dot_nt(grad_ref[...], joined(pieces))

    @pl.when(step == 2)
    def _():
        half = own_ref.shape[0]
        own_ref[...] = acc[:half, :]
        other_ref[...] = acc[half:, :].astype(BF16)
        products = acc[:half, :] * n_own_ref[...].astype(F32) + acc[half:, :] * n_other_ref[...].astype(F32)
        row_g = row_q - 4
        zero_ref[...] = jnp.sum(products, axis=0, keepdims=True) / gains_ref[row_g : row_g + 1, :]


def project_back(dq, dkv, mixed, pieces, heads, row_q, normed, gains, after):
    full, width = dq.shape
    wide = gains.shape[1]
    rows = [min(p.shape[0], limit) for p, limit in pieces]
    return run(
        functools.partial(project_back_kernel, row_q, len(pieces)),
        (3,),
        [
            whole(dq.shape),
            column(full, lambda j: jnp.maximum(j - 1, 0)),
            column(full, lambda j: jnp.minimum(j, 1)),
            whole(heads.shape),
            whole((full // 2, wide)),
            whole((full // 2, wide)),
            whole(gains.shape),
        ]
        + [column(r, lambda j: j) for r in rows],
        [
            column(full, lambda j: j),
            whole((full // 2, wide)),
            whole((full // 2, wide)),
            whole((2, width)),
            whole((1, wide)),
        ],
        [
            shaped(full, 3 * width, dtype=BF16),
            shaped(full // 2, wide, dtype=BF16),
            shaped(full // 2, wide),
            shaped(2, width),
            shaped(1, wide),
        ],
        [pltpu.VMEM((full, wide), F32)],
        [dq, dkv, mixed, heads, *normed, gains] + [p for p, _ in pieces],
        6,
        after=after,
    )


def feed_kernel(count, own_ref, other_ref, *refs):
    ups, downs = refs[:count], refs[count : 2 * count]
    values_ref, active_ref, part_other_ref, part_own_ref, acc = refs[2 * count :]
    step = pl.program_id(0)

    @pl.when(step == 0)
    def _():
        acc[...] = jnp.zeros_like(acc)

    weight = joined(ups)
    half = own_ref.shape[0]
    for source, start in ((own_ref, 0), (other_ref, half)):
        values = dot_nn(source[...], weight)
        values_ref[start : start + half, :] = values
        active_ref[start : start + half, :] = (
            0.5 * values * (1.0 + lax.erf(values * F32(ROOT_HALF)))
        ).astype(BF16)
    acc[...] += dot_nt(active_ref[...], joined(downs))

    @pl.when(step == pl.num_programs(0) - 1)
    def _():
        part_own_ref[...] = acc[:half, :]
        part_other_ref[...] = acc[half:, :].astype(BF16)


def feed(second, pieces, hidden):
    own, other = second
    half, wide = own.shape
    steps = hidden // TILE
    rows = [min(p.shape[0], limit) for p, limit in pieces]
    arrays = [p for p, _ in pieces]
    return run(
        functools.partial(feed_kernel, len(pieces)),
        (steps,),
        [whole(own.shape), whole(other.shape)]
        + [column(r, lambda j: j) for r in rows]
        + [column(r, lambda j: j + steps) for r in rows],
        [
            column(2 * half, lambda j: j),
            column(2 * half, lambda j: j),
            whole((half, wide)),
            whole((half, wide)),
        ],
        [
            shaped(2 * half, hidden),
            shaped(2 * half, hidden, dtype=BF16),
            shaped(half, wide, dtype=BF16),
            shaped(half, wide),
        ],
        [pltpu.VMEM((2 * half, wide), F32)],
        [own, other] + arrays + arrays,
        7,
    )


def feed_back_kernel(count, own_ref, other_ref, values_ref, *refs):
    ups, downs = refs[:count], refs[count : 2 * count]
    grad_ref, part_other_ref, part_own_ref, acc = refs[2 * count :]
    step = pl.program_id(0)

    @pl.when(step == 0)
    def _():
        acc[...] = jnp.zeros_like(acc)

    weight = joined(downs)
    half = own_ref.shape[0]
    for source, start in ((own_ref, 0), (other_ref, half)):
        incoming = dot_nn(source[...], weight)
        values = values_ref[start : start + half, :]
        slope = 0.5 * (1.0 + lax.erf(values * F32(ROOT_HALF))) + values * (
            jnp.exp(-0.5 * values * values) * F32(BELL)
        )
        grad_ref[start : start + half, :] = (incoming * slope).astype(BF16)
    acc[...] += dot_nt(grad_ref[...], joined(ups))

    @pl.when(step == pl.num_programs(0) - 1)
    def _():
        part_own_ref[...] = acc[:half, :]
        part_other_ref[...] = acc[half:, :].astype(BF16)


def feed_back(grads, values, pieces):
    own, other = grads
    half, wide = own.shape
    hidden = values.shape[1]
    steps = hidden // TILE
    rows = [min(p.shape[0], limit) for p, limit in pieces]
    arrays = [p for p, _ in pieces]
    return run(
        functools.partial(feed_back_kernel, len(pieces)),
        (steps,),
        [whole(own.shape), whole(other.shape), column(2 * half, lambda j: j)]
        + [column(r, lambda j: j) for r in rows]
        + [column(r, lambda j: j + steps) for r in rows],
        [column(2 * half, lambda j: j), whole((half, wide)), whole((half, wide))],
        [
            shaped(2 * half, hidden, dtype=BF16),
            shaped(half, wide, dtype=BF16),
            shaped(half, wide),
        ],
        [pltpu.VMEM((2 * half, wide), F32)],
        [own, other, values] + arrays + arrays,
        3,
    )


def feed_both_kernel(own_ref, other_ref, g_own_ref, g_other_ref, up_ref, down_ref, *refs):
    active_ref, grad_ref, part_other_ref, part_own_ref, back_other_ref, back_own_ref, acc, back = refs
    step = pl.program_id(0)

    @pl.when(step == 0)
    def _():
        acc[...] = jnp.zeros_like(acc)
        back[...] = jnp.zeros_like(back)

    up, down = up_ref[...], down_ref[...]
    half = own_ref.shape[0]
    for source, g_source, start in ((own_ref, g_own_ref, 0), (other_ref, g_other_ref, half)):
        values = dot_nn(source[...], up)
        gate_part = 0.5 * (1.0 + lax.erf(values * F32(ROOT_HALF)))
        active_ref[start : start + half, :] = (values * gate_part).astype(BF16)
        slope = gate_part + values * (jnp.exp(-0.5 * values * values) * F32(BELL))
        grad_ref[start : start + half, :] = (dot_nn(g_source[...], down) * slope).astype(BF16)
    acc[...] += dot_nt(active_ref[...], down)
    back[...] += dot_nt(grad_ref[...], up)

    @pl.when(step == pl.num_programs(0) - 1)
    def _():
        part_own_ref[...] = acc[:half, :]
        part_other_ref[...] = acc[half:, :].astype(BF16)
        back_own_ref[...] = back[:half, :]
        back_other_ref[...] = back[half:, :].astype(BF16)


def feed_both(second, grads, weight, hidden):
    half, wide = second[0].shape
    steps = hidden // TILE
    return run(
        feed_both_kernel,
        (steps,),
        [whole((half, wide))] * 4 + [column(wide, lambda j: j), column(wide, lambda j: j + steps)],
        [column(2 * half, lambda j: j)] * 2 + [whole((half, wide))] * 4,
        [shaped(2 * half, hidden, dtype=BF16)] * 2 + [shaped(half, wide, dtype=BF16), shaped(half, wide)] * 2,
        [pltpu.VMEM((2 * half, wide), F32)] * 2,
        [*second, *grads, weight, weight],
        10,
    )


def weight_kernel(split, a_own, a_other, b_own, b_other, first_ref, second_ref, out_ref, turned):
    step = pl.program_id(0)
    half = a_own.shape[0]

    def turn(own, other):
        turned[:, :half] = own[...].T
        turned[:, half:] = other[...].T

    @pl.when(step == 0)
    def _():
        turn(a_own, a_other)

    @pl.when(step == split)
    def _():
        turn(b_own, b_other)

    @pl.when(step < split)
    def _():
        out_ref[...] = dot_nn(turned[...], first_ref[...]).astype(BF16)

    @pl.when(step >= split)
    def _():
        out_ref[...] = dot_nn(turned[...], second_ref[...]).astype(BF16)


def gate_kernel(*refs):
    pass


def gate(value, after):
    anywhere = pl.BlockSpec(memory_space=pl.ANY)
    return run(
        gate_kernel, (1,), [anywhere], anywhere, jax.ShapeDtypeStruct(value.shape, value.dtype), [], [value], 0.1,
        aliases={0: 0}, after=after,
    )


def one_weight_kernel(own, other, right_ref, out_ref, turned):
    half = own.shape[0]

    @pl.when(pl.program_id(0) == 0)
    def _():
        turned[:, :half] = own[...].T
        turned[:, half:] = other[...].T

    out_ref[...] = dot_nn(turned[...], right_ref[...]).astype(BF16)


def one_weight_grads(a, right, us, after):
    half, wide = a[0].shape
    return run(
        one_weight_kernel,
        (right.shape[1] // TILE,),
        [whole((half, wide))] * 2 + [column(2 * half, lambda j: j)],
        column(wide, lambda j: j),
        shaped(wide, right.shape[1], dtype=BF16),
        [pltpu.VMEM((wide, 2 * half), BF16)],
        [*a, right],
        us,
        after=after,
    )


def weight_grads(a, first, b, second, us, after):
    half, wide = a[0].shape
    split = first.shape[1] // TILE
    steps = split + second.shape[1] // TILE
    return run(
        functools.partial(weight_kernel, split),
        (steps,),
        [whole((half, wide))] * 4
        + [
            column(2 * half, lambda j: jnp.minimum(j, split - 1)),
            column(2 * half, lambda j: jnp.maximum(j - split, 0)),
        ],
        column(wide, lambda j: j),
        shaped(wide, steps * TILE, dtype=BF16),
        [pltpu.VMEM((wide, 2 * half), BF16)],
        [*a, *b, first, second],
        us,
        after=after,
    )


def finish_ff_kernel(part_ref, *refs):
    up_ref, down_ref = refs[-2:]
    hidden = up_ref.shape[2]
    up_ref[0] = part_ref[:, :hidden].astype(F32)
    down_ref[0] = part_ref[:, hidden:].astype(F32).T


def finish_two_kernel(up_part_ref, down_part_ref, up_ref, down_ref):
    up_ref[0] = up_part_ref[...].astype(F32)
    down_ref[0] = down_part_ref[...].astype(F32).T


def finish_at_kernel(part_ref, *refs):
    qkv_ref, out_ref = refs[-2:]
    width = qkv_ref.shape[3]
    for i in range(3):
        qkv_ref[0, i] = part_ref[:, i * width : (i + 1) * width].astype(F32)
    out_ref[0] = part_ref[:, 3 * width :].astype(F32).T


def finish(kernel, parts, shapes, block, earlier):
    specs = [
        pl.BlockSpec((1,) + s[1:], functools.partial(lambda b, r, *_: (b,) + (0,) * (r - 1), block, len(s)))
        for s in shapes
    ]
    return run(
        kernel,
        (1,),
        [whole(part.shape) for part in parts] + [pl.BlockSpec(memory_space=pl.ANY)] * len(earlier),
        specs,
        [shaped(*s) for s in shapes],
        [],
        [*parts, *earlier],
        2,
        aliases={len(parts) + i: i for i in range(len(earlier))},
    )


def fetch_start(table_ref, sources, ring, buffer, sems, count):
    flen = buffer.shape[1]
    for j in range(count):
        if not ring:
            start = pl.multiple_of(table_ref[j] * flen, flen)
            pltpu.make_async_copy(sources[0].at[pl.ds(start, flen)], buffer.at[j], sems.at[j]).start()
            continue
        for k in range(8):

            @pl.when(table_ref[j] == k)
            def _(j=j, k=k):
                if k == 4:
                    cut = sources[4].shape[0]
                    pltpu.make_async_copy(sources[4], buffer.at[j, pl.ds(0, cut)], sems.at[j]).start()
                    pltpu.make_async_copy(
                        sources[5], buffer.at[j, pl.ds(cut, flen - cut)], sems.at[j]
                    ).start()
                else:
                    source = sources[k if k < 4 else k + 1]
                    pltpu.make_async_copy(source, buffer.at[j], sems.at[j]).start()


def fetch_wait(sources, buffer, sems, j):
    pltpu.make_async_copy(buffer.at[j], buffer.at[j], sems.at[j]).wait()


def attend_kernel(ring, n_kv, count, table_ref, lens_ref, facts_ref, q_ref, *refs):
    sources, pieces = refs[:n_kv], refs[n_kv : n_kv + count]
    out_ref, lse_ref, part_other_ref, part_own_ref = refs[n_kv + count : n_kv + count + 4]
    acc, sums, stack, buffer, sems = refs[n_kv + count + 4 :]
    step = pl.program_id(0)
    steps = buffer.shape[0]
    rows, width = q_ref.shape
    heads = width // HEAD_DIM

    @pl.when(step == 0)
    def _():
        fetch_start(table_ref, sources, ring, buffer, sems, steps)
        acc[...] = jnp.zeros_like(acc)
        sums[...] = jnp.zeros_like(sums)
        for head in range(heads):
            mine = jnp.where(head_mask((rows, width), head), q_ref[...], 0) * BF16(SCALING)
            stack[head * rows : (head + 1) * rows, :] = mine

    fetch_wait(sources, buffer, sems, step)
    live = live_keys(buffer.shape[1], facts_ref[1], lens_ref[table_ref[step]])
    values_t = buffer[step, :, width:].T
    powers = jnp.where(live, jnp.exp(dot_nt(buffer[step, :, :width], stack[...])), 0.0)
    sums[0:1, :] += jnp.sum(powers, axis=0, keepdims=True)
    low = powers.astype(BF16)
    for head in range(heads):
        lanes = slice(head * HEAD_DIM, (head + 1) * HEAD_DIM)
        acc[lanes, :] += dot_nn(values_t[lanes, :], low[:, head * rows : (head + 1) * rows])

    @pl.when(step == steps - 1)
    def _():
        lse_ref[...] = jnp.zeros_like(lse_ref)
        for head in range(heads):
            lanes = slice(head * HEAD_DIM, (head + 1) * HEAD_DIM)
            total = sums[0:1, head * rows : (head + 1) * rows]
            lse_ref[head : head + 1, :] = jnp.log(total)
            acc[lanes, :] = acc[lanes, :] / total
        out_ref[...] = acc[...].T.astype(BF16)
        weight = joined(pieces)
        half = rows // 2
        part_other_ref[...] = dot_nt(out_ref[half:, :], weight).astype(BF16)
        part_own_ref[...] = dot_nt(out_ref[:half, :], weight)


def attend(queries, sources, ring, pieces, table, lens, facts, wide):
    rows, width = queries.shape
    steps = table.shape[0]
    counts = [min(p.shape[0], limit) for p, limit in pieces]
    return run(
        functools.partial(attend_kernel, ring, len(sources), len(pieces)),
        (steps,),
        [whole(queries.shape)]
        + [pl.BlockSpec(memory_space=pl.ANY)] * len(sources)
        + [column(r, lambda j: 3) for r in counts],
        [whole((rows, width)), whole((8, rows)), whole((rows // 2, wide)), whole((rows // 2, wide))],
        [
            shaped(rows, width, dtype=BF16),
            shaped(8, rows),
            shaped(rows // 2, wide, dtype=BF16),
            shaped(rows // 2, wide),
        ],
        [
            pltpu.VMEM((width, rows), F32),
            pltpu.VMEM((8, rows * width // HEAD_DIM), F32),
            pltpu.VMEM((rows * width // HEAD_DIM, width), BF16),
            pltpu.VMEM((steps, rows, 2 * width), BF16),
            pltpu.SemaphoreType.DMA((steps,)),
        ],
        [table, lens, facts, queries, *sources] + [p for p, _ in pieces],
        3 + 2 * steps,
        prefetch=3,
    )


def attend_back_kernel(ring, n_kv, count, n_out, table_ref, lens_ref, facts_ref, *refs):
    q_ref, o_ref, lse_ref, g_own_ref, g_other_ref = refs[:5]
    refs = refs[5:]
    sources, pieces = refs[:n_kv], refs[n_kv : n_kv + count]
    dq_ref = refs[n_kv + count]
    outs = refs[n_kv + count + 1 : n_kv + count + 1 + n_out]
    acc, lines, stack_q, stack_g, buffer, sems = refs[n_kv + count + 1 + n_out :]
    step = pl.program_id(0)
    steps = buffer.shape[0]
    rows, width = q_ref.shape
    heads = width // HEAD_DIM

    @pl.when(step == 0)
    def _():
        fetch_start(table_ref, sources, ring, buffer, sems, steps)
        acc[...] = jnp.zeros_like(acc)
        if ring:
            for out in outs:
                out[...] = jnp.zeros_like(out)
        weight = joined(pieces)
        grads = jnp.concatenate([dot_nn(ref[...], weight).astype(BF16) for ref in (g_own_ref, g_other_ref)], axis=0)
        turned = (grads.astype(F32) * o_ref[...].astype(F32)).T
        for head in range(heads):
            lanes = slice(head * HEAD_DIM, (head + 1) * HEAD_DIM)
            columns = slice(head * rows, (head + 1) * rows)
            lines[0:1, columns] = lse_ref[head : head + 1, :]
            lines[1:2, columns] = jnp.sum(turned[lanes, :], axis=0, keepdims=True)
            inside = head_mask((rows, width), head)
            stack_q[columns, :] = jnp.where(inside, q_ref[...], 0) * BF16(SCALING)
            stack_g[columns, :] = jnp.where(inside, grads, 0)

    fetch_wait(sources, buffer, sems, step)
    live = live_keys(buffer.shape[1], facts_ref[1], lens_ref[table_ref[step]])
    keys = buffer[step, :, :width]
    keys_t = keys.T
    scores = dot_nt(keys, stack_q[...])
    full = jnp.where(live, jnp.exp(scores - lines[0:1, :]), 0.0)
    grad_probs = dot_nt(buffer[step, :, width:], stack_g[...])
    steep = (full * (grad_probs - lines[1:2, :])).astype(BF16)
    grad_v = dot_nn(full.astype(BF16), stack_g[...])
    grad_k = dot_nn(steep, stack_q[...])
    for head in range(heads):
        lanes = slice(head * HEAD_DIM, (head + 1) * HEAD_DIM)
        acc[lanes, :] += dot_nn(keys_t[lanes, :], steep[:, head * rows : (head + 1) * rows])

    if not ring:
        outs[0][0, :, :width] = grad_k.astype(outs[0].dtype)
        outs[0][0, :, width:] = grad_v.astype(outs[0].dtype)
    else:
        for k in range(8):

            @pl.when(table_ref[step] == k)
            def _(k=k):
                if k == 4:
                    cut = outs[4].shape[0]
                    outs[4][:, :width] = grad_k[:cut].astype(BF16)
                    outs[4][:, width:] = grad_v[:cut].astype(BF16)
                    outs[5][:, :width] = grad_k[cut:].astype(BF16)
                    outs[5][:, width:] = grad_v[cut:].astype(BF16)
                else:
                    out = outs[k if k < 4 else k + 1]
                    out[:, :width] = grad_k.astype(BF16)
                    out[:, width:] = grad_v.astype(BF16)

    @pl.when(step == steps - 1)
    def _():
        dq_ref[...] = acc[...].T * F32(SCALING)


def attend_back(queries, grads, attended, lse, sources, ring, pieces, table, lens, facts, dtype):
    rows, width = queries.shape
    steps = table.shape[0]
    counts = [min(p.shape[0], limit) for p, limit in pieces]
    wide = grads[0].shape[1]
    if ring:
        out_specs = [whole(s.shape) for s in sources]
        out_shape = [shaped(*s.shape, dtype=BF16) for s in sources]
    else:
        out_specs = [pl.BlockSpec((1, rows, 2 * width), lambda j, *_: (j, 0, 0))]
        out_shape = [shaped(steps, rows, 2 * width, dtype=dtype)]
    return run(
        functools.partial(attend_back_kernel, ring, len(sources), len(pieces), len(out_specs)),
        (steps,),
        [
            whole((rows, width)),
            whole((rows, width)),
            whole((8, rows)),
            whole((rows // 2, wide)),
            whole((rows // 2, wide)),
        ]
        + [pl.BlockSpec(memory_space=pl.ANY)] * len(sources)
        + [column(r, lambda j: 3) for r in counts],
        [whole((rows, width))] + out_specs,
        [shaped(rows, width)] + out_shape,
        [
            pltpu.VMEM((width, rows), F32),
            pltpu.VMEM((8, rows * width // HEAD_DIM), F32),
            pltpu.VMEM((rows * width // HEAD_DIM, width), BF16),
            pltpu.VMEM((rows * width // HEAD_DIM, width), BF16),
            pltpu.VMEM((steps, rows, 2 * width), BF16),
            pltpu.SemaphoreType.DMA((steps,)),
        ],
        [table, lens, facts, queries, attended, lse, *grads, *sources] + [p for p, _ in pieces],
        1 + 0.5 * steps,
        prefetch=3,
    )


def per_device(
    block_input,
    cotangent,
    frame_lengths,
    frame_scenes,
    qkv_weight,
    out_weight,
    up_weight,
    down_weight,
    block_gains,
):
    quarter, wide = block_input.shape
    frames = lax.axis_size("frame")
    ring = on_ring()
    my_frame = lax.axis_index("frame")
    my_row = lax.axis_index("row")
    chip, core = my_row // 2, my_row % 2
    width = qkv_weight.shape[3]
    hidden = up_weight.shape[2]
    shard = wide // frames
    half = 2 * quarter
    facts = jnp.stack([chip, core, frame_lengths[my_frame]]).astype(jnp.int32)

    if ring:
        walk = jnp.array(RING, jnp.int32)
        at = jnp.argmax(walk == my_frame).astype(jnp.int32)
        order = lax.dynamic_slice_in_dim(jnp.concatenate([walk, walk]), at, frames)
        lane_order = RING
    else:
        order = jnp.arange(frames, dtype=jnp.int32)
        lane_order = tuple(range(wide // LANES))
    rel_lens = frame_lengths[order]
    other_scene = (frame_scenes[order] != frame_scenes[my_frame]).astype(jnp.int32)
    scene_table = jnp.argsort(other_scene, stable=True)[: frames // 2].astype(jnp.int32)
    frame_table = jnp.zeros((1,), jnp.int32)
    frame_lens = frame_lengths[my_frame].reshape(1)

    def enter(values, masked):
        return run(
            functools.partial(enter_kernel, masked, lane_order),
            (1,),
            [whole(values.shape)] * 2,
            whole((half, wide)),
            shaped(half, wide),
            [],
            [facts, values, row_take(values, 2)],
            1,
            prefetch=1,
        )

    big = whole((half, wide))
    part = pl.BlockSpec((half // 2, wide), lambda j, *_: (j, 0))

    qkv_shard = jnp.transpose(qkv_weight, (0, 2, 1, 3))
    if ring:
        pick = lambda s, b: pl.BlockSpec((1,) + s[1:], lambda *_: (b,) + (0,) * (len(s) - 1))

        def pack_at(block):
            return run(
                pack_at_kernel,
                (1,),
                [pick(qkv_shard.shape, block), pick(out_weight.shape, block)],
                whole((shard, 4 * width)),
                shaped(shard, 4 * width, dtype=BF16),
                [],
                [qkv_shard, out_weight],
                1,
            )

        def pack_ff(block, after=()):
            return run(
                pack_ff_kernel,
                (1,),
                [pick(up_weight.shape, block), pick(down_weight.shape, block)],
                whole((shard, 2 * hidden)),
                shaped(shard, 2 * hidden, dtype=BF16),
                [],
                [up_weight, down_weight],
                1,
                after=after,
            )

    else:

        def pack_at(block):
            return jnp.concatenate([*qkv_shard[block], out_weight[block].T], axis=1)

        def pack_ff(block, after=()):
            return jnp.concatenate([up_weight[block], down_weight[block].T], axis=1)

    def gather(packed):
        return [(lax.all_gather(packed, "frame", axis=0, tiled=True, axis_index_groups=frame_groups()), wide)]

    def scatter(grads):
        return lax.psum_scatter(
            grads, "frame", scatter_dimension=0, tiled=True, axis_index_groups=frame_groups()
        )

    at_zero, ff_zero, at_one = gather(pack_at(0)), gather(pack_ff(0)), gather(pack_at(1))
    ff_one = pack_ff(1)
    weights = [(at_zero, ff_zero), None]
    if ring:
        rows = jnp.concatenate([block_gains[0], block_gains[1], jnp.zeros((4, shard), BF16)]).astype(F32)
        spread = lax.all_to_all(jnp.broadcast_to(rows[None], (frames, 16, shard)), "frame", 0, 0)
        gains_abs = jnp.swapaxes(spread, 0, 1).reshape(16, wide)
    else:
        gains_abs = lax.all_gather(block_gains, "frame", axis=2, tiled=True).astype(F32).reshape(12, wide)
        gains_abs = jnp.concatenate([gains_abs, jnp.zeros((4, wide), F32)])
    heads = lax.dynamic_slice_in_dim(gains_abs, my_row * width, width, 1)
    gains = jnp.concatenate([gains_abs[:, k * LANES : (k + 1) * LANES] for k in lane_order], axis=1)
    h = enter(block_input, False)
    normed = run(
        functools.partial(first_norm_kernel, 0),
        (1,),
        [big, whole(gains.shape)],
        big,
        shaped(half, wide, dtype=BF16),
        [],
        [h, gains],
        1,
    )

    gspec = whole(gains.shape)

    def reduce_rows(other, own):
        near = (own + row_take(other, 1).astype(F32)).astype(BF16)
        return near, row_take(near, 2)

    stored = []
    grad = enter(cotangent, True)
    scaled = run(
        functools.partial(scale_kernel, 9),
        (1,),
        [big, gspec],
        big,
        shaped(half, wide, dtype=BF16),
        [],
        [grad, gains],
        1,
    )
    grad_down = (scaled, row_take(scaled, 1))
    for block in range(2):
        base = 6 * block
        at, ff = weights[block] or (at_one, None)
        normed = (normed, row_take(normed, 1))
        early = [*grad_down, scene_table, rel_lens] if block == 0 else []
        queries, kv, mixed = project(normed, at, heads, base + 4, early)
        if block == 0:
            sources, walking, table, lens = [kv], False, frame_table, frame_lens
        else:
            table, lens, walking = scene_table, rel_lens, ring
            sources = ring_gather(kv, half) if ring else [lax.all_gather(kv, "frame", axis=0, tiled=True)]
            ff = gather(gate(ff_one, [sources[3], sources[6]]) if ring else ff_one)
            weights[1] = (at, ff)
        attended, lse, part_other, part_own = attend(
            queries, sources, walking, at, table, lens, facts, wide
        )
        branch = reduce_rows(part_other, part_own)
        middle, second = run(
            functools.partial(residual_kernel, base + 2, base + 1),
            (2,),
            [part, part, part, gspec],
            [part, part],
            [shaped(half, wide), shaped(half, wide, dtype=BF16)],
            [],
            [h, *branch, gains],
            2,
        )
        second = (second, row_take(second, 1))
        if block == 0:
            up_values, active, part_other, part_own = feed(second, ff, hidden)
        else:
            both = feed_both(second, grad_down, ff[0][0], hidden)
            active, grad_up, part_other, part_own, back_other, back_own = both
            up_values = None
        stored.append(
            (h, normed, queries, mixed, (sources, walking, table, lens), attended, lse, branch)
            + (middle, second, up_values, active)
        )
        if block == 0:
            down_zero = reduce_rows(part_other, part_own)
            h, normed = run(
                functools.partial(residual_kernel, base + 3, base + 6),
                (2,),
                [part, part, part, gspec],
                [part, part],
                [shaped(half, wide), shaped(half, wide, dtype=BF16)],
                [],
                [middle, *down_zero, gains],
                2,
            )

    last_other, last_own = row_take(part_other, 1), part_own
    at_shapes = [(2, 3, shard, width), (2, width, shard)]
    ff_shapes = [(2, shard, hidden), (2, hidden, shard)]
    at_out, ff_out = [], []
    gain_sums = [None, None]
    input_grad = None
    for block in (1, 0):
        base = 6 * block
        at, ff = weights[block]
        h, normed, queries, mixed, keys, attended, lse, branch, middle, second, up_values, active = stored[block]
        sources, walking, table, lens = keys
        if block == 1:
            part_other, part_own = back_other, back_own
        else:
            grad_up, part_other, part_own = feed_back(grad_down, up_values, ff)
        incoming = reduce_rows(part_other, part_own)
        if block == 1:
            up_grads = one_weight_grads(second, grad_up, 5, [incoming[0]])
            ff_grads = one_weight_grads(grad_down, active, 5, [incoming[0]])
            up_sum = scatter(up_grads)
        else:
            ff_grads = weight_grads(second, grad_up, grad_down, active, 3, [incoming[0]])
            ff_grads = gate(ff_grads, [at_sum, incoming[1]])
            ff_sum = scatter(ff_grads)
            if ring:
                ff_out = finish(finish_ff_kernel, [ff_sum], ff_shapes, block, ff_out)
        grad_middle, scaled, sums_middle = run(
            functools.partial(middle_back_kernel, base),
            (2,),
            [part] * 6 + [gspec],
            [part, part, whole((2, wide))],
            [shaped(half, wide), shaped(half, wide, dtype=BF16), shaped(2, wide)],
            [],
            [grad, *incoming, middle, *branch, gains],
            2,
            after=[up_grads, ff_grads] if block == 1 else [ff_grads, *(at_out[:1] if ring else [])],
        )
        grad_branch = (scaled, row_take(scaled, 1))
        if block == 1:
            near = run(
                add_kernel, (1,), [big, big], big, shaped(half, wide, dtype=BF16), [], [last_own, last_other], 1,
                after=[incoming[1]],
            )
            output, sum_three = run(
                functools.partial(output_kernel, base + 3, lane_order),
                (1,),
                [big, big, big, gspec, big],
                [whole((quarter, wide)), whole((1, wide))],
                [shaped(quarter, wide, dtype=BF16), shaped(1, wide)],
                [pltpu.VMEM((half, wide), F32)],
                [facts, middle, near, row_take(near, 2), gains, grad],
                1,
                prefetch=1,
            )
        dq, *dkv_parts = attend_back(
            queries,
            grad_branch,
            attended,
            lse,
            sources,
            walking,
            at,
            table,
            lens,
            facts,
            F32 if block == 0 else BF16,
        )
        if block == 0:
            dkv = dkv_parts[0][0]
        elif ring:
            (own, right, left), sent_last = ring_scatter(dkv_parts)
            dkv = own.astype(F32) + right.astype(F32) + left.astype(F32)
        else:
            spread = jnp.zeros((frames,) + dkv_parts[0].shape[1:], BF16).at[table].set(dkv_parts[0])
            dkv = lax.psum_scatter(spread, "frame", scatter_dimension=0, tiled=False).astype(F32)
        if block == 1:
            down_sum = scatter(gate(ff_grads, [*(sent_last if ring else [dkv]), up_sum]))
            ff_sum = down_sum
            if ring:
                ff_out = finish(finish_two_kernel, [up_sum, down_sum], ff_shapes, 1, ff_out)
        grad_mixed, part_other, part_own, sums_heads, sum_zero = project_back(
            dq, dkv, mixed, at, heads, base + 4, normed, gains, [output] if block == 1 else ()
        )
        gain_sums[block] = (sum_zero, sums_middle, sum_three, sums_heads)
        incoming = reduce_rows(part_other, part_own)
        at_grads = weight_grads(normed, grad_mixed, grad_branch, attended, 4, [incoming[0]])
        at_grads = gate(at_grads, [ff_sum, incoming[1]])
        if block == 1:
            grad, scaled, sum_three = run(
                functools.partial(between_kernel, base),
                (2,),
                [part] * 4 + [gspec, part, part],
                [part, part, whole((1, wide))],
                [shaped(half, wide), shaped(half, wide, dtype=BF16), shaped(1, wide)],
                [],
                [grad_middle, *incoming, h, gains, *down_zero],
                3,
                after=[at_grads],
            )
            grad_down = (scaled, row_take(scaled, 1))
        else:
            input_grad = run(
                functools.partial(last_back_kernel, lane_order),
                (1,),
                [big] * 4 + [gspec],
                whole((quarter, wide)),
                shaped(quarter, wide, dtype=BF16),
                [pltpu.VMEM((half, wide), F32)],
                [facts, grad_middle, *incoming, h, gains],
                2,
                prefetch=1,
                after=[],
            )
        at_sum = scatter(at_grads)
        if ring:
            at_out = finish(finish_at_kernel, [at_sum], at_shapes, block, at_out)
        else:
            ff_parts = [up_sum, down_sum] if block == 1 else [ff_sum[:, :hidden], ff_sum[:, hidden:]]
            ff_out = [(ff_parts[0].astype(F32), ff_parts[1].astype(F32).T)] + ff_out
            at_last = at_sum.astype(F32)
            qkv_sum = jnp.stack([at_last[:, i * width : (i + 1) * width] for i in range(3)])
            at_out = [(qkv_sum, at_last[:, 3 * width :].T)] + at_out
    if not ring:
        ff_out = [jnp.stack(both) for both in zip(*ff_out, strict=True)]
        at_out = [jnp.stack(both) for both in zip(*at_out, strict=True)]

    if ring:
        operands = [*gain_sums[0], *gain_sums[1]]
        sent = run(
            functools.partial(gain_sums_kernel, lane_order),
            (1,),
            [whole(v.shape) for v in operands],
            whole((frames, 16, LANES)),
            shaped(frames, 16, LANES),
            [],
            [facts, *operands],
            1,
            prefetch=1,
            after=[input_grad],
        )
        total = jnp.sum(lax.all_to_all(sent, "frame", 0, 0), axis=0)
        total = total + row_take(total, 1)
        total = total + row_take(total, 2)
        gains_grad = total[:12].reshape(2, 6, LANES)
    else:
        rows = [jnp.concatenate([sums[0], sums[1] * F32(0.5), sums[2] * F32(0.5)]) for sums in gain_sums]
        rows = jnp.stack(rows)
        per_head = lax.dynamic_update_slice_in_dim(
            jnp.zeros((2, 2, wide), F32),
            jnp.stack([gain_sums[0][3], gain_sums[1][3]]),
            my_row * width,
            2,
        )
        total = lax.psum(jnp.concatenate([rows, per_head], axis=1), ("frame", "row"))
        gains_grad = lax.dynamic_slice_in_dim(total, my_frame * shard, shard, 2)
    return (
        output,
        input_grad,
        jnp.transpose(at_out[0], (0, 2, 1, 3)),
        at_out[1],
        ff_out[0],
        ff_out[1],
        gains_grad,
    )


def solution(mesh):
    return jax.shard_map(
        per_device,
        mesh=mesh,
        in_specs=(
            P(("frame", "row"), None),
            P(("frame", "row"), None),
            P(),
            P(),
            P(None, "frame", None, "row"),
            P(None, "row", "frame"),
            P(None, "frame", "row"),
            P(None, "row", "frame"),
            P(None, None, "frame"),
        ),
        out_specs=(
            P(("frame", "row"), None),
            P(("frame", "row"), None),
            P(None, "frame", None, "row"),
            P(None, "row", "frame"),
            P(None, "frame", "row"),
            P(None, "row", "frame"),
            P(None, None, "frame"),
        ),
        check_vma=False,
    )
```

```python
import functools

import jax
import jax.numpy as jnp
from jax import lax
from jax.experimental import pallas as pl
from jax.experimental.pallas import tpu as pltpu
from jax.sharding import PartitionSpec as P

HEAD_DIM = 64
EPSILON = 1e-06
F32 = jnp.float32
BF16 = jnp.bfloat16
LANES = 128
TILE = 256
ROOT_HALF = 0.7071067811865476
BELL = 0.3989422804014327
SCALING = HEAD_DIM**-0.5

RING = (0, 2, 4, 6, 7, 5, 3, 1)


def on_ring():
    return lax.axis_size("frame") == len(RING)


def frame_groups():
    return [list(RING)] if on_ring() else None


def frame_order(frames):
    return RING if on_ring() else tuple(range(frames))


def ring_take(value, step):
    count = len(RING)
    return lax.ppermute(value, "frame", [(RING[(i + step) % count], RING[i]) for i in range(count)])


def row_take(value, bit):
    return lax.ppermute(value, "row", [(i ^ bit, i) for i in range(4)])


def ring_gather(shard, cut):
    ahead, behind = [shard], [shard]
    for _ in range(3):
        ahead.append(ring_take(ahead[-1], 1))
        behind.append(ring_take(behind[-1], -1))
    far_low = ring_take(ahead[3][:cut], 1)
    far_high = ring_take(behind[3][cut:], -1)
    return ahead + [far_low, far_high] + behind[3:0:-1]


def add_pair(a, b):
    return (a.astype(F32) + b.astype(F32)).astype(BF16)


def ring_scatter(pieces):
    ahead = pieces[1:4]
    far_low, far_high = pieces[4:6]
    behind = pieces[8:5:-1]
    cut = far_low.shape[0]
    low = ring_take(far_low, -1)
    high = ring_take(far_high, 1)
    right = jnp.concatenate([add_pair(ahead[2][:cut], low), ahead[2][cut:]])
    left = jnp.concatenate([behind[2][:cut], add_pair(behind[2][cut:], high)])
    for place in (1, 0):
        right = add_pair(ahead[place], ring_take(right, -1))
        left = add_pair(behind[place], ring_take(left, 1))
    return (pieces[0], ring_take(right, -1), ring_take(left, 1)), [right, left]


def dot_nt(a, b):
    return lax.dot_general(a, b, (((1,), (1,)), ((), ())), preferred_element_type=F32)


def dot_nn(a, b):
    return lax.dot_general(a, b, (((1,), (0,)), ((), ())), preferred_element_type=F32)


def whole(shape):
    return pl.BlockSpec(shape, lambda *_: (0,) * len(shape))


def column(rows, place):
    return pl.BlockSpec((rows, TILE), lambda j, *_: (0, place(j)))


WEIGH = 3.0


def cost(us):
    return pl.CostEstimate(
        flops=int(us * WEIGH * 1.0e9), bytes_accessed=int(us * WEIGH * 2.0e6), transcendentals=0
    )


def run(kernel, grid, in_specs, out_specs, out_shape, scratch, operands, us, prefetch=0, aliases=None, after=()):
    count = len(operands)

    def body(*refs):
        kernel(*refs[:count], *refs[count + len(after) :])

    in_specs = list(in_specs) + [pl.BlockSpec(memory_space=pl.ANY)] * len(after)
    operands = [*operands, *after]
    return pl.pallas_call(
        body,
        grid_spec=pltpu.PrefetchScalarGridSpec(
            num_scalar_prefetch=prefetch,
            grid=grid,
            in_specs=in_specs,
            out_specs=out_specs,
            scratch_shapes=scratch,
        ),
        out_shape=out_shape,
        input_output_aliases=aliases or {},
        compiler_params=pltpu.CompilerParams(vmem_limit_bytes=56 * 1024 * 1024),
        cost_estimate=cost(us),
    )(*operands)


def shaped(*shape, dtype=F32):
    return jax.ShapeDtypeStruct(shape, dtype)


def norm_parts(values):
    center = values - jnp.mean(values, axis=-1, keepdims=True)
    scale = lax.rsqrt(jnp.mean(center * center, axis=-1, keepdims=True) + EPSILON)
    return center * scale, scale


def norm_back(unit, scale, gain, grad):
    inner = grad * gain
    return scale * (
        inner
        - jnp.mean(inner, axis=-1, keepdims=True)
        - unit * jnp.mean(inner * unit, axis=-1, keepdims=True)
    )


def head_means(values):
    width = values.shape[-1]
    rows = lax.broadcasted_iota(jnp.int32, (width, width), 0) // HEAD_DIM
    cols = lax.broadcasted_iota(jnp.int32, (width, width), 1) // HEAD_DIM
    spread = jnp.where(rows == cols, F32(1.0 / HEAD_DIM), F32(0)).astype(BF16)
    high = values.astype(BF16)
    low = (values - high.astype(F32)).astype(BF16)
    return dot_nn(high, spread) + dot_nn(low, spread)


def head_parts(values):
    center = values - head_means(values)
    scale = lax.rsqrt(head_means(center * center) + EPSILON)
    return center * scale, scale


def head_back(unit, scale, gain, grad):
    inner = grad * gain
    return scale * (inner - head_means(inner) - unit * head_means(inner * unit))


def joined(refs):
    if len(refs) == 1:
        return refs[0][...]
    return jnp.concatenate([ref[...] for ref in refs], axis=0)


def head_mask(shape, head):
    lanes = lax.broadcasted_iota(jnp.int32, shape, 1)
    return (lanes // HEAD_DIM) == head


def live_keys(count, core, length):
    place = lax.broadcasted_iota(jnp.int32, (count, 1), 0)
    quarter = count // 4
    half = place // (2 * quarter)
    chip = (place // quarter) % 2
    slot = (chip * 2 + (half ^ core)) * quarter + place % quarter
    return slot < length


def pack_at_kernel(qkv_ref, out_ref, at_ref):
    rows = out_ref.shape[2]
    width = qkv_ref.shape[3]
    for i in range(3):
        at_ref[:rows, i * width : (i + 1) * width] = qkv_ref[0, i]
    at_ref[:rows, 3 * width :] = out_ref[0].T


def pack_ff_kernel(up_ref, down_ref, ff_ref):
    ff = up_ref.shape[2]
    ff_ref[:, :ff] = up_ref[0]
    ff_ref[:, ff:] = down_ref[0].T


def gain_sums_kernel(order, facts_ref, *refs):
    out_ref = refs[-1]
    out_ref[...] = jnp.zeros_like(out_ref)
    row = facts_ref[0] * 2 + facts_ref[1]
    for block in range(2):
        zero, middle, three, heads = refs[4 * block : 4 * block + 4]
        base = 6 * block
        for k in range(out_ref.shape[0]):
            lanes = slice(k * LANES, (k + 1) * LANES)
            place = order[k]
            out_ref[place, base : base + 1, :] = zero[:, lanes]
            out_ref[place, base + 1 : base + 3, :] = middle[:, lanes] * 0.5
            out_ref[place, base + 3 : base + 4, :] = three[:, lanes] * 0.5
        for k in range(2):
            lanes = slice(k * LANES, (k + 1) * LANES)
            out_ref[row * 2 + k, base + 4 : base + 6, :] = heads[:, lanes]


def enter_kernel(masked, order, facts_ref, own_ref, far_ref, out_ref):
    rows = own_ref.shape[0]
    chip, core, length = facts_ref[0], facts_ref[1], facts_ref[2]
    for k in range(len(order)):
        lanes = slice(order[k] * LANES, (order[k] + 1) * LANES)
        for source, place in ((own_ref, chip), (far_ref, 1 - chip)):
            values = source[:, lanes].astype(F32)
            if masked:
                slots = (place * 2 + core) * rows + lax.broadcasted_iota(jnp.int32, (rows, 1), 0)
                values = jnp.where(slots < length, values, 0.0)
            start = pl.multiple_of(place * rows, rows)
            out_ref[pl.ds(start, rows), k * LANES : (k + 1) * LANES] = values


def leave(values_ref, order, facts_ref, out_ref):
    rows = out_ref.shape[0]
    start = pl.multiple_of(facts_ref[0] * rows, rows)
    for k in range(len(order)):
        lanes = slice(order[k] * LANES, (order[k] + 1) * LANES)
        values = values_ref[pl.ds(start, rows), k * LANES : (k + 1) * LANES]
        out_ref[:, lanes] = values.astype(out_ref.dtype)


def first_norm_kernel(row, h_ref, gains_ref, normed_ref):
    unit, _ = norm_parts(h_ref[...])
    normed_ref[...] = (unit * gains_ref[row : row + 1, :]).astype(BF16)


def accumulate(ref, make):
    @pl.when(pl.program_id(0) == 0)
    def _():
        ref[...] = make()

    @pl.when(pl.program_id(0) > 0)
    def _():
        ref[...] += make()


def add_up(ref, value):
    ref[...] = jnp.where(pl.program_id(0) == 0, value, ref[...] + value)


def total_of(own_ref, far_ref):
    return own_ref[...].astype(F32) + far_ref[...].astype(F32)


def residual_kernel(scale_row, norm_row, h_ref, own_ref, far_ref, gains_ref, next_ref, normed_ref):
    value = h_ref[...] + gains_ref[scale_row : scale_row + 1, :] * total_of(own_ref, far_ref)
    next_ref[...] = value
    unit, _ = norm_parts(value)
    normed_ref[...] = (unit * gains_ref[norm_row : norm_row + 1, :]).astype(BF16)


def add_kernel(own_ref, other_ref, sum_ref):
    sum_ref[...] = (own_ref[...] + other_ref[...].astype(F32)).astype(BF16)


def output_kernel(scale_row, order, facts_ref, h_ref, own_ref, far_ref, gains_ref, grad_ref, out_ref, sums_ref, held):
    total = total_of(own_ref, far_ref)
    held[...] = h_ref[...] + gains_ref[scale_row : scale_row + 1, :] * total
    sums_ref[...] = jnp.sum(grad_ref[...] * total, axis=0, keepdims=True)
    leave(held, order, facts_ref, out_ref)


def scale_kernel(row, grad_ref, gains_ref, scaled_ref):
    scaled_ref[...] = (grad_ref[...] * gains_ref[row : row + 1, :]).astype(BF16)


def middle_back_kernel(
    base, grad_ref, own_ref, far_ref, middle_ref, b_own_ref, b_far_ref, gains_ref, next_ref, scaled_ref, sums_ref
):
    grad_in = total_of(own_ref, far_ref)
    unit, scale = norm_parts(middle_ref[...])
    first = jnp.sum(grad_in * unit, axis=0, keepdims=True)
    grad = grad_ref[...] + norm_back(unit, scale, gains_ref[base + 1 : base + 2, :], grad_in)
    next_ref[...] = grad
    second = jnp.sum(grad * total_of(b_own_ref, b_far_ref), axis=0, keepdims=True)
    add_up(sums_ref, jnp.concatenate([first, second], axis=0))
    scaled_ref[...] = (grad * gains_ref[base + 2 : base + 3, :]).astype(BF16)


def first_back(base, grad_ref, own_ref, far_ref, h_ref, gains_ref):
    unit, scale = norm_parts(h_ref[...])
    return grad_ref[...] + norm_back(unit, scale, gains_ref[base : base + 1, :], total_of(own_ref, far_ref))


def between_kernel(
    base, grad_ref, own_ref, far_ref, h_ref, gains_ref, d_own_ref, d_far_ref, next_ref, scaled_ref, sums_ref
):
    grad = first_back(base, grad_ref, own_ref, far_ref, h_ref, gains_ref)
    next_ref[...] = grad
    scaled_ref[...] = (grad * gains_ref[base - 3 : base - 2, :]).astype(BF16)
    add_up(sums_ref, jnp.sum(grad * total_of(d_own_ref, d_far_ref), axis=0, keepdims=True))


def last_back_kernel(order, facts_ref, grad_ref, own_ref, far_ref, h_ref, gains_ref, out_ref, held):
    held[...] = first_back(0, grad_ref, own_ref, far_ref, h_ref, gains_ref)
    leave(held, order, facts_ref, out_ref)


def project_kernel(row_q, count, own_ref, other_ref, *refs):
    pieces = refs[:count]
    heads_ref, q_ref, kv_ref, mixed_ref = refs[count:]
    step = pl.program_id(0)
    weight = joined(pieces)
    half = own_ref.shape[0]
    mixed = jnp.concatenate([dot_nn(own_ref[...], weight), dot_nn(other_ref[...], weight)], axis=0)

    @pl.when(step < 2)
    def _():
        mixed_ref[...] = mixed
        unit, _ = head_parts(mixed)
        gain = jnp.where(step == 0, heads_ref[row_q : row_q + 1, :], heads_ref[row_q + 1 : row_q + 2, :])
        scaled = (unit * gain).astype(BF16)

        @pl.when(step == 0)
        def _():
            q_ref[...] = scaled

        @pl.when(step == 1)
        def _():
            kv_ref[...] = scaled

    @pl.when(step == 2)
    def _():
        kv_ref[...] = mixed.astype(BF16)


def project(normed, pieces, heads, row_q, after):
    own, other = normed
    half, wide = own.shape
    width = heads.shape[1]
    rows = [min(p.shape[0], limit) for p, limit in pieces]
    return run(
        functools.partial(project_kernel, row_q, len(pieces)),
        (3,),
        [whole(own.shape), whole(other.shape)]
        + [column(r, lambda j: j) for r in rows]
        + [whole(heads.shape)],
        [
            whole((2 * half, width)),
            column(2 * half, lambda j: jnp.maximum(j - 1, 0)),
            column(2 * half, lambda j: jnp.minimum(j, 1)),
        ],
        [
            shaped(2 * half, width, dtype=BF16),
            shaped(2 * half, 2 * width, dtype=BF16),
            shaped(2 * half, 2 * width),
        ],
        [],
        [own, other] + [p for p, _ in pieces] + [heads],
        5,
        after=after,
    )


def project_back_kernel(row_q, count, dq_ref, dkv_ref, mixed_ref, heads_ref, n_own_ref, n_other_ref, gains_ref, *refs):
    pieces = refs[:count]
    grad_ref, other_ref, own_ref, sums_ref, zero_ref, acc = refs[count:]
    step = pl.program_id(0)

    def normed(incoming, row, place):
        unit, scale = head_parts(mixed_ref[...])
        sums_ref[place : place + 1, :] = jnp.sum(incoming * unit, axis=0, keepdims=True)
        grad_ref[...] = head_back(unit, scale, heads_ref[row : row + 1, :], incoming).astype(BF16)

    @pl.when(step == 0)
    def _():
        normed(dq_ref[...], row_q, 0)

    @pl.when(step == 1)
    def _():
        normed(dkv_ref[...].astype(F32), row_q + 1, 1)

    @pl.when(step == 2)
    def _():
        grad_ref[...] = dkv_ref[...].astype(BF16)

    accumulate(acc, lambda: dot_nt(grad_ref[...], joined(pieces)))

    @pl.when(step == 2)
    def _():
        half = own_ref.shape[0]
        own_ref[...] = acc[:half, :]
        other_ref[...] = acc[half:, :].astype(BF16)
        products = acc[:half, :] * n_own_ref[...].astype(F32) + acc[half:, :] * n_other_ref[...].astype(F32)
        row_g = row_q - 4
        zero_ref[...] = jnp.sum(products, axis=0, keepdims=True) / gains_ref[row_g : row_g + 1, :]


def project_back(dq, dkv, mixed, pieces, heads, row_q, normed, gains, after):
    full, width = dq.shape
    wide = gains.shape[1]
    rows = [min(p.shape[0], limit) for p, limit in pieces]
    return run(
        functools.partial(project_back_kernel, row_q, len(pieces)),
        (3,),
        [
            whole(dq.shape),
            column(full, lambda j: jnp.maximum(j - 1, 0)),
            column(full, lambda j: jnp.minimum(j, 1)),
            whole(heads.shape),
            whole((full // 2, wide)),
            whole((full // 2, wide)),
            whole(gains.shape),
        ]
        + [column(r, lambda j: j) for r in rows],
        [
            column(full, lambda j: j),
            whole((full // 2, wide)),
            whole((full // 2, wide)),
            whole((2, width)),
            whole((1, wide)),
        ],
        [
            shaped(full, 3 * width, dtype=BF16),
            shaped(full // 2, wide, dtype=BF16),
            shaped(full // 2, wide),
            shaped(2, width),
            shaped(1, wide),
        ],
        [pltpu.VMEM((full, wide), F32)],
        [dq, dkv, mixed, heads, *normed, gains] + [p for p, _ in pieces],
        6,
        after=after,
    )


def feed_kernel(count, own_ref, other_ref, *refs):
    ups, downs = refs[:count], refs[count : 2 * count]
    values_ref, active_ref, part_other_ref, part_own_ref, acc = refs[2 * count :]
    step = pl.program_id(0)

    weight = joined(ups)
    half = own_ref.shape[0]
    for source, start in ((own_ref, 0), (other_ref, half)):
        values = dot_nn(source[...], weight)
        values_ref[start : start + half, :] = values
        active_ref[start : start + half, :] = (
            0.5 * values * (1.0 + lax.erf(values * F32(ROOT_HALF)))
        ).astype(BF16)
    accumulate(acc, lambda: dot_nt(active_ref[...], joined(downs)))

    @pl.when(step == pl.num_programs(0) - 1)
    def _():
        part_own_ref[...] = acc[:half, :]
        part_other_ref[...] = acc[half:, :].astype(BF16)


def feed(second, pieces, hidden):
    own, other = second
    half, wide = own.shape
    steps = hidden // TILE
    rows = [min(p.shape[0], limit) for p, limit in pieces]
    arrays = [p for p, _ in pieces]
    return run(
        functools.partial(feed_kernel, len(pieces)),
        (steps,),
        [whole(own.shape), whole(other.shape)]
        + [column(r, lambda j: j) for r in rows]
        + [column(r, lambda j: j + steps) for r in rows],
        [
            column(2 * half, lambda j: j),
            column(2 * half, lambda j: j),
            whole((half, wide)),
            whole((half, wide)),
        ],
        [
            shaped(2 * half, hidden),
            shaped(2 * half, hidden, dtype=BF16),
            shaped(half, wide, dtype=BF16),
            shaped(half, wide),
        ],
        [pltpu.VMEM((2 * half, wide), F32)],
        [own, other] + arrays + arrays,
        7,
    )


def feed_back_kernel(count, own_ref, other_ref, values_ref, *refs):
    ups, downs = refs[:count], refs[count : 2 * count]
    grad_ref, part_other_ref, part_own_ref, acc = refs[2 * count :]
    step = pl.program_id(0)

    weight = joined(downs)
    half = own_ref.shape[0]
    for source, start in ((own_ref, 0), (other_ref, half)):
        incoming = dot_nn(source[...], weight)
        values = values_ref[start : start + half, :]
        slope = 0.5 * (1.0 + lax.erf(values * F32(ROOT_HALF))) + values * (
            jnp.exp(-0.5 * values * values) * F32(BELL)
        )
        grad_ref[start : start + half, :] = (incoming * slope).astype(BF16)
    accumulate(acc, lambda: dot_nt(grad_ref[...], joined(ups)))

    @pl.when(step == pl.num_programs(0) - 1)
    def _():
        part_own_ref[...] = acc[:half, :]
        part_other_ref[...] = acc[half:, :].astype(BF16)


def feed_back(grads, values, pieces):
    own, other = grads
    half, wide = own.shape
    hidden = values.shape[1]
    steps = hidden // TILE
    rows = [min(p.shape[0], limit) for p, limit in pieces]
    arrays = [p for p, _ in pieces]
    return run(
        functools.partial(feed_back_kernel, len(pieces)),
        (steps,),
        [whole(own.shape), whole(other.shape), column(2 * half, lambda j: j)]
        + [column(r, lambda j: j) for r in rows]
        + [column(r, lambda j: j + steps) for r in rows],
        [column(2 * half, lambda j: j), whole((half, wide)), whole((half, wide))],
        [
            shaped(2 * half, hidden, dtype=BF16),
            shaped(half, wide, dtype=BF16),
            shaped(half, wide),
        ],
        [pltpu.VMEM((2 * half, wide), F32)],
        [own, other, values] + arrays + arrays,
        3,
    )


def feed_both_kernel(own_ref, other_ref, g_own_ref, g_other_ref, up_ref, down_ref, *refs):
    active_ref, grad_ref, part_other_ref, part_own_ref, back_other_ref, back_own_ref, acc, back = refs
    step = pl.program_id(0)

    up, down = up_ref[...], down_ref[...]
    half = own_ref.shape[0]
    for source, g_source, start in ((own_ref, g_own_ref, 0), (other_ref, g_other_ref, half)):
        values = dot_nn(source[...], up)
        gate_part = 0.5 * (1.0 + lax.erf(values * F32(ROOT_HALF)))
        active_ref[start : start + half, :] = (values * gate_part).astype(BF16)
        slope = gate_part + values * (jnp.exp(-0.5 * values * values) * F32(BELL))
        grad_ref[start : start + half, :] = (dot_nn(g_source[...], down) * slope).astype(BF16)
    accumulate(acc, lambda: dot_nt(active_ref[...], down))
    accumulate(back, lambda: dot_nt(grad_ref[...], up))

    @pl.when(step == pl.num_programs(0) - 1)
    def _():
        part_own_ref[...] = acc[:half, :]
        part_other_ref[...] = acc[half:, :].astype(BF16)
        back_own_ref[...] = back[:half, :]
        back_other_ref[...] = back[half:, :].astype(BF16)


def feed_both(second, grads, weight, hidden):
    half, wide = second[0].shape
    steps = hidden // TILE
    return run(
        feed_both_kernel,
        (steps,),
        [whole((half, wide))] * 4 + [column(wide, lambda j: j), column(wide, lambda j: j + steps)],
        [column(2 * half, lambda j: j)] * 2 + [whole((half, wide))] * 4,
        [shaped(2 * half, hidden, dtype=BF16)] * 2 + [shaped(half, wide, dtype=BF16), shaped(half, wide)] * 2,
        [pltpu.VMEM((2 * half, wide), F32)] * 2,
        [*second, *grads, weight, weight],
        10,
    )


def weight_kernel(split, a_own, a_other, b_own, b_other, first_ref, second_ref, out_ref, turned):
    step = pl.program_id(0)
    half = a_own.shape[0]

    def turn(own, other):
        turned[:, :half] = own[...].T
        turned[:, half:] = other[...].T

    @pl.when(step == 0)
    def _():
        turn(a_own, a_other)

    @pl.when(step == split)
    def _():
        turn(b_own, b_other)

    @pl.when(step < split)
    def _():
        out_ref[...] = dot_nn(turned[...], first_ref[...]).astype(BF16)

    @pl.when(step >= split)
    def _():
        out_ref[...] = dot_nn(turned[...], second_ref[...]).astype(BF16)


def gate_kernel(*refs):
    pass


def gate(value, after):
    anywhere = pl.BlockSpec(memory_space=pl.ANY)
    return run(
        gate_kernel, (1,), [anywhere], anywhere, jax.ShapeDtypeStruct(value.shape, value.dtype), [], [value], 0.1,
        aliases={0: 0}, after=after,
    )


def one_weight_kernel(own, other, right_ref, out_ref, turned):
    half = own.shape[0]

    @pl.when(pl.program_id(0) == 0)
    def _():
        turned[:, :half] = own[...].T
        turned[:, half:] = other[...].T

    out_ref[...] = dot_nn(turned[...], right_ref[...]).astype(BF16)


def one_weight_grads(a, right, us, after):
    half, wide = a[0].shape
    return run(
        one_weight_kernel,
        (right.shape[1] // TILE,),
        [whole((half, wide))] * 2 + [column(2 * half, lambda j: j)],
        column(wide, lambda j: j),
        shaped(wide, right.shape[1], dtype=BF16),
        [pltpu.VMEM((wide, 2 * half), BF16)],
        [*a, right],
        us,
        after=after,
    )


def weight_grads(a, first, b, second, us, after):
    half, wide = a[0].shape
    split = first.shape[1] // TILE
    steps = split + second.shape[1] // TILE
    return run(
        functools.partial(weight_kernel, split),
        (steps,),
        [whole((half, wide))] * 4
        + [
            column(2 * half, lambda j: jnp.minimum(j, split - 1)),
            column(2 * half, lambda j: jnp.maximum(j - split, 0)),
        ],
        column(wide, lambda j: j),
        shaped(wide, steps * TILE, dtype=BF16),
        [pltpu.VMEM((wide, 2 * half), BF16)],
        [*a, *b, first, second],
        us,
        after=after,
    )


def finish_ff_kernel(part_ref, *refs):
    up_ref, down_ref = refs[-2:]
    hidden = up_ref.shape[2]
    up_ref[0] = part_ref[:, :hidden].astype(F32)
    down_ref[0] = part_ref[:, hidden:].astype(F32).T


def finish_two_kernel(up_part_ref, down_part_ref, up_ref, down_ref):
    up_ref[0] = up_part_ref[...].astype(F32)
    down_ref[0] = down_part_ref[...].astype(F32).T


def finish_at_kernel(part_ref, *refs):
    qkv_ref, out_ref = refs[-2:]
    width = qkv_ref.shape[3]
    for i in range(3):
        qkv_ref[0, i] = part_ref[:, i * width : (i + 1) * width].astype(F32)
    out_ref[0] = part_ref[:, 3 * width :].astype(F32).T


def finish(kernel, parts, shapes, block, earlier):
    specs = [
        pl.BlockSpec((1,) + s[1:], functools.partial(lambda b, r, *_: (b,) + (0,) * (r - 1), block, len(s)))
        for s in shapes
    ]
    return run(
        kernel,
        (1,),
        [whole(part.shape) for part in parts] + [pl.BlockSpec(memory_space=pl.ANY)] * len(earlier),
        specs,
        [shaped(*s) for s in shapes],
        [],
        [*parts, *earlier],
        2,
        aliases={len(parts) + i: i for i in range(len(earlier))},
    )


def fetch_start(table_ref, sources, ring, buffer, sems, count):
    flen = buffer.shape[1]
    for j in range(count):
        if not ring:
            start = pl.multiple_of(table_ref[j] * flen, flen)
            pltpu.make_async_copy(sources[0].at[pl.ds(start, flen)], buffer.at[j], sems.at[j]).start()
            continue
        for k in range(8):

            @pl.when(table_ref[j] == k)
            def _(j=j, k=k):
                if k == 4:
                    cut = sources[4].shape[0]
                    pltpu.make_async_copy(sources[4], buffer.at[j, pl.ds(0, cut)], sems.at[j]).start()
                    pltpu.make_async_copy(
                        sources[5], buffer.at[j, pl.ds(cut, flen - cut)], sems.at[j]
                    ).start()
                else:
                    source = sources[k if k < 4 else k + 1]
                    pltpu.make_async_copy(source, buffer.at[j], sems.at[j]).start()


def fetch_wait(sources, buffer, sems, j):
    pltpu.make_async_copy(buffer.at[j], buffer.at[j], sems.at[j]).wait()


def attend_kernel(ring, n_kv, count, table_ref, lens_ref, facts_ref, q_ref, *refs):
    sources, pieces = refs[:n_kv], refs[n_kv : n_kv + count]
    out_ref, lse_ref, part_other_ref, part_own_ref = refs[n_kv + count : n_kv + count + 4]
    acc, sums, stack, buffer, sems = refs[n_kv + count + 4 :]
    step = pl.program_id(0)
    steps = buffer.shape[0]
    rows, width = q_ref.shape
    heads = width // HEAD_DIM

    @pl.when(step == 0)
    def _():
        fetch_start(table_ref, sources, ring, buffer, sems, steps)
        acc[...] = jnp.zeros_like(acc)
        sums[...] = jnp.zeros_like(sums)
        for head in range(heads):
            mine = jnp.where(head_mask((rows, width), head), q_ref[...], 0) * BF16(SCALING)
            stack[head * rows : (head + 1) * rows, :] = mine

    fetch_wait(sources, buffer, sems, step)
    live = live_keys(buffer.shape[1], facts_ref[1], lens_ref[table_ref[step]])
    values_t = buffer[step, :, width:].T
    powers = jnp.where(live, jnp.exp(dot_nt(buffer[step, :, :width], stack[...])), 0.0)
    sums[0:1, :] += jnp.sum(powers, axis=0, keepdims=True)
    low = powers.astype(BF16)
    for head in range(heads):
        lanes = slice(head * HEAD_DIM, (head + 1) * HEAD_DIM)
        acc[lanes, :] += dot_nn(values_t[lanes, :], low[:, head * rows : (head + 1) * rows])

    @pl.when(step == steps - 1)
    def _():
        lse_ref[...] = jnp.zeros_like(lse_ref)
        for head in range(heads):
            lanes = slice(head * HEAD_DIM, (head + 1) * HEAD_DIM)
            total = sums[0:1, head * rows : (head + 1) * rows]
            lse_ref[head : head + 1, :] = jnp.log(total)
            acc[lanes, :] = acc[lanes, :] / total
        out_ref[...] = acc[...].T.astype(BF16)
        weight = joined(pieces)
        half = rows // 2
        part_other_ref[...] = dot_nt(out_ref[half:, :], weight).astype(BF16)
        part_own_ref[...] = dot_nt(out_ref[:half, :], weight)


def attend(queries, sources, ring, pieces, table, lens, facts, wide):
    rows, width = queries.shape
    steps = table.shape[0]
    counts = [min(p.shape[0], limit) for p, limit in pieces]
    return run(
        functools.partial(attend_kernel, ring, len(sources), len(pieces)),
        (steps,),
        [whole(queries.shape)]
        + [pl.BlockSpec(memory_space=pl.ANY)] * len(sources)
        + [column(r, lambda j: 3) for r in counts],
        [whole((rows, width)), whole((8, rows)), whole((rows // 2, wide)), whole((rows // 2, wide))],
        [
            shaped(rows, width, dtype=BF16),
            shaped(8, rows),
            shaped(rows // 2, wide, dtype=BF16),
            shaped(rows // 2, wide),
        ],
        [
            pltpu.VMEM((width, rows), F32),
            pltpu.VMEM((8, rows * width // HEAD_DIM), F32),
            pltpu.VMEM((rows * width // HEAD_DIM, width), BF16),
            pltpu.VMEM((steps, rows, 2 * width), BF16),
            pltpu.SemaphoreType.DMA((steps,)),
        ],
        [table, lens, facts, queries, *sources] + [p for p, _ in pieces],
        3 + 2 * steps,
        prefetch=3,
    )


def attend_back_kernel(ring, n_kv, count, n_out, table_ref, lens_ref, facts_ref, *refs):
    q_ref, o_ref, lse_ref, g_own_ref, g_other_ref = refs[:5]
    refs = refs[5:]
    sources, pieces = refs[:n_kv], refs[n_kv : n_kv + count]
    dq_ref = refs[n_kv + count]
    outs = refs[n_kv + count + 1 : n_kv + count + 1 + n_out]
    acc, lines, stack_q, stack_g, buffer, sems = refs[n_kv + count + 1 + n_out :]
    step = pl.program_id(0)
    steps = buffer.shape[0]
    rows, width = q_ref.shape
    heads = width // HEAD_DIM

    @pl.when(step == 0)
    def _():
        fetch_start(table_ref, sources, ring, buffer, sems, steps)
        acc[...] = jnp.zeros_like(acc)
        if ring:
            for out in outs:
                out[...] = jnp.zeros_like(out)
        weight = joined(pieces)
        grads = jnp.concatenate([dot_nn(ref[...], weight).astype(BF16) for ref in (g_own_ref, g_other_ref)], axis=0)
        turned = (grads.astype(F32) * o_ref[...].astype(F32)).T
        for head in range(heads):
            lanes = slice(head * HEAD_DIM, (head + 1) * HEAD_DIM)
            columns = slice(head * rows, (head + 1) * rows)
            lines[0:1, columns] = lse_ref[head : head + 1, :]
            lines[1:2, columns] = jnp.sum(turned[lanes, :], axis=0, keepdims=True)
            inside = head_mask((rows, width), head)
            stack_q[columns, :] = jnp.where(inside, q_ref[...], 0) * BF16(SCALING)
            stack_g[columns, :] = jnp.where(inside, grads, 0)

    fetch_wait(sources, buffer, sems, step)
    live = live_keys(buffer.shape[1], facts_ref[1], lens_ref[table_ref[step]])
    keys = buffer[step, :, :width]
    keys_t = keys.T
    scores = dot_nt(keys, stack_q[...])
    full = jnp.where(live, jnp.exp(scores - lines[0:1, :]), 0.0)
    grad_probs = dot_nt(buffer[step, :, width:], stack_g[...])
    steep = (full * (grad_probs - lines[1:2, :])).astype(BF16)
    grad_v = dot_nn(full.astype(BF16), stack_g[...])
    grad_k = dot_nn(steep, stack_q[...])
    for head in range(heads):
        lanes = slice(head * HEAD_DIM, (head + 1) * HEAD_DIM)
        acc[lanes, :] += dot_nn(keys_t[lanes, :], steep[:, head * rows : (head + 1) * rows])

    if not ring:
        outs[0][0, :, :width] = grad_k.astype(outs[0].dtype)
        outs[0][0, :, width:] = grad_v.astype(outs[0].dtype)
    else:
        for k in range(8):

            @pl.when(table_ref[step] == k)
            def _(k=k):
                if k == 4:
                    cut = outs[4].shape[0]
                    outs[4][:, :width] = grad_k[:cut].astype(BF16)
                    outs[4][:, width:] = grad_v[:cut].astype(BF16)
                    outs[5][:, :width] = grad_k[cut:].astype(BF16)
                    outs[5][:, width:] = grad_v[cut:].astype(BF16)
                else:
                    out = outs[k if k < 4 else k + 1]
                    out[:, :width] = grad_k.astype(BF16)
                    out[:, width:] = grad_v.astype(BF16)

    @pl.when(step == steps - 1)
    def _():
        dq_ref[...] = acc[...].T * F32(SCALING)


def attend_back(queries, grads, attended, lse, sources, ring, pieces, table, lens, facts, dtype):
    rows, width = queries.shape
    steps = table.shape[0]
    counts = [min(p.shape[0], limit) for p, limit in pieces]
    wide = grads[0].shape[1]
    if ring:
        out_specs = [whole(s.shape) for s in sources]
        out_shape = [shaped(*s.shape, dtype=BF16) for s in sources]
    else:
        out_specs = [pl.BlockSpec((1, rows, 2 * width), lambda j, *_: (j, 0, 0))]
        out_shape = [shaped(steps, rows, 2 * width, dtype=dtype)]
    return run(
        functools.partial(attend_back_kernel, ring, len(sources), len(pieces), len(out_specs)),
        (steps,),
        [
            whole((rows, width)),
            whole((rows, width)),
            whole((8, rows)),
            whole((rows // 2, wide)),
            whole((rows // 2, wide)),
        ]
        + [pl.BlockSpec(memory_space=pl.ANY)] * len(sources)
        + [column(r, lambda j: 3) for r in counts],
        [whole((rows, width))] + out_specs,
        [shaped(rows, width)] + out_shape,
        [
            pltpu.VMEM((width, rows), F32),
            pltpu.VMEM((8, rows * width // HEAD_DIM), F32),
            pltpu.VMEM((rows * width // HEAD_DIM, width), BF16),
            pltpu.VMEM((rows * width // HEAD_DIM, width), BF16),
            pltpu.VMEM((steps, rows, 2 * width), BF16),
            pltpu.SemaphoreType.DMA((steps,)),
        ],
        [table, lens, facts, queries, attended, lse, *grads, *sources] + [p for p, _ in pieces],
        1 + 0.5 * steps,
        prefetch=3,
    )


def per_device(
    block_input,
    cotangent,
    frame_lengths,
    frame_scenes,
    qkv_weight,
    out_weight,
    up_weight,
    down_weight,
    block_gains,
):
    quarter, wide = block_input.shape
    frames = lax.axis_size("frame")
    ring = on_ring()
    my_frame = lax.axis_index("frame")
    my_row = lax.axis_index("row")
    chip, core = my_row // 2, my_row % 2
    width = qkv_weight.shape[3]
    hidden = up_weight.shape[2]
    shard = wide // frames
    half = 2 * quarter
    facts = jnp.stack([chip, core, frame_lengths[my_frame]]).astype(jnp.int32)

    if ring:
        walk = jnp.array(RING, jnp.int32)
        at = jnp.argmax(walk == my_frame).astype(jnp.int32)
        order = lax.dynamic_slice_in_dim(jnp.concatenate([walk, walk]), at, frames)
        lane_order = RING
    else:
        order = jnp.arange(frames, dtype=jnp.int32)
        lane_order = tuple(range(wide // LANES))
    rel_lens = frame_lengths[order]
    other_scene = (frame_scenes[order] != frame_scenes[my_frame]).astype(jnp.int32)
    scene_table = jnp.argsort(other_scene, stable=True)[: frames // 2].astype(jnp.int32)
    frame_table = jnp.zeros((1,), jnp.int32)
    frame_lens = frame_lengths[my_frame].reshape(1)

    def enter(values, masked):
        return run(
            functools.partial(enter_kernel, masked, lane_order),
            (1,),
            [whole(values.shape)] * 2,
            whole((half, wide)),
            shaped(half, wide),
            [],
            [facts, values, row_take(values, 2)],
            1,
            prefetch=1,
        )

    big = whole((half, wide))
    part = pl.BlockSpec((half // 2, wide), lambda j, *_: (j, 0))

    qkv_shard = jnp.transpose(qkv_weight, (0, 2, 1, 3))
    if ring:
        pick = lambda s, b: pl.BlockSpec((1,) + s[1:], lambda *_: (b,) + (0,) * (len(s) - 1))

        def pack_at(block):
            return run(
                pack_at_kernel,
                (1,),
                [pick(qkv_shard.shape, block), pick(out_weight.shape, block)],
                whole((shard, 4 * width)),
                shaped(shard, 4 * width, dtype=BF16),
                [],
                [qkv_shard, out_weight],
                1,
            )

        def pack_ff(block, after=()):
            return run(
                pack_ff_kernel,
                (1,),
                [pick(up_weight.shape, block), pick(down_weight.shape, block)],
                whole((shard, 2 * hidden)),
                shaped(shard, 2 * hidden, dtype=BF16),
                [],
                [up_weight, down_weight],
                1,
                after=after,
            )

    else:

        def pack_at(block):
            return jnp.concatenate([*qkv_shard[block], out_weight[block].T], axis=1)

        def pack_ff(block, after=()):
            return jnp.concatenate([up_weight[block], down_weight[block].T], axis=1)

    def gather(packed):
        return [(lax.all_gather(packed, "frame", axis=0, tiled=True, axis_index_groups=frame_groups()), wide)]

    def scatter(grads):
        return lax.psum_scatter(
            grads, "frame", scatter_dimension=0, tiled=True, axis_index_groups=frame_groups()
        )

    at_zero, ff_zero, at_one = gather(pack_at(0)), gather(pack_ff(0)), gather(pack_at(1))
    ff_one = pack_ff(1)
    weights = [(at_zero, ff_zero), None]
    if ring:
        rows = jnp.concatenate([block_gains[0], block_gains[1], jnp.zeros((4, shard), BF16)]).astype(F32)
        spread = lax.all_to_all(jnp.broadcast_to(rows[None], (frames, 16, shard)), "frame", 0, 0)
        gains_abs = jnp.swapaxes(spread, 0, 1).reshape(16, wide)
    else:
        gains_abs = lax.all_gather(block_gains, "frame", axis=2, tiled=True).astype(F32).reshape(12, wide)
        gains_abs = jnp.concatenate([gains_abs, jnp.zeros((4, wide), F32)])
    heads = lax.dynamic_slice_in_dim(gains_abs, my_row * width, width, 1)
    gains = jnp.concatenate([gains_abs[:, k * LANES : (k + 1) * LANES] for k in lane_order], axis=1)
    h = enter(block_input, False)
    normed = run(
        functools.partial(first_norm_kernel, 0),
        (1,),
        [big, whole(gains.shape)],
        big,
        shaped(half, wide, dtype=BF16),
        [],
        [h, gains],
        1,
    )

    gspec = whole(gains.shape)

    def reduce_rows(other, own):
        near = (own + row_take(other, 1).astype(F32)).astype(BF16)
        return near, row_take(near, 2)

    stored = []
    grad = enter(cotangent, True)
    scaled = run(
        functools.partial(scale_kernel, 9),
        (1,),
        [big, gspec],
        big,
        shaped(half, wide, dtype=BF16),
        [],
        [grad, gains],
        1,
    )
    grad_down = (scaled, row_take(scaled, 1))
    for block in range(2):
        base = 6 * block
        at, ff = weights[block] or (at_one, None)
        normed = (normed, row_take(normed, 1))
        early = [*grad_down, scene_table, rel_lens] if block == 0 else []
        queries, kv, mixed = project(normed, at, heads, base + 4, early)
        if block == 0:
            sources, walking, table, lens = [kv], False, frame_table, frame_lens
        else:
            table, lens, walking = scene_table, rel_lens, ring
            sources = ring_gather(kv, half) if ring else [lax.all_gather(kv, "frame", axis=0, tiled=True)]
            ff = gather(gate(ff_one, [sources[3], sources[6]]) if ring else ff_one)
            weights[1] = (at, ff)
        attended, lse, part_other, part_own = attend(
            queries, sources, walking, at, table, lens, facts, wide
        )
        branch = reduce_rows(part_other, part_own)
        middle, second = run(
            functools.partial(residual_kernel, base + 2, base + 1),
            (2,),
            [part, part, part, gspec],
            [part, part],
            [shaped(half, wide), shaped(half, wide, dtype=BF16)],
            [],
            [h, *branch, gains],
            2,
        )
        second = (second, row_take(second, 1))
        if block == 0:
            up_values, active, part_other, part_own = feed(second, ff, hidden)
        else:
            both = feed_both(second, grad_down, ff[0][0], hidden)
            active, grad_up, part_other, part_own, back_other, back_own = both
            up_values = None
        stored.append(
            (h, normed, queries, mixed, (sources, walking, table, lens), attended, lse, branch)
            + (middle, second, up_values, active)
        )
        if block == 0:
            down_zero = reduce_rows(part_other, part_own)
            h, normed = run(
                functools.partial(residual_kernel, base + 3, base + 6),
                (2,),
                [part, part, part, gspec],
                [part, part],
                [shaped(half, wide), shaped(half, wide, dtype=BF16)],
                [],
                [middle, *down_zero, gains],
                2,
            )

    last_other, last_own = row_take(part_other, 1), part_own
    at_shapes = [(2, 3, shard, width), (2, width, shard)]
    ff_shapes = [(2, shard, hidden), (2, hidden, shard)]
    at_out, ff_out = [], []
    gain_sums = [None, None]
    input_grad = None
    for block in (1, 0):
        base = 6 * block
        at, ff = weights[block]
        h, normed, queries, mixed, keys, attended, lse, branch, middle, second, up_values, active = stored[block]
        sources, walking, table, lens = keys
        if block == 1:
            part_other, part_own = back_other, back_own
        else:
            grad_up, part_other, part_own = feed_back(grad_down, up_values, ff)
        incoming = reduce_rows(part_other, part_own)
        if block == 1:
            up_grads = one_weight_grads(second, grad_up, 5, [incoming[0]])
            ff_grads = one_weight_grads(grad_down, active, 5, [incoming[0]])
            up_sum = scatter(up_grads)
        else:
            ff_grads = weight_grads(second, grad_up, grad_down, active, 3, [incoming[0]])
            ff_grads = gate(ff_grads, [at_sum, incoming[1]])
            ff_sum = scatter(ff_grads)
            if ring:
                ff_out = finish(finish_ff_kernel, [ff_sum], ff_shapes, block, ff_out)
        grad_middle, scaled, sums_middle = run(
            functools.partial(middle_back_kernel, base),
            (2,),
            [part] * 6 + [gspec],
            [part, part, whole((2, wide))],
            [shaped(half, wide), shaped(half, wide, dtype=BF16), shaped(2, wide)],
            [],
            [grad, *incoming, middle, *branch, gains],
            2,
            after=[up_grads, ff_grads] if block == 1 else [ff_grads, *(at_out[:1] if ring else [])],
        )
        grad_branch = (scaled, row_take(scaled, 1))
        if block == 1:
            near = run(
                add_kernel, (1,), [big, big], big, shaped(half, wide, dtype=BF16), [], [last_own, last_other], 1,
                after=[incoming[1]],
            )
            output, sum_three = run(
                functools.partial(output_kernel, base + 3, lane_order),
                (1,),
                [big, big, big, gspec, big],
                [whole((quarter, wide)), whole((1, wide))],
                [shaped(quarter, wide, dtype=BF16), shaped(1, wide)],
                [pltpu.VMEM((half, wide), F32)],
                [facts, middle, near, row_take(near, 2), gains, grad],
                1,
                prefetch=1,
            )
        dq, *dkv_parts = attend_back(
            queries,
            grad_branch,
            attended,
            lse,
            sources,
            walking,
            at,
            table,
            lens,
            facts,
            F32 if block == 0 else BF16,
        )
        if block == 0:
            dkv = dkv_parts[0][0]
        elif ring:
            (own, right, left), sent_last = ring_scatter(dkv_parts)
            dkv = own.astype(F32) + right.astype(F32) + left.astype(F32)
        else:
            spread = jnp.zeros((frames,) + dkv_parts[0].shape[1:], BF16).at[table].set(dkv_parts[0])
            dkv = lax.psum_scatter(spread, "frame", scatter_dimension=0, tiled=False).astype(F32)
        if block == 1:
            down_sum = scatter(gate(ff_grads, [*(sent_last if ring else [dkv]), up_sum]))
            ff_sum = down_sum
            if ring:
                ff_out = finish(finish_two_kernel, [up_sum, down_sum], ff_shapes, 1, ff_out)
        grad_mixed, part_other, part_own, sums_heads, sum_zero = project_back(
            dq, dkv, mixed, at, heads, base + 4, normed, gains, [output] if block == 1 else ()
        )
        gain_sums[block] = (sum_zero, sums_middle, sum_three, sums_heads)
        incoming = reduce_rows(part_other, part_own)
        at_grads = weight_grads(normed, grad_mixed, grad_branch, attended, 4, [incoming[0]])
        at_grads = gate(at_grads, [ff_sum, incoming[1]])
        if block == 1:
            grad, scaled, sum_three = run(
                functools.partial(between_kernel, base),
                (2,),
                [part] * 4 + [gspec, part, part],
                [part, part, whole((1, wide))],
                [shaped(half, wide), shaped(half, wide, dtype=BF16), shaped(1, wide)],
                [],
                [grad_middle, *incoming, h, gains, *down_zero],
                3,
                after=[at_grads],
            )
            grad_down = (scaled, row_take(scaled, 1))
        else:
            input_grad = run(
                functools.partial(last_back_kernel, lane_order),
                (1,),
                [big] * 4 + [gspec],
                whole((quarter, wide)),
                shaped(quarter, wide, dtype=BF16),
                [pltpu.VMEM((half, wide), F32)],
                [facts, grad_middle, *incoming, h, gains],
                2,
                prefetch=1,
                after=[],
            )
        at_sum = scatter(at_grads)
        if ring:
            at_out = finish(finish_at_kernel, [at_sum], at_shapes, block, at_out)
        else:
            ff_parts = [up_sum, down_sum] if block == 1 else [ff_sum[:, :hidden], ff_sum[:, hidden:]]
            ff_out = [(ff_parts[0].astype(F32), ff_parts[1].astype(F32).T)] + ff_out
            at_last = at_sum.astype(F32)
            qkv_sum = jnp.stack([at_last[:, i * width : (i + 1) * width] for i in range(3)])
            at_out = [(qkv_sum, at_last[:, 3 * width :].T)] + at_out
    if not ring:
        ff_out = [jnp.stack(both) for both in zip(*ff_out, strict=True)]
        at_out = [jnp.stack(both) for both in zip(*at_out, strict=True)]

    if ring:
        operands = [*gain_sums[0], *gain_sums[1]]
        sent = run(
            functools.partial(gain_sums_kernel, lane_order),
            (1,),
            [whole(v.shape) for v in operands],
            whole((frames, 16, LANES)),
            shaped(frames, 16, LANES),
            [],
            [facts, *operands],
            1,
            prefetch=1,
            after=[input_grad],
        )
        total = jnp.sum(lax.all_to_all(sent, "frame", 0, 0), axis=0)
        total = total + row_take(total, 1)
        total = total + row_take(total, 2)
        gains_grad = total[:12].reshape(2, 6, LANES)
    else:
        rows = [jnp.concatenate([sums[0], sums[1] * F32(0.5), sums[2] * F32(0.5)]) for sums in gain_sums]
        rows = jnp.stack(rows)
        per_head = lax.dynamic_update_slice_in_dim(
            jnp.zeros((2, 2, wide), F32),
            jnp.stack([gain_sums[0][3], gain_sums[1][3]]),
            my_row * width,
            2,
        )
        total = lax.psum(jnp.concatenate([rows, per_head], axis=1), ("frame", "row"))
        gains_grad = lax.dynamic_slice_in_dim(total, my_frame * shard, shard, 2)
    return (
        output,
        input_grad,
        jnp.transpose(at_out[0], (0, 2, 1, 3)),
        at_out[1],
        ff_out[0],
        ff_out[1],
        gains_grad,
    )


def solution(mesh):
    return jax.shard_map(
        per_device,
        mesh=mesh,
        in_specs=(
            P(("frame", "row"), None),
            P(("frame", "row"), None),
            P(),
            P(),
            P(None, "frame", None, "row"),
            P(None, "row", "frame"),
            P(None, "frame", "row"),
            P(None, "row", "frame"),
            P(None, None, "frame"),
        ),
        out_specs=(
            P(("frame", "row"), None),
            P(("frame", "row"), None),
            P(None, "frame", None, "row"),
            P(None, "row", "frame"),
            P(None, "frame", "row"),
            P(None, "row", "frame"),
            P(None, None, "frame"),
        ),
        check_vma=False,
    )
```
